256 devices in a mesh: row: 16 (over z, core), col: 16 (over y, x).
Axes of the slice: x: 4, y: 4, z: 8, core: 2. Of those that a mesh axis runs over, the one named last changes fastest.
Arguments:
- features: bfloat16 [65536, 512], P(('row', 'col')), may hold values from -6 to 6
- w_self: bfloat16 [512, 512], replicated, may hold values from -0.25 to 0.25
- w_neigh: bfloat16 [512, 512], replicated, may hold values from -0.25 to 0.25
- block_vals: bfloat16 [16, 16, 128, 128, 128], P('row', 'col'), may hold values from -0.09375 to 0.09375
- block_coords: int32 [16, 16, 2, 128], P('row', 'col'), may hold values from 0 to 31, as said below
- block_count: int32 [16, 16], P('row', 'col'), may hold values from 16 to 128, as said below
- cotangent: bfloat16 [65536, 512], P(('row', 'col')), may hold values from -6 to 6
Outputs:
- layer_out: bfloat16 [65536, 512], P(('row', 'col'))
- grad_features: bfloat16 [65536, 512], P(('row', 'col'))
- grad_self: float32 [512, 512], replicated
- grad_neigh: float32 [512, 512], replicated
The draws below stay inside these ranges and needn't reach their ends.
Inputs may be any that keep to these rules, and one draw needn't show every extreme that they name: block_coords[r, c, 0, k] is below 32 and block_coords[r, c, 1, k] below 32; no two slots of one device name the same block. `block_count`: some device has all 128 slots live.
All inputs are finite; a program needn't handle non-finite values.
Results may differ from the reference program's by a relative error of at most 0.024.
Values may be sent and summed in bfloat16 or wider, within the bound.
No kernel may reach another device: no remote copies, remote signals or barrier semaphores. Data moves between devices by JAX's collectives and lax.ppermute only.
A program may use at most 128 MiB of HBM per device.

```python
import jax
import jax.numpy as jnp
from jax import lax

F = 512
BLK = 128
NODE_DEV = 256
NNZ_DEV = 128
NODES = 65536
N_ROW = 16
N_COL = 16


def draw_block_coords(key, part):
    key = jax.random.fold_in(key, 11)
    block_rows = N_ROW * NODE_DEV // BLK
    block_cols = N_COL * NODE_DEV // BLK
    device_keys = jax.random.split(key, N_ROW * N_COL)

    def pick(device_key):
        return jax.random.permutation(device_key, block_rows * block_cols)[:NNZ_DEV]
    chosen = jax.vmap(pick)(device_keys).astype(jnp.int32)
    stacked = jnp.stack([chosen // block_cols, chosen % block_cols], axis=1)
    return stacked.reshape(N_ROW, N_COL, 2, NNZ_DEV).astype(jnp.int32)


def draw_block_count(key, part):
    key = jax.random.fold_in(key, 23)
    first_key, second_key, third_key = jax.random.split(key, 3)
    counts = jax.random.randint(first_key, (N_ROW * N_COL,), NNZ_DEV // 8, NNZ_DEV // 2 + 1)
    heavy = jax.random.randint(second_key, (N_ROW * N_COL,), 0, 4) == 0
    forced = jax.random.randint(third_key, (), 0, N_ROW * N_COL)
    heavy = heavy | (jnp.arange(N_ROW * N_COL) == forced)
    counts = jnp.where(heavy, NNZ_DEV, counts)
    return counts.reshape(N_ROW, N_COL).astype(jnp.int32)


def block_scale(own_key, dims, cuts, low, high):
    factor_of = 1.0
    for dim, shards_of in cuts:
        draws = jax.random.uniform(jax.random.fold_in(jax.random.fold_in(own_key, 6), dim), (shards_of,), jnp.float32, low / len(cuts), high / len(cuts))
        factor_of = factor_of * jnp.repeat(jnp.exp(draws), dims[dim] // shards_of).reshape((-1,) + (1,) * (len(dims) - 1 - dim))
    return factor_of


def gaussian(stream_key, shape, scale, limit, shards=(), held_as=jnp.bfloat16):
    factor_of = block_scale(stream_key, shape, shards, -0.22, 0.18) if shards else 1.0
    result = jax.random.normal(stream_key, shape, jnp.float32) * scale * factor_of
    return jnp.minimum(jnp.maximum(result, -limit), limit).astype(held_as)


def setup_inputs(seed: int = 0) -> dict:
    key_list = jax.random.split(jax.random.key(seed), 8)
    features = gaussian(key_list[0], (NODES, F), 1.0, 6.0, ((0, 256),))
    w_self = gaussian(key_list[1], (F, F), F ** -0.5, 0.25)
    w_neigh = gaussian(key_list[2], (F, F), F ** -0.5, 0.25)
    block_vals = gaussian(key_list[3], (N_ROW, N_COL, NNZ_DEV, BLK, BLK), (NNZ_DEV * BLK * BLK // (2 * NODE_DEV)) ** -0.5, 0.09375, ((0, 16), (1, 16)))
    block_coords = draw_block_coords(jax.random.fold_in(key_list[7], 71), 0)
    block_count = draw_block_count(jax.random.fold_in(key_list[7], 71), 0)
    cotangent = gaussian(key_list[6], (NODES, F), 1.0, 6.0, ((0, 256),))
    return dict(features=features, w_self=w_self, w_neigh=w_neigh, block_vals=block_vals, block_coords=block_coords, block_count=block_count, cotangent=cotangent)


def round_keep(values):
    rounded = lax.optimization_barrier(values.astype(jnp.bfloat16))
    return rounded.astype(jnp.float32)


def tile_forward(tile_vals, coords, live_count, gathered):
    slots = tile_vals.shape[0]
    blocks = gathered.reshape(-1, BLK, F)[coords[1]].astype(jnp.float32)
    product = jnp.einsum("kab,kbf->kaf", tile_vals.astype(jnp.float32), blocks)
    live_mask = (jnp.arange(slots) < live_count).astype(jnp.float32)
    product = product * live_mask[:, None, None]
    total = jnp.zeros((N_ROW * NODE_DEV // BLK, BLK, F), jnp.float32).at[coords[0]].add(product)
    return total.reshape(-1, F)


def tile_backward(tile_vals, coords, live_count, gathered):
    slots = tile_vals.shape[0]
    blocks = gathered.reshape(-1, BLK, F)[coords[0]].astype(jnp.float32)
    product = jnp.einsum("kab,kaf->kbf", tile_vals.astype(jnp.float32), blocks)
    live_mask = (jnp.arange(slots) < live_count).astype(jnp.float32)
    product = product * live_mask[:, None, None]
    total = jnp.zeros((N_COL * NODE_DEV // BLK, BLK, F), jnp.float32).at[coords[1]].add(product)
    return total.reshape(-1, F)


def reference(features, w_self, w_neigh, block_vals, block_coords, block_count, cotangent):
    row_groups = features.reshape(N_ROW, N_COL * NODE_DEV, F)

    def forward_row(total, row_items):
        vals_row, coords_row, count_row, gathered = row_items

        def apply_tile(tile_items):
            return round_keep(tile_forward(tile_items[0], tile_items[1], tile_items[2], gathered))

        partials = lax.map(apply_tile, (vals_row, coords_row, count_row))
        return total + partials, None

    initial = jnp.zeros((N_COL, N_ROW * NODE_DEV, F), jnp.float32)
    neigh_sums, _ = lax.scan(forward_row, initial, (block_vals, block_coords, block_count, row_groups))
    neighbours = neigh_sums.reshape(N_COL, N_ROW, NODE_DEV, F).transpose(1, 0, 2, 3).reshape(NODES, F)
    neighbours = neighbours.astype(jnp.bfloat16)
    preact = jnp.dot(features, w_self, preferred_element_type=jnp.float32)
    preact = preact + jnp.dot(neighbours, w_neigh, preferred_element_type=jnp.float32)
    gate_value = jax.nn.sigmoid(preact)
    layer_out = (preact * gate_value).astype(jnp.bfloat16)
    slope_grad = (cotangent.astype(jnp.float32) * gate_value * (1.0 + preact * (1.0 - gate_value))).astype(jnp.bfloat16)
    grad_self = jnp.dot(features.T, slope_grad, preferred_element_type=jnp.float32)
    grad_neigh = jnp.dot(neighbours.T, slope_grad, preferred_element_type=jnp.float32)
    neigh_grad = jnp.dot(slope_grad, w_neigh.T, preferred_element_type=jnp.float32).astype(jnp.bfloat16)
    grad_columns = neigh_grad.reshape(N_ROW, N_COL, NODE_DEV, F).transpose(1, 0, 2, 3).reshape(N_COL, N_ROW * NODE_DEV, F)

    def backward_row(row_items):
        vals_row, coords_row, count_row = row_items

        def apply_tile(tile_items):
            return round_keep(tile_backward(tile_items[0], tile_items[1], tile_items[2], tile_items[3]))

        partials = lax.map(apply_tile, (vals_row, coords_row, count_row, grad_columns))
        return jnp.sum(partials, axis=0)

    back_rows = lax.map(backward_row, (block_vals, block_coords, block_count)).reshape(NODES, F)
    own_grad = jnp.dot(slope_grad, w_self.T, preferred_element_type=jnp.float32)
    grad_features = (own_grad + back_rows).astype(jnp.bfloat16)
    return layer_out, grad_features, grad_self, grad_neigh
```

```python
import functools

import jax
import jax.numpy as jnp
from jax import lax
from jax.experimental import pallas as pl
from jax.experimental.pallas import tpu as pltpu
from jax.sharding import PartitionSpec as P

AXES = ("row", "col")
NX, NY, NZ, CORES = 4, 4, 8, 2
BLK = 128
UNIT = 512


def place(x, y, z, core):
    return ((z % NZ) * CORES + core) * (NX * NY) + (y % NY) * NX + x % NX


def pairs(move):
    return [
        (place(x, y, z, c), place(*move(x, y, z, c)))
        for z in range(NZ)
        for c in range(CORES)
        for y in range(NY)
        for x in range(NX)
    ]


def along_first(step):
    return pairs(
        lambda x, y, z, c: (x + step, y, z, c) if c == 0 else (x, y + step, z, c)
    )


def along_second(step):
    return pairs(
        lambda x, y, z, c: (x, y + step, z, c) if c == 0 else (x + step, y, z, c)
    )


def along_z(step):
    return pairs(lambda x, y, z, c: (x, y, z + step, c))


def send(value, moved):
    return lax.ppermute(value, AXES, moved)


def swap(value):
    return send(value, pairs(lambda x, y, z, c: (x, y, z, 1 - c)))


def tile_kernel(offsets, transposed, out_blocks, unroll, chunk, *refs):
    count = len(offsets)
    live, source, target, vals_a, vals_b = refs[:5]
    pieces = refs[5 : 5 + count]
    out = refs[5 + count]
    held, vals, total, piece_sem, vals_sem = refs[6 + count :]
    slots = vals_a.shape[0]
    parts = slots // chunk
    piece_copies = [
        pltpu.make_async_copy(p, held.at[pl.ds(o, p.shape[0])], piece_sem.at[i])
        for i, (p, o) in enumerate(zip(pieces, offsets))
    ]
    for copy in piece_copies:
        copy.start()
    vals_copies = []
    for k, given in enumerate((vals_a, vals_b)):
        for j in range(parts):
            copy = pltpu.make_async_copy(
                given.at[pl.ds(j * chunk, chunk)],
                vals.at[pl.ds((k * parts + j) * chunk, chunk)],
                vals_sem.at[k * parts + j],
            )
            copy.start()
            vals_copies.append(copy)

    @pl.loop(0, out_blocks)
    def _(i):
        total[pl.ds(i * BLK, BLK), :] = jnp.zeros((BLK, total.shape[1]), jnp.float32)

    for copy in piece_copies:
        copy.wait()
    dims = (((0,), (0,)), ((), ())) if transposed else (((1,), (0,)), ((), ()))
    for k in range(CORES):
        for j in range(parts):
            vals_copies[k * parts + j].wait()
            here = jnp.clip(live[k] - j * chunk, 0, chunk)

            @pl.loop(0, (here + unroll - 1) // unroll)
            def _(g):
                for u in range(unroll):
                    s = k * slots + j * chunk + g * unroll + u
                    taken = held[pl.ds(pl.multiple_of(source[s] * BLK, BLK), BLK), :]
                    product = lax.dot_general(
                        vals[s], taken, dims, preferred_element_type=jnp.float32
                    )
                    placed = pl.ds(pl.multiple_of(target[s] * BLK, BLK), BLK)
                    total[placed, :] = total[placed, :] + product

    @pl.loop(0, out_blocks)
    def _(i):
        rows = pl.ds(i * BLK, BLK)
        out[rows, :] = total[rows, :].astype(jnp.bfloat16)


def tile_product(live, source, target, vals_a, vals_b, pieces, offsets, out_blocks, transposed):
    chunk, unroll = 64, 8
    slots = vals_a.shape[0]
    width = pieces[0].shape[1]
    rows = max(o + p.shape[0] for o, p in zip(offsets, pieces))
    slot = jnp.arange(slots, dtype=jnp.int32)[None]
    target = jnp.where(slot < live[:, None], target, out_blocks).reshape(-1)
    in_specs = [pl.BlockSpec(memory_space=pltpu.SMEM)] * 3
    in_specs += [pl.BlockSpec(memory_space=pl.ANY)] * (2 + len(pieces))
    return pl.pallas_call(
        functools.partial(tile_kernel, tuple(offsets), transposed, out_blocks, unroll, chunk),
        out_shape=jax.ShapeDtypeStruct((out_blocks * BLK, width), jnp.bfloat16),
        in_specs=in_specs,
        out_specs=pl.BlockSpec(memory_space=pltpu.VMEM),
        scratch_shapes=[
            pltpu.VMEM((rows, width), jnp.bfloat16),
            pltpu.VMEM((2 * slots, BLK, BLK), jnp.bfloat16),
            pltpu.VMEM(((out_blocks + 1) * BLK, width), jnp.float32),
            pltpu.SemaphoreType.DMA((len(pieces),)),
            pltpu.SemaphoreType.DMA((2 * (slots // chunk),)),
        ],
        compiler_params=pltpu.CompilerParams(vmem_limit_bytes=40 * 2**20),
        name="tile_product",
    )(live, source.reshape(-1), target, vals_a, vals_b, *pieces)


def gather_four(value, ahead, behind):
    rows = value.shape[0]
    half = rows // 2
    last = send(value, ahead)
    following = send(value, behind)
    top = send(following[:half], behind)
    bottom = send(last[half:], ahead)
    return [value, following, top, bottom, last], [0, rows, 2 * rows, 2 * rows + half, 3 * rows]


def widened(*values):
    return functools.reduce(lambda a, b: a + b, [v.astype(jnp.float32) for v in values]).astype(
        jnp.bfloat16
    )


def sum_four(value, ahead, behind):
    rows = value.shape[0] // 4
    half = rows // 2
    part = [value[i * rows : (i + 1) * rows] for i in range(4)]
    top = send(part[2][:half], ahead)
    bottom = send(part[2][half:], behind)
    to_ahead = jnp.concatenate([widened(part[1][:half], top), part[1][half:]], 0)
    to_behind = jnp.concatenate([part[3][:half], widened(part[3][half:], bottom)], 0)
    return [part[0], send(to_ahead, ahead), send(to_behind, behind)]


def gather_z(value):
    rows = value.shape[0]
    half = rows // 2
    ahead, behind = along_z(1), along_z(-1)
    pieces, offsets = [value], [0]
    last, following = value, value
    for step in range(1, NZ // 2):
        last, following = send(last, ahead), send(following, behind)
        pieces += [following, last]
        offsets += [step * rows, (NZ - step) * rows]
    pieces += [send(following[:half], behind), send(last[half:], ahead)]
    offsets += [NZ // 2 * rows, NZ // 2 * rows + half]
    return pieces, offsets


def sum_z(value):
    rows = value.shape[0] // NZ
    half = rows // 2
    ahead, behind = along_z(1), along_z(-1)
    part = [value[i * rows : (i + 1) * rows] for i in range(NZ)]
    top = send(part[NZ // 2][:half], ahead)
    bottom = send(part[NZ // 2][half:], behind)
    d = NZ // 2 - 1
    to_ahead = jnp.concatenate([widened(part[d][:half], top), part[d][half:]], 0)
    to_behind = jnp.concatenate([part[NZ - d][:half], widened(part[NZ - d][half:], bottom)], 0)
    for d in range(NZ // 2 - 2, -1, -1):
        from_behind, from_ahead = send(to_ahead, ahead), send(to_behind, behind)
        if d:
            to_ahead = widened(part[d], from_behind)
            to_behind = widened(part[NZ - d], from_ahead)
    return [part[0], from_behind, from_ahead]


def own_rows(halves, core, node_rows, width):
    half = width // 2
    mine = lax.dynamic_slice_in_dim(halves, core * node_rows, node_rows, 0)
    other = swap(lax.dynamic_slice_in_dim(halves, (1 - core) * node_rows, node_rows, 0))
    first = jnp.where(core == 0, mine, other)
    second = jnp.where(core == 0, other, mine)
    return jnp.concatenate([first, second], 1)


def own_half(rows, core, width):
    half = width // 2
    mine = lax.dynamic_slice_in_dim(rows, core * half, half, 1)
    other = swap(lax.dynamic_slice_in_dim(rows, (1 - core) * half, half, 1))
    first = jnp.where(core == 0, mine, other)
    second = jnp.where(core == 0, other, mine)
    return jnp.concatenate([first, second], 0)


def sum_everywhere(value):
    devices = NX * NY * NZ * CORES
    rows, width = value.shape
    given = value.reshape(devices, rows // devices, width)
    taken = lax.all_to_all(given, AXES, 0, 0, tiled=True)
    summed = jnp.sum(taken.astype(jnp.float32), axis=0).astype(value.dtype)
    spread = jnp.broadcast_to(summed[None], given.shape)
    return lax.all_to_all(spread, AXES, 0, 0, tiled=True).reshape(rows, width)


def per_device(features, w_self, w_neigh, block_vals, block_coords, block_count, cotangent):
    bf16, f32 = jnp.bfloat16, jnp.float32
    node_rows, width = features.shape
    row, col = lax.axis_index("row"), lax.axis_index("col")
    z, core = row // CORES, row % CORES
    y, x = col // NX, col % NX
    near_first, near_second = along_first(1), along_second(1)
    far_first, far_second = along_first(-1), along_second(-1)

    vals = block_vals[0, 0]
    slots = vals.shape[0]
    facts = jnp.concatenate(
        [block_coords[0, 0], jnp.broadcast_to(block_count[0, 0], (1, slots))], 0
    )
    unit = own_half(features, core, width)
    other_facts = swap(facts)
    other_vals = swap(vals)
    both = jnp.stack([facts, other_facts])
    live = both[:, 2, 0]
    tile_core = jnp.stack([core, 1 - core])[:, None]
    block_row, block_col = both[:, 0], both[:, 1]
    per_chip = CORES * (node_rows // BLK)
    row_place = ((block_row // per_chip - z) % NZ) * per_chip + block_row % per_chip
    per_dev = node_rows // BLK
    owner = block_col // per_dev
    dx, dy = (owner % NX - x) % NX, (owner // NX - y) % NY
    distance = jnp.where(core == 0, dy * NX + dx, dx * NY + dy)
    col_place = distance * per_chip + tile_core * per_dev + block_col % per_dev

    first, first_at = gather_four(unit, near_first, far_first)
    line = jnp.concatenate(first, 0)
    pieces, offsets = gather_four(line, near_second, far_second)
    partial = tile_product(
        live, col_place, row_place, vals, other_vals, pieces, offsets, NZ * per_chip, False
    )
    neighbours = own_rows(widened(*sum_z(partial)), core, node_rows, width)

    preact = jnp.dot(features, w_self, preferred_element_type=f32)
    preact = preact + jnp.dot(neighbours, w_neigh, preferred_element_type=f32)
    gate = jax.nn.sigmoid(preact)
    layer_out = (preact * gate).astype(bf16)
    slope_grad = (cotangent.astype(f32) * gate * (1.0 + preact * (1.0 - gate))).astype(bf16)
    contract_rows = (((0,), (0,)), ((), ()))
    contract_cols = (((1,), (1,)), ((), ()))
    neigh_grad = lax.dot_general(
        slope_grad, w_neigh, contract_cols, preferred_element_type=f32
    ).astype(bf16)
    grad_unit = own_half(neigh_grad, core, width)

    both_inputs = jnp.concatenate([features, neighbours], 1)
    grads = lax.dot_general(
        both_inputs, slope_grad, contract_rows, preferred_element_type=f32
    ).astype(bf16)
    grads = sum_everywhere(grads).astype(f32)
    grad_self, grad_neigh = grads[:width], grads[width:]

    pieces, offsets = gather_z(grad_unit)
    back = tile_product(
        live,
        row_place,
        col_place,
        vals,
        other_vals,
        pieces,
        offsets,
        NX * NY * per_chip,
        True,
    )
    back = widened(*sum_four(back, near_second, far_second))
    back = widened(*sum_four(back, near_first, far_first))
    back_rows = own_rows(back, core, node_rows, width)
    own_grad = lax.dot_general(slope_grad, w_self, contract_cols, preferred_element_type=f32)
    grad_features = (own_grad + back_rows.astype(f32)).astype(bf16)
    return layer_out, grad_features, grad_self, grad_neigh


def solution(mesh):
    in_specs = (
        P(("row", "col"), None),
        P(),
        P(),
        P("row", "col", None, None, None),
        P("row", "col", None, None),
        P("row", "col"),
        P(("row", "col"), None),
    )
    out_specs = (P(("row", "col"), None), P(("row", "col"), None), P(), P())
    return jax.shard_map(
        per_device, mesh=mesh, in_specs=in_specs, out_specs=out_specs, check_vma=False
    )
```

```python
import functools

import jax
import jax.numpy as jnp
from jax import lax
from jax.experimental import pallas as pl
from jax.experimental.pallas import tpu as pltpu
from jax.sharding import PartitionSpec as P

AXES = ("row", "col")
NX, NY, NZ, CORES = 4, 4, 8, 2
BLK = 128
UNIT = 512


def place(x, y, z, core):
    return ((z % NZ) * CORES + core) * (NX * NY) + (y % NY) * NX + x % NX


def pairs(move):
    return [
        (place(x, y, z, c), place(*move(x, y, z, c)))
        for z in range(NZ)
        for c in range(CORES)
        for y in range(NY)
        for x in range(NX)
    ]


def along_first(step):
    return pairs(
        lambda x, y, z, c: (x + step, y, z, c) if c == 0 else (x, y + step, z, c)
    )


def along_second(step):
    return pairs(
        lambda x, y, z, c: (x, y + step, z, c) if c == 0 else (x + step, y, z, c)
    )


def along_z(step):
    return pairs(lambda x, y, z, c: (x, y, z + step, c))


def send(value, moved):
    return lax.ppermute(value, AXES, moved)


def swap(value):
    return send(value, pairs(lambda x, y, z, c: (x, y, z, 1 - c)))


def tile_kernel(offsets, transposed, out_blocks, unroll, chunk, *refs):
    count = len(offsets)
    live, source, target, vals_a, vals_b = refs[:5]
    pieces = refs[5 : 5 + count]
    out = refs[5 + count]
    held, vals, total, piece_sem, vals_sem = refs[6 + count :]
    slots = vals_a.shape[0]
    parts = slots // chunk
    piece_copies = [
        pltpu.make_async_copy(p, held.at[pl.ds(o, p.shape[0])], piece_sem.at[i])
        for i, (p, o) in enumerate(zip(pieces, offsets))
    ]
    for copy in piece_copies:
        copy.start()
    vals_copies = []
    for k, given in enumerate((vals_a, vals_b)):
        for j in range(parts):
            copy = pltpu.make_async_copy(
                given.at[pl.ds(j * chunk, chunk)],
                vals.at[pl.ds((k * parts + j) * chunk, chunk)],
                vals_sem.at[k * parts + j],
            )
            copy.start()
            vals_copies.append(copy)

    @pl.loop(0, out_blocks)
    def _(i):
        total[pl.ds(i * BLK, BLK), :] = jnp.zeros((BLK, total.shape[1]), jnp.float32)

    for copy in piece_copies:
        copy.wait()
    dims = (((0,), (0,)), ((), ())) if transposed else (((1,), (0,)), ((), ()))
    for k in range(CORES):
        for j in range(parts):
            vals_copies[k * parts + j].wait()
            here = jnp.clip(live[k] - j * chunk, 0, chunk)

            @pl.loop(0, (here + unroll - 1) // unroll)
            def _(g):
                for u in range(unroll):
                    s = k * slots + j * chunk + g * unroll + u
                    taken = held[pl.ds(pl.multiple_of(source[s] * BLK, BLK), BLK), :]
                    product = lax.dot_general(
                        vals[s], taken, dims, preferred_element_type=jnp.float32
                    )
                    placed = pl.ds(pl.multiple_of(target[s] * BLK, BLK), BLK)
                    total[placed, :] = total[placed, :] + product

    @pl.loop(0, out_blocks)
    def _(i):
        rows = pl.ds(i * BLK, BLK)
        out[rows, :] = total[rows, :].astype(jnp.bfloat16)


def tile_product(live, source, target, vals_a, vals_b, pieces, offsets, out_blocks, transposed):
    chunk, unroll = 64, 8
    slots = vals_a.shape[0]
    width = pieces[0].shape[1]
    rows = max(o + p.shape[0] for o, p in zip(offsets, pieces))
    slot = jnp.arange(slots, dtype=jnp.int32)[None]
    target = jnp.where(slot < live[:, None], target, out_blocks).reshape(-1)
    in_specs = [pl.BlockSpec(memory_space=pltpu.SMEM)] * 3
    in_specs += [pl.BlockSpec(memory_space=pltpu.HBM)] * 2
    in_specs += [pl.BlockSpec(memory_space=pl.ANY)] * len(pieces)
    return pl.pallas_call(
        functools.partial(tile_kernel, tuple(offsets), transposed, out_blocks, unroll, chunk),
        out_shape=jax.ShapeDtypeStruct((out_blocks * BLK, width), jnp.bfloat16),
        in_specs=in_specs,
        out_specs=pl.BlockSpec(memory_space=pltpu.VMEM),
        scratch_shapes=[
            pltpu.VMEM((rows, width), jnp.bfloat16),
            pltpu.VMEM((2 * slots, BLK, BLK), jnp.bfloat16),
            pltpu.VMEM(((out_blocks + 1) * BLK, width), jnp.float32),
            pltpu.SemaphoreType.DMA((len(pieces),)),
            pltpu.SemaphoreType.DMA((2 * (slots // chunk),)),
        ],
        compiler_params=pltpu.CompilerParams(vmem_limit_bytes=40 * 2**20),
        name="tile_product",
    )(live, source.reshape(-1), target, vals_a, vals_b, *pieces)


def tied(*values):
    return lax.optimization_barrier(values)


def gather_four(value, ahead, behind, split):
    rows = value.shape[0]
    half = rows // 2
    at = [0] + [rows + i * half for i in range(6)]
    if not split:
        last, following = send(value, ahead), send(value, behind)
        across = [send(following[:half], behind), send(last[half:], ahead)]
        return [value, following, *across, last], [0, rows, at[3], at[4], at[5]]
    top, bottom = value[:half], value[half:]
    last_bottom, following_top = send(bottom, ahead), send(top, behind)
    last_top, following_bottom = send(top, ahead), send(bottom, behind)
    across_top, across_bottom = send(following_top, behind), send(last_bottom, ahead)
    pieces = [value, following_top, following_bottom, across_top, across_bottom]
    pieces += [last_top, last_bottom]
    return pieces, at


def widened(*values):
    return functools.reduce(lambda a, b: a + b, [v.astype(jnp.float32) for v in values]).astype(
        jnp.bfloat16
    )


def sum_ring(value, size, ahead, behind):
    rows = value.shape[0] // size
    half = rows // 2
    far = size // 2
    part = [value[i * rows : (i + 1) * rows] for i in range(size)]
    top, bottom = send(part[far][:half], ahead), send(part[far][half:], behind)
    if size == 4:
        low, high = send(part[1][half:], ahead), send(part[3][:half], behind)
        top, bottom = lax.optimization_barrier((top, bottom))
        top, bottom = tied(widened(part[1][:half], top), widened(part[3][half:], bottom))
        top, bottom = tied(send(top, ahead), send(bottom, behind))
        first = widened(part[0][:half], top, high)
        second = widened(part[0][half:], bottom, low)
        return jnp.concatenate([first, second], 0)
    top, bottom = lax.optimization_barrier((top, bottom))
    d = far - 1
    to_ahead = jnp.concatenate([widened(part[d][:half], top), part[d][half:]], 0)
    to_behind = jnp.concatenate([part[size - d][:half], widened(part[size - d][half:], bottom)], 0)
    for d in range(far - 2, -1, -1):
        to_ahead, to_behind = lax.optimization_barrier((to_ahead, to_behind))
        from_behind, from_ahead = send(to_ahead, ahead), send(to_behind, behind)
        from_behind, from_ahead = lax.optimization_barrier((from_behind, from_ahead))
        if d:
            to_ahead = widened(part[d], from_behind)
            to_behind = widened(part[size - d], from_ahead)
    return widened(part[0], from_behind, from_ahead)


def gather_z(value):
    rows = value.shape[0]
    half = rows // 2
    ahead, behind = along_z(1), along_z(-1)
    top, bottom = value[:half], value[half:]
    pieces, offsets = [value], [0]
    lead, rest = [top, bottom], [bottom, top]
    for d in range(1, NZ // 2):
        lead = [send(lead[0], behind), send(lead[1], ahead)]
        rest = [send(rest[0], behind), send(rest[1], ahead)]
        pieces += [lead[0], rest[0], rest[1], lead[1]]
        offsets += [d * rows, d * rows + half, (NZ - d) * rows, (NZ - d) * rows + half]
    pieces += [send(lead[0], behind), send(lead[1], ahead)]
    offsets += [NZ // 2 * rows, NZ // 2 * rows + half]
    return pieces, offsets


def own_rows(halves, core, node_rows, width):
    half = width // 2
    mine = lax.dynamic_slice_in_dim(halves, core * node_rows, node_rows, 0)
    other = swap(lax.dynamic_slice_in_dim(halves, (1 - core) * node_rows, node_rows, 0))
    first = jnp.where(core == 0, mine, other)
    second = jnp.where(core == 0, other, mine)
    return jnp.concatenate([first, second], 1)


def own_half(rows, core, width):
    half = width // 2
    mine = lax.dynamic_slice_in_dim(rows, core * half, half, 1)
    other = swap(lax.dynamic_slice_in_dim(rows, (1 - core) * half, half, 1))
    first = jnp.where(core == 0, mine, other)
    second = jnp.where(core == 0, other, mine)
    return jnp.concatenate([first, second], 0)


def pair_sum(first, second, core):
    mine = jnp.where(core == 0, first, second)
    other = swap(jnp.where(core == 0, second, first))
    return widened(mine, other)


def plane_parts(value):
    rows, width = value.shape
    given = value.reshape(NX * NY, rows // (NX * NY), width)
    return lax.all_to_all(given, "col", 0, 0, tiled=True)


def summed(parts):
    return jnp.sum(parts.astype(jnp.float32), axis=0).astype(parts.dtype)


def line_parts(value):
    groups = [[z * CORES + c for z in range(NZ)] for c in range(CORES)]
    spread = jnp.broadcast_to(value[None], (NZ, *value.shape))
    return lax.all_to_all(spread, "row", 0, 0, axis_index_groups=groups, tiled=True)


def plane_whole(value):
    spread = jnp.broadcast_to(value[None], (NX * NY, *value.shape))
    return lax.all_to_all(spread, "col", 0, 0, tiled=True).reshape(-1, value.shape[1])


def per_device(features, w_self, w_neigh, block_vals, block_coords, block_count, cotangent):
    bf16, f32 = jnp.bfloat16, jnp.float32
    node_rows, width = features.shape
    row, col = lax.axis_index("row"), lax.axis_index("col")
    z, core = row // CORES, row % CORES
    y, x = col // NX, col % NX
    near_first, near_second = along_first(1), along_second(1)
    far_first, far_second = along_first(-1), along_second(-1)

    vals = block_vals[0, 0]
    slots = vals.shape[0]
    facts = jnp.concatenate(
        [block_coords[0, 0], jnp.broadcast_to(block_count[0, 0], (1, slots))], 0
    )
    unit = own_half(features, core, width)
    later_facts, later_vals, unit = lax.optimization_barrier((facts, vals, unit))
    other_facts = swap(later_facts)
    other_vals = swap(later_vals)
    both = jnp.stack([facts, other_facts])
    live = both[:, 2, 0]
    tile_core = jnp.stack([core, 1 - core])[:, None]
    block_row, block_col = both[:, 0], both[:, 1]
    per_chip = CORES * (node_rows // BLK)
    row_place = ((block_row // per_chip - z) % NZ) * per_chip + block_row % per_chip
    per_dev = node_rows // BLK
    owner = block_col // per_dev
    dx, dy = (owner % NX - x) % NX, (owner // NX - y) % NY
    distance = jnp.where(core == 0, dy * NX + dx, dx * NY + dy)
    col_place = distance * per_chip + tile_core * per_dev + block_col % per_dev

    first, first_at = gather_four(unit, near_first, far_first, False)
    line = jnp.concatenate(first, 0)
    pieces, offsets = gather_four(line, near_second, far_second, True)
    partial = tile_product(
        live, col_place, row_place, vals, other_vals, pieces, offsets, NZ * per_chip, False
    )
    neighbours = sum_ring(partial, NZ, along_z(1), along_z(-1))
    neighbours = own_rows(neighbours, core, node_rows, width)

    preact = jnp.dot(features, w_self, preferred_element_type=f32)
    preact = preact + jnp.dot(neighbours, w_neigh, preferred_element_type=f32)
    gate = jax.nn.sigmoid(preact)
    layer_out = (preact * gate).astype(bf16)
    slope_grad = (cotangent.astype(f32) * gate * (1.0 + preact * (1.0 - gate))).astype(bf16)
    contract_rows = (((0,), (0,)), ((), ()))
    contract_cols = (((1,), (1,)), ((), ()))
    neigh_grad = lax.dot_general(
        slope_grad, w_neigh, contract_cols, preferred_element_type=f32
    ).astype(bf16)
    grad_unit = own_half(neigh_grad, core, width)

    grads = [
        lax.dot_general(v, slope_grad, contract_rows, preferred_element_type=f32).astype(bf16)
        for v in (features, neighbours)
    ]
    pieces, offsets = gather_z(grad_unit)
    total = plane_parts(pair_sum(*grads, core))
    *pieces, total = tied(*pieces, total)
    total = line_parts(summed(total))
    back = tile_product(
        live,
        row_place,
        col_place,
        vals,
        other_vals,
        pieces,
        offsets,
        NX * NY * per_chip,
        True,
    )
    back, total = tied(back, total)
    total = plane_whole(summed(total))
    back = sum_ring(back, NY, near_second, far_second)
    back, total = tied(back, total)
    other_total = swap(total)
    grad_self = jnp.where(core == 0, total, other_total).astype(f32)
    grad_neigh = jnp.where(core == 0, other_total, total).astype(f32)
    back = sum_ring(back, NX, near_first, far_first)
    back, grad_self, grad_neigh = tied(back, grad_self, grad_neigh)
    back_rows = own_rows(back, core, node_rows, width)
    own_grad = lax.dot_general(slope_grad, w_self, contract_cols, preferred_element_type=f32)
    grad_features = (own_grad + back_rows.astype(f32)).astype(bf16)
    return layer_out, grad_features, grad_self, grad_neigh


def solution(mesh):
    in_specs = (
        P(("row", "col"), None),
        P(),
        P(),
        P("row", "col", None, None, None),
        P("row", "col", None, None),
        P("row", "col"),
        P(("row", "col"), None),
    )
    out_specs = (P(("row", "col"), None), P(("row", "col"), None), P(), P())
    return jax.shard_map(
        per_device, mesh=mesh, in_specs=in_specs, out_specs=out_specs, check_vma=False
    )
```

```python
import functools

import jax
import jax.numpy as jnp
from jax import lax
from jax.experimental import pallas as pl
from jax.experimental.pallas import tpu as pltpu
from jax.sharding import PartitionSpec as P

AXES = ("row", "col")
NX, NY, NZ, CORES = 4, 4, 8, 2
BLK = 128
UNROLL = 8


def place(x, y, z, core):
    return ((z % NZ) * CORES + core) * (NX * NY) + (y % NY) * NX + x % NX


def pairs(move):
    return [
        (place(x, y, z, c), place(*move(x, y, z, c)))
        for z in range(NZ)
        for c in range(CORES)
        for y in range(NY)
        for x in range(NX)
    ]


def along_first(step):
    return pairs(
        lambda x, y, z, c: (x + step, y, z, c) if c == 0 else (x, y + step, z, c)
    )


def along_second(step):
    return pairs(
        lambda x, y, z, c: (x, y + step, z, c) if c == 0 else (x + step, y, z, c)
    )


def along_z(step):
    return pairs(lambda x, y, z, c: (x, y, z + step, c))


def send(value, moved):
    return lax.ppermute(value, AXES, moved)


def swap(value):
    return send(value, pairs(lambda x, y, z, c: (x, y, z, 1 - c)))


def tile_kernel(offsets, transposed, group, unroll, depth, cuts, *refs):
    table, bounds, vals_a, vals_b = refs[:4]
    refs = refs[4:]
    pieces, refs = refs[: len(offsets)], refs[len(offsets) :]
    if offsets:
        outs, held = refs[: len(cuts)], refs[len(cuts)]
        total, ring, ring_sem, sem = refs[len(cuts) + 1 :]
    else:
        held, outs = refs[0], refs[1 : len(cuts) + 1]
        total, ring, ring_sem = refs[len(cuts) + 1 :]
    copies = [
        pltpu.make_async_copy(p, held.at[pl.ds(o, p.shape[0])], sem.at[i])
        for i, (p, o) in enumerate(zip(pieces, offsets))
    ]
    for copy in copies:
        copy.start()
    blocks = sum(cuts)
    low, middle, high = [bounds[CORES * group + k] for k in range(CORES + 1)]
    first_steps = (middle - low + unroll - 1) // unroll
    steps = first_steps + (high - middle + unroll - 1) // unroll

    def begin(i):
        return jnp.where(i < first_steps, low + i * unroll, middle + (i - first_steps) * unroll)

    def fetch(i, vals):
        base = begin(i)
        room = lax.rem(i, depth)
        for u in range(unroll):
            pltpu.make_async_copy(
                vals.at[table[base + u] & 127], ring.at[room, u], ring_sem.at[room]
            ).start()

    def ahead(i):
        @pl.when(i < first_steps)
        def _():
            fetch(i, vals_a)

        @pl.when((i >= first_steps) & (i < steps))
        def _():
            fetch(i, vals_b)

    for i in range(depth - 1):
        ahead(jnp.int32(i))

    @pl.loop(0, blocks)
    def _(i):
        total[pl.ds(i * BLK, BLK), :] = jnp.zeros((BLK, total.shape[1]), jnp.float32)

    for copy in copies:
        copy.wait()
    dims = (((0,), (0,)), ((), ())) if transposed else (((1,), (0,)), ((), ()))

    @pl.loop(0, steps)
    def _(i):
        ahead(i + depth - 1)
        room = lax.rem(i, depth)
        pltpu.make_async_copy(
            vals_a.at[pl.ds(0, unroll)], ring.at[room], ring_sem.at[room]
        ).wait()
        base = begin(i)
        limit = jnp.where(i < first_steps, middle, high)
        for u in range(unroll):
            entry = table[base + u]
            source = lax.shift_right_logical(entry, 7) & 63
            target = jnp.where(base + u < limit, lax.shift_right_logical(entry, 13), blocks)
            taken = held[pl.ds(pl.multiple_of(source * BLK, BLK), BLK), :]
            product = lax.dot_general(
                ring[room, u], taken, dims, preferred_element_type=jnp.float32
            )
            placed = pl.ds(pl.multiple_of(target * BLK, BLK), BLK)
            total[placed, :] = total[placed, :] + product

    at = 0
    for out, size in zip(outs, cuts):
        first = at

        @pl.loop(0, size)
        def _(i):
            rows = pl.ds((first + i) * BLK, BLK)
            out[pl.ds(i * BLK, BLK), :] = total[rows, :].astype(jnp.bfloat16)

        at += size


def tile_product(table, bounds, vals_a, vals_b, sources, offsets, group, cuts, transposed):
    unroll, depth = UNROLL, 3
    width = sources[0].shape[1]
    blocks = sum(cuts)
    vmem = pl.BlockSpec(memory_space=pltpu.VMEM)
    hbm = pl.BlockSpec(memory_space=pltpu.HBM)
    in_specs = [pl.BlockSpec(memory_space=pltpu.SMEM)] * 2 + [hbm] * 2
    out_shape = [jax.ShapeDtypeStruct((c * BLK, width), jnp.bfloat16) for c in cuts]
    scratch = [
        pltpu.VMEM(((blocks + 1) * BLK, width), jnp.float32),
        pltpu.VMEM((depth, unroll, BLK, BLK), jnp.bfloat16),
        pltpu.SemaphoreType.DMA((depth,)),
    ]
    if offsets:
        rows = max(o + p.shape[0] for o, p in zip(offsets, sources))
        in_specs += [hbm] * len(sources)
        out_shape.append(jax.ShapeDtypeStruct((rows, width), jnp.bfloat16))
        scratch.append(pltpu.SemaphoreType.DMA((len(sources),)))
    else:
        in_specs += [vmem]
    return pl.pallas_call(
        functools.partial(
            tile_kernel, tuple(offsets), transposed, group, unroll, depth, tuple(cuts)
        ),
        out_shape=out_shape,
        in_specs=in_specs,
        out_specs=[vmem] * len(out_shape),
        scratch_shapes=scratch,
        compiler_params=pltpu.CompilerParams(vmem_limit_bytes=52 * 2**20),
        cost_estimate=pl.CostEstimate(
            flops=2 * BLK * BLK * width * 8 * blocks, bytes_accessed=2**20, transcendentals=0
        ),
        name="tile_product",
    )(table, bounds, vals_a, vals_b, *sources)


def chosen(index, values):
    return sum(jnp.where(index == i, v, 0) for i, v in enumerate(values) if v) + 0 * index


def slot_table(live, source, target, group, groups):
    slots = source.shape[1]
    slot = jnp.arange(slots, dtype=jnp.int32)[None]
    tile = jnp.arange(CORES, dtype=jnp.int32)[:, None]
    key = jnp.where(slot < live[:, None], group * CORES + tile, groups * CORES).reshape(-1)
    entry = (slot + source * 128 + target * 8192).reshape(-1)
    place = jnp.arange(CORES * slots, dtype=jnp.int32)
    before = key[None] < key[:, None]
    before |= (key[None] == key[:, None]) & (place[None] < place[:, None])
    rank = jnp.sum(before.astype(jnp.int32), axis=1)
    seat = jnp.arange(CORES * slots + UNROLL, dtype=jnp.int32)[:, None]
    table = jnp.sum(jnp.where(rank[None] == seat, entry[None], 0), axis=1)
    starts = jnp.arange(groups * CORES + 1, dtype=jnp.int32)[:, None]
    bounds = jnp.sum((key[None] < starts).astype(jnp.int32), axis=1)
    return table, bounds


def tied(*values):
    return lax.optimization_barrier(values)


def gather_plane(unit, first_ahead, first_behind, second_ahead, second_behind):
    half = unit.shape[0] // 2
    last, following = send(unit, first_ahead), send(unit, first_behind)
    last, following = tied(last, following)
    top = jnp.concatenate([unit[:half], following[:half], last[:half]], 0)
    bottom = jnp.concatenate([unit[half:], following[half:], last[half:]], 0)
    top, bottom = tied(top, bottom)
    behind_top, ahead_bottom = send(top, second_behind), send(bottom, second_ahead)
    across = [send(following[:half], first_behind), send(last[half:], first_ahead)]
    behind_bottom, ahead_top = send(bottom, second_behind), send(top, second_ahead)
    far_top, far_bottom = send(behind_top, second_behind), send(ahead_bottom, second_ahead)
    across = jnp.concatenate(across, 0)
    behind_across, ahead_across = send(across, second_behind), send(across, second_ahead)
    far_across = [
        send(behind_across[:half], second_behind),
        send(ahead_across[half:], second_ahead),
    ]
    lines = [
        [top, bottom, across],
        [behind_top, behind_bottom, behind_across],
        [far_top, far_bottom, *far_across],
        [ahead_top, ahead_bottom, ahead_across],
    ]
    pieces, offsets = [], []
    at = 0
    for line in lines:
        for piece in line:
            pieces.append(piece)
            offsets.append(at)
            at += piece.shape[0]
    return pieces, offsets


def widened(*values):
    return functools.reduce(lambda a, b: a + b, [v.astype(jnp.float32) for v in values]).astype(
        jnp.bfloat16
    )


def sum_four(near, beside, far, ahead, behind):
    half = near.shape[0] // 2
    top, bottom = send(far[0], ahead), send(far[1], behind)
    (one_top, one_bottom), (three_top, three_bottom) = beside()
    low, high = send(one_bottom, ahead), send(three_top, behind)
    top, bottom = tied(top, bottom)
    top, bottom = tied(widened(one_top, top), widened(three_bottom, bottom))
    top, bottom = tied(send(top, ahead), send(bottom, behind))
    first = widened(near[:half], top, high)
    second = widened(near[half:], bottom, low)
    return jnp.concatenate([first, second], 0)


def sum_z(part, far, ahead, behind):
    half = part[0].shape[0] // 2
    top, bottom = tied(send(far[0], ahead), send(far[1], behind))
    to_ahead = jnp.concatenate([widened(part[3][:half], top), part[3][half:]], 0)
    to_behind = jnp.concatenate([part[5][:half], widened(part[5][half:], bottom)], 0)
    for d in (2, 1, 0):
        to_ahead, to_behind = tied(to_ahead, to_behind)
        from_behind, from_ahead = tied(send(to_ahead, ahead), send(to_behind, behind))
        if d:
            to_ahead = widened(part[d], from_behind)
            to_behind = widened(part[NZ - d], from_ahead)
    return widened(part[0], from_behind, from_ahead)


def gather_z(value):
    rows = value.shape[0]
    half = rows // 2
    ahead, behind = along_z(1), along_z(-1)
    top, bottom = value[:half], value[half:]
    pieces, offsets = [value], [0]
    lead, rest = [top, bottom], [bottom, top]
    for d in range(1, NZ // 2):
        lead = [send(lead[0], behind), send(lead[1], ahead)]
        rest = [send(rest[0], behind), send(rest[1], ahead)]
        pieces += [lead[0], rest[0], rest[1], lead[1]]
        offsets += [d * rows, d * rows + half, (NZ - d) * rows, (NZ - d) * rows + half]
    pieces += [send(lead[0], behind), send(lead[1], ahead)]
    offsets += [NZ // 2 * rows, NZ // 2 * rows + half]
    return pieces, offsets


def own_rows(halves, core, node_rows, width):
    half = width // 2
    mine = lax.dynamic_slice_in_dim(halves, core * node_rows, node_rows, 0)
    other = swap(lax.dynamic_slice_in_dim(halves, (1 - core) * node_rows, node_rows, 0))
    first = jnp.where(core == 0, mine, other)
    second = jnp.where(core == 0, other, mine)
    return jnp.concatenate([first, second], 1)


def own_half(rows, core, width):
    half = width // 2
    mine = lax.dynamic_slice_in_dim(rows, core * half, half, 1)
    other = swap(lax.dynamic_slice_in_dim(rows, (1 - core) * half, half, 1))
    first = jnp.where(core == 0, mine, other)
    second = jnp.where(core == 0, other, mine)
    return jnp.concatenate([first, second], 0)


def plane_parts(value):
    rows, width = value.shape
    given = value.reshape(NX * NY, rows // (NX * NY), width)
    return lax.all_to_all(given, "col", 0, 0, tiled=True)


def summed(parts):
    return jnp.sum(parts.astype(jnp.float32), axis=0).astype(parts.dtype)


def plane_whole(value):
    spread = jnp.broadcast_to(value[None], (NX * NY, *value.shape))
    return lax.all_to_all(spread, "col", 0, 0, tiled=True)


def per_device(features, w_self, w_neigh, block_vals, block_coords, block_count, cotangent):
    bf16, f32 = jnp.bfloat16, jnp.float32
    node_rows, width = features.shape
    row, col = lax.axis_index("row"), lax.axis_index("col")
    z, core = row // CORES, row % CORES
    y, x = col // NX, col % NX
    near_first, near_second = along_first(1), along_second(1)
    far_first, far_second = along_first(-1), along_second(-1)

    vals = block_vals[0, 0]
    slots = vals.shape[0]
    facts = jnp.concatenate(
        [block_coords[0, 0], jnp.broadcast_to(block_count[0, 0], (1, slots))], 0
    )
    unit = own_half(features, core, width)
    later_facts, later_vals, unit = lax.optimization_barrier((facts, vals, unit))
    other_facts = swap(later_facts)
    other_vals = swap(later_vals)
    both = jnp.stack([facts, other_facts])
    live = both[:, 2, 0]
    tile_core = jnp.stack([core, 1 - core])[:, None]
    block_row, block_col = both[:, 0], both[:, 1]
    per_dev = node_rows // BLK
    per_chip = CORES * per_dev
    line = NX * per_chip
    z_away = (block_row // per_chip - z) % NZ
    row_in = block_row % per_chip
    owner = block_col // per_dev
    col_in = block_col % per_dev
    dx, dy = (owner % NX - x) % NX, (owner // NX - y) % NY
    first_away, second_away = jnp.where(core == 0, dx, dy), jnp.where(core == 0, dy, dx)
    in_line = jnp.where(
        first_away == 2,
        6 * per_dev + tile_core * per_dev,
        3 * per_dev * tile_core + per_dev * jnp.minimum(first_away, 2),
    )
    forward = slot_table(
        live,
        second_away * line + in_line + col_in,
        chosen(z_away, [2 * per_chip, 0, 2 * per_chip, 0, 0, per_chip, 3 * per_chip, per_chip])
        + row_in,
        chosen(z_away, [2, 2, 1, 1, 0, 1, 1, 2]),
        3,
    )
    backward = slot_table(
        live,
        z_away * per_chip + row_in,
        jnp.where(second_away == 3, line, 0)
        + first_away * per_chip
        + tile_core * per_dev
        + col_in,
        chosen(second_away, [2, 1, 0, 1]),
        3,
    )

    pieces, offsets = gather_plane(unit, near_first, far_first, near_second, far_second)
    half_chip = per_chip // 2
    *far, held = tile_product(
        *forward, vals, other_vals, pieces, offsets, 0, [half_chip] * 2, False
    )
    part = [None] * NZ
    part[3], part[5], part[2], part[6] = tile_product(
        *forward, vals, other_vals, [held], [], 1, [per_chip] * 4, False
    )
    part[1], part[7], part[0] = tile_product(
        *forward, vals, other_vals, [held], [], 2, [per_chip] * 3, False
    )
    neighbours = sum_z(part, far, along_z(1), along_z(-1))
    neighbours = own_rows(neighbours, core, node_rows, width)

    preact = jnp.dot(features, w_self, preferred_element_type=f32)
    preact = preact + jnp.dot(neighbours, w_neigh, preferred_element_type=f32)
    gate = jax.nn.sigmoid(preact)
    layer_out = (preact * gate).astype(bf16)
    slope_grad = (cotangent.astype(f32) * gate * (1.0 + preact * (1.0 - gate))).astype(bf16)
    contract_rows = (((0,), (0,)), ((), ()))
    contract_cols = (((1,), (1,)), ((), ()))
    neigh_grad = lax.dot_general(
        slope_grad, w_neigh, contract_cols, preferred_element_type=f32
    ).astype(bf16)
    grad_unit = own_half(neigh_grad, core, width)

    grads = lax.dot_general(
        jnp.concatenate([features, neighbours], 1),
        slope_grad,
        contract_rows,
        preferred_element_type=f32,
    ).astype(bf16)
    pieces, offsets = gather_z(grad_unit)
    total = plane_parts(grads)
    pieces[-1], total = tied(pieces[-1], total)
    total = summed(lax.all_gather(summed(total), "row", axis=0))

    *far, held = tile_product(
        *backward, vals, other_vals, pieces, offsets, 0, [line // 2] * 2, True
    )

    def beside():
        parts = tile_product(
            *backward, vals, other_vals, [held], [], 1, [line // 2] * 4, True
        )
        return parts[:2], parts[2:]

    (near,) = tile_product(*backward, vals, other_vals, [held], [], 2, [line], True)
    back = sum_four(near, beside, far, near_second, far_second)
    back, total = tied(back, total)
    strip = total.shape[0] // CORES
    total = plane_whole(lax.dynamic_slice_in_dim(total, core * strip, strip, 0))
    quarter = node_rows
    cut = [back[i * quarter : (i + 1) * quarter] for i in range(2 * NX)]
    back = sum_four(
        jnp.concatenate(cut[:2], 0),
        lambda: (cut[2:4], cut[6:8]),
        cut[4:6],
        near_first,
        far_first,
    )
    back, total = tied(back, total)
    other_total = swap(total)
    halves = [jnp.where(core == 0, total, other_total), jnp.where(core == 0, other_total, total)]
    half = total.shape[0] // 2
    grad_self, grad_neigh = [
        jnp.stack([h[cut] for h in halves], 1).reshape(width, width).astype(f32)
        for cut in (slice(0, half), slice(half, None))
    ]
    back_rows = own_rows(back, core, node_rows, width)
    own_grad = lax.dot_general(slope_grad, w_self, contract_cols, preferred_element_type=f32)
    grad_features = (own_grad + back_rows.astype(f32)).astype(bf16)
    return layer_out, grad_features, grad_self, grad_neigh


def solution(mesh):
    in_specs = (
        P(("row", "col"), None),
        P(),
        P(),
        P("row", "col", None, None, None),
        P("row", "col", None, None),
        P("row", "col"),
        P(("row", "col"), None),
    )
    out_specs = (P(("row", "col"), None), P(("row", "col"), None), P(), P())
    return jax.shard_map(
        per_device, mesh=mesh, in_specs=in_specs, out_specs=out_specs, check_vma=False
    )
```

```python
import functools

import jax
import jax.numpy as jnp
from jax import lax
from jax.experimental import pallas as pl
from jax.experimental.pallas import tpu as pltpu
from jax.sharding import PartitionSpec as P

AXES = ("row", "col")
NX, NY, NZ, CORES = 4, 4, 8, 2
BLK = 128
UNROLL = 8


def place(x, y, z, core):
    return ((z % NZ) * CORES + core) * (NX * NY) + (y % NY) * NX + x % NX


def pairs(move):
    return [
        (place(x, y, z, c), place(*move(x, y, z, c)))
        for z in range(NZ)
        for c in range(CORES)
        for y in range(NY)
        for x in range(NX)
    ]


def along_first(step):
    return pairs(
        lambda x, y, z, c: (x + step, y, z, c) if c == 0 else (x, y + step, z, c)
    )


def along_second(step):
    return pairs(
        lambda x, y, z, c: (x, y + step, z, c) if c == 0 else (x + step, y, z, c)
    )


def along_z(step):
    return pairs(lambda x, y, z, c: (x, y, z + step, c))


def send(value, moved):
    return lax.ppermute(value, AXES, moved)


def exchange_z(value, bit):
    return send(value, pairs(lambda x, y, z, c: (x, y, z ^ bit, c)))


def swap(value):
    return send(value, pairs(lambda x, y, z, c: (x, y, z, 1 - c)))


def tile_kernel(offsets, transposed, group, unroll, depth, cuts, *refs):
    table, bounds, vals_a, vals_b = refs[:4]
    refs = refs[4:]
    pieces, refs = refs[: len(offsets)], refs[len(offsets) :]
    if offsets:
        outs, held = refs[: len(cuts)], refs[len(cuts)]
        total, ring, ring_sem, sem = refs[len(cuts) + 1 :]
    else:
        held, outs = refs[0], refs[1 : len(cuts) + 1]
        total, ring, ring_sem = refs[len(cuts) + 1 :]
    copies = [
        pltpu.make_async_copy(p, held.at[pl.ds(o, p.shape[0])], sem.at[i])
        for i, (p, o) in enumerate(zip(pieces, offsets))
    ]
    for copy in copies:
        copy.start()
    blocks = sum(cuts)
    low, middle, high = [bounds[CORES * group + k] for k in range(CORES + 1)]
    first_steps = (middle - low + unroll - 1) // unroll
    steps = first_steps + (high - middle + unroll - 1) // unroll

    def begin(i):
        return jnp.where(i < first_steps, low + i * unroll, middle + (i - first_steps) * unroll)

    def fetch(i, vals):
        base = begin(i)
        room = lax.rem(i, depth)
        for u in range(unroll):
            pltpu.make_async_copy(
                vals.at[table[base + u] & 127], ring.at[room, u], ring_sem.at[room]
            ).start()

    def ahead(i):
        @pl.when(i < first_steps)
        def _():
            fetch(i, vals_a)

        @pl.when((i >= first_steps) & (i < steps))
        def _():
            fetch(i, vals_b)

    for i in range(depth - 1):
        ahead(jnp.int32(i))

    @pl.loop(0, blocks)
    def _(i):
        total[pl.ds(i * BLK, BLK), :] = jnp.zeros((BLK, total.shape[1]), jnp.float32)

    for copy in copies:
        copy.wait()
    dims = (((0,), (0,)), ((), ())) if transposed else (((1,), (0,)), ((), ()))

    @pl.loop(0, steps)
    def _(i):
        ahead(i + depth - 1)
        room = lax.rem(i, depth)
        pltpu.make_async_copy(
            vals_a.at[pl.ds(0, unroll)], ring.at[room], ring_sem.at[room]
        ).wait()
        base = begin(i)
        limit = jnp.where(i < first_steps, middle, high)
        for u in range(unroll):
            entry = table[base + u]
            source = lax.shift_right_logical(entry, 7) & 63
            target = jnp.where(base + u < limit, lax.shift_right_logical(entry, 13), blocks)
            taken = held[pl.ds(pl.multiple_of(source * BLK, BLK), BLK), :]
            product = lax.dot_general(
                ring[room, u], taken, dims, preferred_element_type=jnp.float32
            )
            placed = pl.ds(pl.multiple_of(target * BLK, BLK), BLK)
            total[placed, :] = total[placed, :] + product

    at = 0
    for out, size in zip(outs, cuts):
        first = at

        @pl.loop(0, size)
        def _(i):
            rows = pl.ds((first + i) * BLK, BLK)
            out[pl.ds(i * BLK, BLK), :] = total[rows, :].astype(jnp.bfloat16)

        at += size


def kept(value):
    return pltpu.with_memory_space_constraint(value, pltpu.HBM)


def tile_product(table, bounds, vals_a, vals_b, sources, offsets, group, cuts, transposed):
    unroll, depth = UNROLL, 3
    width = sources[0].shape[1]
    blocks = sum(cuts)
    vmem = pl.BlockSpec(memory_space=pltpu.VMEM)
    hbm = pl.BlockSpec(memory_space=pltpu.HBM)
    in_specs = [pl.BlockSpec(memory_space=pltpu.SMEM)] * 2 + [hbm] * 2
    out_shape = [jax.ShapeDtypeStruct((c * BLK, width), jnp.bfloat16) for c in cuts]
    scratch = [
        pltpu.VMEM(((blocks + 1) * BLK, width), jnp.float32),
        pltpu.VMEM((depth, unroll, BLK, BLK), jnp.bfloat16),
        pltpu.SemaphoreType.DMA((depth,)),
    ]
    if offsets:
        rows = max(o + p.shape[0] for o, p in zip(offsets, sources))
        in_specs += [pl.BlockSpec(memory_space=pl.ANY)] * len(sources)
        out_shape.append(jax.ShapeDtypeStruct((rows, width), jnp.bfloat16))
        scratch.append(pltpu.SemaphoreType.DMA((len(sources),)))
    else:
        in_specs += [vmem]
    return pl.pallas_call(
        functools.partial(
            tile_kernel, tuple(offsets), transposed, group, unroll, depth, tuple(cuts)
        ),
        out_shape=out_shape,
        in_specs=in_specs,
        out_specs=[vmem] * len(out_shape),
        scratch_shapes=scratch,
        compiler_params=pltpu.CompilerParams(vmem_limit_bytes=20 * 2**20),
        cost_estimate=pl.CostEstimate(
            flops=2 * BLK * BLK * width * 8 * blocks, bytes_accessed=2**20, transcendentals=0
        ),
        name="tile_product",
    )(table, bounds, *[kept(v) for v in (vals_a, vals_b)], *sources)


def chosen(index, values):
    return sum(jnp.where(index == i, v, 0) for i, v in enumerate(values) if v) + 0 * index


def slot_table(live, source, target, group, groups):
    slots = source.shape[1]
    slot = jnp.arange(slots, dtype=jnp.int32)[None]
    tile = jnp.arange(CORES, dtype=jnp.int32)[:, None]
    key = jnp.where(slot < live[:, None], group * CORES + tile, groups * CORES).reshape(-1)
    entry = (slot + source * 128 + target * 8192).reshape(-1)
    place = jnp.arange(CORES * slots, dtype=jnp.int32)
    before = key[None] < key[:, None]
    before |= (key[None] == key[:, None]) & (place[None] < place[:, None])
    rank = jnp.sum(before.astype(jnp.int32), axis=1)
    seat = jnp.arange(CORES * slots + UNROLL, dtype=jnp.int32)[:, None]
    table = jnp.sum(jnp.where(rank[None] == seat, entry[None], 0), axis=1)
    starts = jnp.arange(groups * CORES + 1, dtype=jnp.int32)[:, None]
    bounds = jnp.sum((key[None] < starts).astype(jnp.int32), axis=1)
    return table, bounds


def tied(*values):
    return lax.optimization_barrier(values)


def gather_plane(unit, first_ahead, first_behind, second_ahead, second_behind):
    half = unit.shape[0] // 2
    last, following = send(unit, first_ahead), send(unit, first_behind)
    last, following = tied(last, following)
    near = [unit, following, last]
    near = jnp.concatenate([v[:half] for v in near] + [v[half:] for v in near], 0)
    behind_near, ahead_near = send(near, second_behind), send(near, second_ahead)
    across = [send(following[:half], first_behind), send(last[half:], first_ahead)]
    across = jnp.concatenate(across, 0)
    behind_across, ahead_across = send(across, second_behind), send(across, second_ahead)
    middle = near.shape[0] // 2
    behind_near, ahead_near = tied(behind_near, ahead_near)
    far = [send(behind_near[:middle], second_behind), send(ahead_near[middle:], second_ahead)]
    far_across = [
        send(behind_across[:half], second_behind),
        send(ahead_across[half:], second_ahead),
    ]
    lines = [[near, across], [behind_near, behind_across], [*far, *far_across]]
    lines += [[ahead_near, ahead_across]]
    pieces, offsets = [], []
    at = 0
    for line in lines:
        for piece in line:
            pieces.append(piece)
            offsets.append(at)
            at += piece.shape[0]
    return pieces, offsets


def widened(*values):
    return functools.reduce(lambda a, b: a + b, [v.astype(jnp.float32) for v in values]).astype(
        jnp.bfloat16
    )


def sum_four(near, free, bound, far, ahead, behind):
    top, bottom = send(far[0], ahead), send(far[1], behind)
    low, high = free()
    low, high = send(low, ahead), send(high, behind)
    one, three = bound()
    top, bottom = tied(top, bottom)
    top, bottom = tied(widened(one, top), widened(three, bottom))
    low, high = tied(low, high)
    near, low, high = near(low, high)
    half = near.shape[0] // 2
    top, bottom = tied(send(top, ahead), send(bottom, behind))
    first = widened(near[:half], top, high)
    second = widened(near[half:], bottom, low)
    return jnp.concatenate([first, second], 0)


def sum_z(part, far, ahead, behind):
    half = part[0].shape[0] // 2
    top, bottom = tied(send(far[0], ahead), send(far[1], behind))
    to_ahead = jnp.concatenate([widened(part[3][:half], top), part[3][half:]], 0)
    to_behind = jnp.concatenate([part[5][:half], widened(part[5][half:], bottom)], 0)
    for d in (2, 1, 0):
        to_ahead, to_behind = tied(to_ahead, to_behind)
        from_behind, from_ahead = tied(send(to_ahead, ahead), send(to_behind, behind))
        if d:
            to_ahead = widened(part[d], from_behind)
            to_behind = widened(part[NZ - d], from_ahead)
    return widened(part[0], from_behind, from_ahead)


def gather_z(value, grads):
    rows = value.shape[0]
    half = rows // 2
    ahead, behind = along_z(1), along_z(-1)
    top, bottom = value[:half], value[half:]
    pieces, offsets = [value], [0]
    lead, rest = [top, bottom], [bottom, top]
    for d in range(1, NZ // 2):
        lead = [send(lead[0], behind), send(lead[1], ahead)]
        if d == 1:
            *lead, grads = tied(*lead, grads)
            grads = lax.all_to_all(grads, "col", 0, 0, tiled=True)
        if d == 3:
            *lead, grads = tied(*lead, grads)
            grads = summed(grads)
            grads = widened(grads, swap(grads))
        rest = [send(rest[0], behind), send(rest[1], ahead)]
        pieces += [lead[0], rest[0], rest[1], lead[1]]
        offsets += [d * rows, d * rows + half, (NZ - d) * rows, (NZ - d) * rows + half]
    lead = [send(lead[0], behind), send(lead[1], ahead)]
    *lead, grads = tied(*lead, grads)
    pieces += lead
    offsets += [NZ // 2 * rows, NZ // 2 * rows + half]
    return pieces, offsets, grads


def own_rows(halves, core, node_rows, width):
    half = width // 2
    mine = lax.dynamic_slice_in_dim(halves, core * node_rows, node_rows, 0)
    other = swap(lax.dynamic_slice_in_dim(halves, (1 - core) * node_rows, node_rows, 0))
    first = jnp.where(core == 0, mine, other)
    second = jnp.where(core == 0, other, mine)
    return jnp.concatenate([first, second], 1)


def own_half(rows, core, width):
    half = width // 2
    mine = lax.dynamic_slice_in_dim(rows, core * half, half, 1)
    other = swap(lax.dynamic_slice_in_dim(rows, (1 - core) * half, half, 1))
    first = jnp.where(core == 0, mine, other)
    second = jnp.where(core == 0, other, mine)
    return jnp.concatenate([first, second], 0)


def summed(parts):
    return jnp.sum(parts.astype(jnp.float32), axis=0).astype(parts.dtype)


def plane_whole(value):
    spread = jnp.broadcast_to(value[None], (NX * NY, *value.shape))
    return lax.all_to_all(spread, "col", 0, 0, tiled=True)


def per_device(features, w_self, w_neigh, block_vals, block_coords, block_count, cotangent):
    bf16, f32 = jnp.bfloat16, jnp.float32
    node_rows, width = features.shape
    row, col = lax.axis_index("row"), lax.axis_index("col")
    z, core = row // CORES, row % CORES
    y, x = col // NX, col % NX
    near_first, near_second = along_first(1), along_second(1)
    far_first, far_second = along_first(-1), along_second(-1)

    vals = block_vals[0, 0]
    slots = vals.shape[0]
    facts = jnp.concatenate(
        [block_coords[0, 0], jnp.broadcast_to(block_count[0, 0], (1, slots))], 0
    )
    unit = own_half(features, core, width)
    later_facts, later_vals, unit = lax.optimization_barrier((facts, vals, unit))
    other_facts = swap(later_facts)
    other_vals = swap(later_vals)
    both = jnp.stack([facts, other_facts])
    live = both[:, 2, 0]
    tile_core = jnp.stack([core, 1 - core])[:, None]
    block_row, block_col = both[:, 0], both[:, 1]
    per_dev = node_rows // BLK
    per_chip = CORES * per_dev
    line = NX * per_chip
    z_away = (block_row // per_chip - z) % NZ
    row_in = block_row % per_chip
    owner = block_col // per_dev
    col_in = block_col % per_dev
    dx, dy = (owner % NX - x) % NX, (owner // NX - y) % NY
    first_away, second_away = jnp.where(core == 0, dx, dy), jnp.where(core == 0, dy, dx)
    in_line = jnp.where(
        first_away == 2,
        6 * per_dev + tile_core * per_dev,
        3 * per_dev * tile_core + per_dev * jnp.minimum(first_away, 2),
    )
    forward = slot_table(
        live,
        second_away * line + in_line + col_in,
        chosen(z_away, [2 * per_chip, 0, 0, 0, 0, per_chip, per_chip, per_chip]) + row_in,
        chosen(z_away, [3, 3, 2, 1, 0, 1, 2, 3]),
        4,
    )
    upper = first_away >= NX // 2
    backward = slot_table(
        live,
        z_away * per_chip + row_in,
        (first_away - jnp.where((second_away % 2 == 1) & upper, NX // 2, 0)) * per_chip
        + jnp.where(second_away == 3, line // 2, 0)
        + tile_core * per_dev
        + col_in,
        jnp.where(
            second_away % 2 == 1,
            jnp.where((second_away == 1) == upper, 1, 2),
            chosen(second_away, [3]),
        ),
        4,
    )

    pieces, offsets = gather_plane(unit, near_first, far_first, near_second, far_second)
    half_chip = per_chip // 2
    *far, held = tile_product(
        *forward, vals, other_vals, pieces, offsets, 0, [half_chip] * 2, False
    )
    part = [None] * NZ
    for group, away in enumerate([(3, 5), (2, 6), (1, 7, 0)], 1):
        made = tile_product(
            *forward, vals, other_vals, [held], [], group, [per_chip] * len(away), False
        )
        for d, value in zip(away, made):
            part[d] = value
    neighbours = sum_z(part, far, along_z(1), along_z(-1))
    neighbours = own_rows(neighbours, core, node_rows, width)

    preact = jnp.dot(features, w_self, preferred_element_type=f32)
    preact = preact + jnp.dot(neighbours, w_neigh, preferred_element_type=f32)
    gate = jax.nn.sigmoid(preact)
    layer_out = (preact * gate).astype(bf16)
    slope_grad = (cotangent.astype(f32) * gate * (1.0 + preact * (1.0 - gate))).astype(bf16)
    contract_rows = (((0,), (0,)), ((), ()))
    contract_cols = (((1,), (1,)), ((), ()))
    neigh_grad = lax.dot_general(
        slope_grad, w_neigh, contract_cols, preferred_element_type=f32
    ).astype(bf16)
    grad_unit = own_half(neigh_grad, core, width)

    plane = NX * NY
    grads = [
        lax.dot_general(v, slope_grad, contract_rows, preferred_element_type=f32)
        .astype(bf16)
        .reshape(plane, width // plane, width)
        for v in (features, neighbours)
    ]
    grads = jnp.concatenate(grads, 1)
    pieces, offsets, total = gather_z(grad_unit, grads)
    term = exchange_z(total, 1)

    *far, held = tile_product(
        *backward,
        vals,
        other_vals,
        [kept(p) for p in pieces],
        offsets,
        0,
        [line // 2] * 2,
        True,
    )

    def group_of(index, held, cuts):
        return tile_product(*backward, vals, other_vals, [held], [], index, cuts, True)

    far[0], term = tied(far[0], term)
    total = widened(total, term)
    term = exchange_z(total, 2)
    sums = [total, term]

    def bound():
        total, term = sums
        one, three, term = tied(*group_of(2, held, [line // 2] * 2), term)
        total = widened(total, term)
        sums[:] = total, exchange_z(total, 4)
        return one, three

    def near(low, high):
        total, term = sums
        given, low, high, term = tied(held, low, high, term)
        sums[0] = widened(total, term)
        return group_of(3, given, [line])[0], low, high

    back = sum_four(
        near,
        lambda: group_of(1, held, [line // 2] * 2),
        bound,
        far,
        near_second,
        far_second,
    )
    strip = width // plane
    total = plane_whole(lax.dynamic_slice_in_dim(sums[0], core * strip, strip, 0))
    quarter = node_rows
    cut = [back[i * quarter : (i + 1) * quarter] for i in range(2 * NX)]
    back = sum_four(
        lambda low, high: (jnp.concatenate(cut[:2], 0), low, high),
        lambda: (cut[3], cut[6]),
        lambda: (cut[2], cut[7]),
        cut[4:6],
        near_first,
        far_first,
    )
    back, total = tied(back, total)
    other_total = swap(total)
    grad_self = jnp.where(core == 0, total, other_total).reshape(width, width).astype(f32)
    grad_neigh = jnp.where(core == 0, other_total, total).reshape(width, width).astype(f32)
    back_rows = own_rows(back, core, node_rows, width)
    own_grad = lax.dot_general(slope_grad, w_self, contract_cols, preferred_element_type=f32)
    grad_features = (own_grad + back_rows.astype(f32)).astype(bf16)
    return layer_out, grad_features, grad_self, grad_neigh


def solution(mesh):
    in_specs = (
        P(("row", "col"), None),
        P(),
        P(),
        P("row", "col", None, None, None),
        P("row", "col", None, None),
        P("row", "col"),
        P(("row", "col"), None),
    )
    out_specs = (P(("row", "col"), None), P(("row", "col"), None), P(), P())
    return jax.shard_map(
        per_device, mesh=mesh, in_specs=in_specs, out_specs=out_specs, check_vma=False
    )
```

```python
import functools

import jax
import jax.numpy as jnp
from jax import lax
from jax.experimental import pallas as pl
from jax.experimental.pallas import tpu as pltpu
from jax.sharding import PartitionSpec as P

AXES = ("row", "col")
NX, NY, NZ, CORES = 4, 4, 8, 2
BLK = 128
UNROLL = 8


def place(x, y, z, core):
    return ((z % NZ) * CORES + core) * (NX * NY) + (y % NY) * NX + x % NX


def pairs(move):
    return [
        (place(x, y, z, c), place(*move(x, y, z, c)))
        for z in range(NZ)
        for c in range(CORES)
        for y in range(NY)
        for x in range(NX)
    ]


def along_first(step):
    return pairs(
        lambda x, y, z, c: (x + step, y, z, c) if c == 0 else (x, y + step, z, c)
    )


def along_second(step):
    return pairs(
        lambda x, y, z, c: (x, y + step, z, c) if c == 0 else (x + step, y, z, c)
    )


def along_z(step):
    return pairs(lambda x, y, z, c: (x, y, z + step, c))


def send(value, moved):
    return lax.ppermute(value, AXES, moved)


def exchange_z(value, bit):
    return send(value, pairs(lambda x, y, z, c: (x, y, z ^ bit, c)))


def swap(value):
    return send(value, pairs(lambda x, y, z, c: (x, y, z, 1 - c)))


def tile_kernel(offsets, transposed, group, unroll, depth, cuts, *refs):
    table, bounds, vals_a, vals_b = refs[:4]
    refs = refs[4:]
    pieces, refs = refs[: len(offsets)], refs[len(offsets) :]
    if offsets:
        outs, held = refs[: len(cuts)], refs[len(cuts)]
        total, ring, ring_sem, sem = refs[len(cuts) + 1 :]
    else:
        held, outs = refs[0], refs[1 : len(cuts) + 1]
        total, ring, ring_sem = refs[len(cuts) + 1 :]
    copies = [
        pltpu.make_async_copy(p, held.at[pl.ds(o, p.shape[0])], sem.at[i])
        for i, (p, o) in enumerate(zip(pieces, offsets))
    ]
    for copy in copies:
        copy.start()
    blocks = sum(cuts)
    low, middle, high = [bounds[CORES * group + k] for k in range(CORES + 1)]
    first_steps = (middle - low + unroll - 1) // unroll
    steps = first_steps + (high - middle + unroll - 1) // unroll

    def begin(i):
        return jnp.where(i < first_steps, low + i * unroll, middle + (i - first_steps) * unroll)

    def fetch(i, vals):
        base = begin(i)
        room = lax.rem(i, depth)
        for u in range(unroll):
            pltpu.make_async_copy(
                vals.at[table[base + u] & 127], ring.at[room, u], ring_sem.at[room]
            ).start()

    def ahead(i):
        @pl.when(i < first_steps)
        def _():
            fetch(i, vals_a)

        @pl.when((i >= first_steps) & (i < steps))
        def _():
            fetch(i, vals_b)

    for i in range(depth - 1):
        ahead(jnp.int32(i))

    @pl.loop(0, blocks)
    def _(i):
        total[pl.ds(i * BLK, BLK), :] = jnp.zeros((BLK, total.shape[1]), jnp.float32)

    for copy in copies:
        copy.wait()
    dims = (((0,), (0,)), ((), ())) if transposed else (((1,), (0,)), ((), ()))

    @pl.loop(0, steps)
    def _(i):
        ahead(i + depth - 1)
        room = lax.rem(i, depth)
        pltpu.make_async_copy(
            vals_a.at[pl.ds(0, unroll)], ring.at[room], ring_sem.at[room]
        ).wait()
        base = begin(i)
        limit = jnp.where(i < first_steps, middle, high)
        for u in range(unroll):
            entry = table[base + u]
            source = lax.shift_right_logical(entry, 7) & 63
            target = jnp.where(base + u < limit, lax.shift_right_logical(entry, 13), blocks)
            taken = held[pl.ds(pl.multiple_of(source * BLK, BLK), BLK), :]
            product = lax.dot_general(
                ring[room, u], taken, dims, preferred_element_type=jnp.float32
            )
            placed = pl.ds(pl.multiple_of(target * BLK, BLK), BLK)
            total[placed, :] = total[placed, :] + product

    at = 0
    for out, size in zip(outs, cuts):
        first = at

        @pl.loop(0, size)
        def _(i):
            rows = pl.ds((first + i) * BLK, BLK)
            out[pl.ds(i * BLK, BLK), :] = total[rows, :].astype(jnp.bfloat16)

        at += size


def kept(value):
    return pltpu.with_memory_space_constraint(value, pltpu.HBM)


def tile_product(table, bounds, vals_a, vals_b, sources, offsets, group, cuts, transposed):
    unroll, depth = UNROLL, 3
    width = sources[0].shape[1]
    blocks = sum(cuts)
    vmem = pl.BlockSpec(memory_space=pltpu.VMEM)
    hbm = pl.BlockSpec(memory_space=pltpu.HBM)
    in_specs = [pl.BlockSpec(memory_space=pltpu.SMEM)] * 2 + [hbm] * 2
    out_shape = [jax.ShapeDtypeStruct((c * BLK, width), jnp.bfloat16) for c in cuts]
    scratch = [
        pltpu.VMEM(((blocks + 1) * BLK, width), jnp.float32),
        pltpu.VMEM((depth, unroll, BLK, BLK), jnp.bfloat16),
        pltpu.SemaphoreType.DMA((depth,)),
    ]
    if offsets:
        rows = max(o + p.shape[0] for o, p in zip(offsets, sources))
        in_specs += [pl.BlockSpec(memory_space=pl.ANY)] * len(sources)
        out_shape.append(jax.ShapeDtypeStruct((rows, width), jnp.bfloat16))
        scratch.append(pltpu.SemaphoreType.DMA((len(sources),)))
    else:
        in_specs += [vmem]
    return pl.pallas_call(
        functools.partial(
            tile_kernel, tuple(offsets), transposed, group, unroll, depth, tuple(cuts)
        ),
        out_shape=out_shape,
        in_specs=in_specs,
        out_specs=[vmem] * len(out_shape),
        scratch_shapes=scratch,
        compiler_params=pltpu.CompilerParams(vmem_limit_bytes=20 * 2**20),
        cost_estimate=pl.CostEstimate(
            flops=2 * BLK * BLK * width * 8 * blocks, bytes_accessed=2**20, transcendentals=0
        ),
        name="tile_product",
    )(table, bounds, *[kept(v) for v in (vals_a, vals_b)], *sources)


def chosen(index, values):
    return sum(jnp.where(index == i, v, 0) for i, v in enumerate(values) if v) + 0 * index


def slot_table(live, source, target, group, groups):
    slots = source.shape[1]
    slot = jnp.arange(slots, dtype=jnp.int32)[None]
    tile = jnp.arange(CORES, dtype=jnp.int32)[:, None]
    key = jnp.where(slot < live[:, None], group * CORES + tile, groups * CORES).reshape(-1)
    entry = (slot + source * 128 + target * 8192).reshape(-1)
    place = jnp.arange(CORES * slots, dtype=jnp.int32)
    before = key[None] < key[:, None]
    before |= (key[None] == key[:, None]) & (place[None] < place[:, None])
    rank = jnp.sum(before.astype(jnp.int32), axis=1)
    seat = jnp.arange(CORES * slots + UNROLL, dtype=jnp.int32)[:, None]
    table = jnp.sum(jnp.where(rank[None] == seat, entry[None], 0), axis=1)
    starts = jnp.arange(groups * CORES + 1, dtype=jnp.int32)[:, None]
    bounds = jnp.sum((key[None] < starts).astype(jnp.int32), axis=1)
    return table, bounds


def tied(*values):
    return lax.optimization_barrier(values)


def gather_plane(unit, first_ahead, first_behind, second_ahead, second_behind):
    half = unit.shape[0] // 2
    last, following = send(unit, first_ahead), send(unit, first_behind)
    last, following = tied(last, following)
    near = [unit, following, last]
    near = jnp.concatenate([v[:half] for v in near] + [v[half:] for v in near], 0)
    behind_near, ahead_near = send(near, second_behind), send(near, second_ahead)
    across = [send(following[:half], first_behind), send(last[half:], first_ahead)]
    across = jnp.concatenate(across, 0)
    behind_across, ahead_across = send(across, second_behind), send(across, second_ahead)
    middle = near.shape[0] // 2
    behind_near, ahead_near = tied(behind_near, ahead_near)
    far = [send(behind_near[:middle], second_behind), send(ahead_near[middle:], second_ahead)]
    far_across = [
        send(behind_across[:half], second_behind),
        send(ahead_across[half:], second_ahead),
    ]
    lines = [[near, across], [behind_near, behind_across], [*far, *far_across]]
    lines += [[ahead_near, ahead_across]]
    pieces, offsets = [], []
    at = 0
    for line in lines:
        for piece in line:
            pieces.append(piece)
            offsets.append(at)
            at += piece.shape[0]
    return pieces, offsets


def widened(*values):
    return functools.reduce(lambda a, b: a + b, [v.astype(jnp.float32) for v in values]).astype(
        jnp.bfloat16
    )


def sum_four(near, free, bound, far, ahead, behind):
    top, bottom = send(far[0], ahead), send(far[1], behind)
    low, high = free()
    low, high = send(low, ahead), send(high, behind)
    one, three = bound()
    top, bottom = tied(top, bottom)
    top, bottom = tied(widened(one, top), widened(three, bottom))
    low, high = tied(low, high)
    near, low, high = near(low, high)
    half = near.shape[0] // 2
    top, bottom = tied(send(top, ahead), send(bottom, behind))
    first = widened(near[:half], top, high)
    second = widened(near[half:], bottom, low)
    return jnp.concatenate([first, second], 0)


def sum_z(part, far, ahead, behind):
    half = part[0].shape[0] // 2
    top, bottom = tied(send(far[0], ahead), send(far[1], behind))
    to_ahead = jnp.concatenate([widened(part[3][:half], top), part[3][half:]], 0)
    to_behind = jnp.concatenate([part[5][:half], widened(part[5][half:], bottom)], 0)
    for d in (2, 1, 0):
        to_ahead, to_behind = tied(to_ahead, to_behind)
        from_behind, from_ahead = tied(send(to_ahead, ahead), send(to_behind, behind))
        if d:
            to_ahead = widened(part[d], from_behind)
            to_behind = widened(part[NZ - d], from_ahead)
    return widened(part[0], from_behind, from_ahead)


def gather_z(value, grads):
    rows = value.shape[0]
    half = rows // 2
    ahead, behind = along_z(1), along_z(-1)
    top, bottom = value[:half], value[half:]
    pieces, offsets = [value], [0]
    lead, rest = [top, bottom], [bottom, top]
    for d in range(1, NZ // 2):
        lead = [send(lead[0], behind), send(lead[1], ahead)]
        if d == 1:
            *lead, grads = tied(*lead, grads)
            grads = lax.all_to_all(grads, "col", 0, 0, tiled=True)
        if d == 2:
            *lead, grads = tied(*lead, grads)
            grads = summed(grads)
            term = exchange_z(grads, 1)
        if d == 3:
            *lead, term = tied(*lead, term)
            grads = widened(grads, term)
            term = exchange_z(grads, 2)
        rest = [send(rest[0], behind), send(rest[1], ahead)]
        pieces += [lead[0], rest[0], rest[1], lead[1]]
        offsets += [d * rows, d * rows + half, (NZ - d) * rows, (NZ - d) * rows + half]
    lead = [send(lead[0], behind), send(lead[1], ahead)]
    *lead, term = tied(*lead, term)
    pieces += lead
    offsets += [NZ // 2 * rows, NZ // 2 * rows + half]
    return pieces, offsets, widened(grads, term)


def own_rows(halves, core, node_rows, width):
    half = width // 2
    mine = lax.dynamic_slice_in_dim(halves, core * node_rows, node_rows, 0)
    other = swap(lax.dynamic_slice_in_dim(halves, (1 - core) * node_rows, node_rows, 0))
    first = jnp.where(core == 0, mine, other)
    second = jnp.where(core == 0, other, mine)
    return jnp.concatenate([first, second], 1)


def own_half(rows, core, width):
    half = width // 2
    mine = lax.dynamic_slice_in_dim(rows, core * half, half, 1)
    other = swap(lax.dynamic_slice_in_dim(rows, (1 - core) * half, half, 1))
    first = jnp.where(core == 0, mine, other)
    second = jnp.where(core == 0, other, mine)
    return jnp.concatenate([first, second], 0)


def summed(parts):
    return jnp.sum(parts.astype(jnp.float32), axis=0).astype(parts.dtype)


def plane_whole(value):
    spread = jnp.broadcast_to(value[None], (NX * NY, *value.shape))
    return lax.all_to_all(spread, "col", 0, 0, tiled=True)


def per_device(features, w_self, w_neigh, block_vals, block_coords, block_count, cotangent):
    bf16, f32 = jnp.bfloat16, jnp.float32
    node_rows, width = features.shape
    row, col = lax.axis_index("row"), lax.axis_index("col")
    z, core = row // CORES, row % CORES
    y, x = col // NX, col % NX
    near_first, near_second = along_first(1), along_second(1)
    far_first, far_second = along_first(-1), along_second(-1)

    vals = block_vals[0, 0]
    slots = vals.shape[0]
    facts = jnp.concatenate(
        [block_coords[0, 0], jnp.broadcast_to(block_count[0, 0], (1, slots))], 0
    )
    unit = own_half(features, core, width)
    later_facts, later_vals, unit = lax.optimization_barrier((facts, vals, unit))
    other_facts = swap(later_facts)
    other_vals = swap(later_vals)
    both = jnp.stack([facts, other_facts])
    live = both[:, 2, 0]
    tile_core = jnp.stack([core, 1 - core])[:, None]
    block_row, block_col = both[:, 0], both[:, 1]
    per_dev = node_rows // BLK
    per_chip = CORES * per_dev
    line = NX * per_chip
    z_away = (block_row // per_chip - z) % NZ
    row_in = block_row % per_chip
    owner = block_col // per_dev
    col_in = block_col % per_dev
    dx, dy = (owner % NX - x) % NX, (owner // NX - y) % NY
    first_away, second_away = jnp.where(core == 0, dx, dy), jnp.where(core == 0, dy, dx)
    in_line = jnp.where(
        first_away == 2,
        6 * per_dev + tile_core * per_dev,
        3 * per_dev * tile_core + per_dev * jnp.minimum(first_away, 2),
    )
    forward = slot_table(
        live,
        second_away * line + in_line + col_in,
        jnp.where(z_away > NZ // 2, per_chip, 0) + row_in,
        jnp.abs(NZ // 2 - z_away),
        5,
    )
    upper = first_away >= NX // 2
    backward = slot_table(
        live,
        z_away * per_chip + row_in,
        (first_away - jnp.where((second_away % 2 == 1) & upper, NX // 2, 0)) * per_chip
        + jnp.where(second_away == 3, line // 2, 0)
        + tile_core * per_dev
        + col_in,
        jnp.where(
            second_away % 2 == 1,
            jnp.where((second_away == 1) == upper, 1, 2),
            chosen(second_away, [3]),
        ),
        4,
    )

    pieces, offsets = gather_plane(unit, near_first, far_first, near_second, far_second)
    half_chip = per_chip // 2
    *far, held = tile_product(
        *forward, vals, other_vals, pieces, offsets, 0, [half_chip] * 2, False
    )
    part = [None] * NZ
    for group, away in enumerate([(3, 5), (2, 6), (1, 7), (0,)], 1):
        made = tile_product(
            *forward, vals, other_vals, [held], [], group, [per_chip] * len(away), False
        )
        for d, value in zip(away, made):
            part[d] = value
    neighbours = sum_z(part, far, along_z(1), along_z(-1))
    neighbours = own_rows(neighbours, core, node_rows, width)

    preact = jnp.dot(features, w_self, preferred_element_type=f32)
    preact = preact + jnp.dot(neighbours, w_neigh, preferred_element_type=f32)
    gate = jax.nn.sigmoid(preact)
    layer_out = (preact * gate).astype(bf16)
    slope_grad = (cotangent.astype(f32) * gate * (1.0 + preact * (1.0 - gate))).astype(bf16)
    contract_rows = (((0,), (0,)), ((), ()))
    contract_cols = (((1,), (1,)), ((), ()))
    neigh_grad = lax.dot_general(
        slope_grad, w_neigh, contract_cols, preferred_element_type=f32
    ).astype(bf16)
    grad_unit = own_half(neigh_grad, core, width)

    plane = NX * NY
    grads = [
        lax.dot_general(v, slope_grad, contract_rows, preferred_element_type=f32).astype(bf16)
        for v in (features, neighbours)
    ]
    mine = jnp.where(core == 0, grads[0], grads[1])
    other = swap(jnp.where(core == 0, grads[1], grads[0]))
    grads = widened(mine, other).reshape(plane, width // plane, width)
    pieces, offsets, total = gather_z(grad_unit, grads)
    term = exchange_z(total, 4)

    *far, held = tile_product(
        *backward,
        vals,
        other_vals,
        [kept(p) for p in pieces],
        offsets,
        0,
        [line // 2] * 2,
        True,
    )

    def group_of(index, held, cuts):
        return tile_product(*backward, vals, other_vals, [held], [], index, cuts, True)

    far[0], term = tied(far[0], term)
    total = plane_whole(widened(total, term))

    def near(low, high):
        given, low, high = tied(held, low, high)
        return group_of(3, given, [line])[0], low, high

    back = sum_four(
        near,
        lambda: group_of(1, held, [line // 2] * 2),
        lambda: group_of(2, held, [line // 2] * 2),
        far,
        near_second,
        far_second,
    )
    back, total = tied(back, total)
    other_total = swap(total)
    quarter = node_rows
    cut = [back[i * quarter : (i + 1) * quarter] for i in range(2 * NX)]
    back = sum_four(
        lambda low, high: (jnp.concatenate(cut[:2], 0), low, high),
        lambda: (cut[3], cut[6]),
        lambda: (cut[2], cut[7]),
        cut[4:6],
        near_first,
        far_first,
    )
    grad_self = jnp.where(core == 0, total, other_total).reshape(width, width).astype(f32)
    grad_neigh = jnp.where(core == 0, other_total, total).reshape(width, width).astype(f32)
    back, grad_self, grad_neigh = tied(back, grad_self, grad_neigh)
    back_rows = own_rows(back, core, node_rows, width)
    own_grad = lax.dot_general(slope_grad, w_self, contract_cols, preferred_element_type=f32)
    grad_features = (own_grad + back_rows.astype(f32)).astype(bf16)
    return layer_out, grad_features, grad_self, grad_neigh


def solution(mesh):
    in_specs = (
        P(("row", "col"), None),
        P(),
        P(),
        P("row", "col", None, None, None),
        P("row", "col", None, None),
        P("row", "col"),
        P(("row", "col"), None),
    )
    out_specs = (P(("row", "col"), None), P(("row", "col"), None), P(), P())
    return jax.shard_map(
        per_device, mesh=mesh, in_specs=in_specs, out_specs=out_specs, check_vma=False
    )
```

```python
import functools

import jax
import jax.numpy as jnp
from jax import lax
from jax.experimental import pallas as pl
from jax.experimental.pallas import tpu as pltpu
from jax.sharding import PartitionSpec as P

AXES = ("row", "col")
NX, NY, NZ, CORES = 4, 4, 8, 2
BLK = 128
UNROLL = 8


def place(x, y, z, core):
    return ((z % NZ) * CORES + core) * (NX * NY) + (y % NY) * NX + x % NX


def pairs(move):
    return [
        (place(x, y, z, c), place(*move(x, y, z, c)))
        for z in range(NZ)
        for c in range(CORES)
        for y in range(NY)
        for x in range(NX)
    ]


def along_first(step):
    return pairs(
        lambda x, y, z, c: (x + step, y, z, c) if c == 0 else (x, y + step, z, c)
    )


def along_second(step):
    return pairs(
        lambda x, y, z, c: (x, y + step, z, c) if c == 0 else (x + step, y, z, c)
    )


def along_z(step):
    return pairs(lambda x, y, z, c: (x, y, z + step, c))


def send(value, moved):
    return lax.ppermute(value, AXES, moved)


def exchange_z(value, bit):
    return send(value, pairs(lambda x, y, z, c: (x, y, z ^ bit, c)))


def swap(value):
    return send(value, pairs(lambda x, y, z, c: (x, y, z, 1 - c)))


def tile_kernel(offsets, transposed, group, unroll, depth, cuts, *refs):
    table, bounds, vals_a, vals_b = refs[:4]
    refs = refs[4:]
    pieces, refs = refs[: len(offsets)], refs[len(offsets) :]
    if offsets:
        outs, held = refs[: len(cuts)], refs[len(cuts)]
        total, ring, ring_sem, sem = refs[len(cuts) + 1 :]
    else:
        held, outs = refs[0], refs[1 : len(cuts) + 1]
        total, ring, ring_sem = refs[len(cuts) + 1 :]
    copies = [
        pltpu.make_async_copy(p, held.at[pl.ds(o, p.shape[0])], sem.at[i])
        for i, (p, o) in enumerate(zip(pieces, offsets))
    ]
    for copy in copies:
        copy.start()
    blocks = sum(cuts)
    low, middle, high = [bounds[CORES * group + k] for k in range(CORES + 1)]
    first_steps = (middle - low + unroll - 1) // unroll
    steps = first_steps + (high - middle + unroll - 1) // unroll

    def begin(i):
        return jnp.where(i < first_steps, low + i * unroll, middle + (i - first_steps) * unroll)

    def fetch(i, vals):
        base = begin(i)
        room = lax.rem(i, depth)
        for u in range(unroll):
            pltpu.make_async_copy(
                vals.at[table[base + u] & 127], ring.at[room, u], ring_sem.at[room]
            ).start()

    def ahead(i):
        @pl.when(i < first_steps)
        def _():
            fetch(i, vals_a)

        @pl.when((i >= first_steps) & (i < steps))
        def _():
            fetch(i, vals_b)

    for i in range(depth - 1):
        ahead(jnp.int32(i))

    @pl.loop(0, blocks)
    def _(i):
        total[pl.ds(i * BLK, BLK), :] = jnp.zeros((BLK, total.shape[1]), jnp.float32)

    for copy in copies:
        copy.wait()
    dims = (((0,), (0,)), ((), ())) if transposed else (((1,), (0,)), ((), ()))

    @pl.loop(0, steps)
    def _(i):
        ahead(i + depth - 1)
        room = lax.rem(i, depth)
        pltpu.make_async_copy(
            vals_a.at[pl.ds(0, unroll)], ring.at[room], ring_sem.at[room]
        ).wait()
        base = begin(i)
        limit = jnp.where(i < first_steps, middle, high)
        for u in range(unroll):
            entry = table[base + u]
            source = lax.shift_right_logical(entry, 7) & 63
            target = jnp.where(base + u < limit, lax.shift_right_logical(entry, 13), blocks)
            taken = held[pl.ds(pl.multiple_of(source * BLK, BLK), BLK), :]
            product = lax.dot_general(
                ring[room, u], taken, dims, preferred_element_type=jnp.float32
            )
            placed = pl.ds(pl.multiple_of(target * BLK, BLK), BLK)
            total[placed, :] = total[placed, :] + product

    at = 0
    for out, size in zip(outs, cuts):
        first = at

        @pl.loop(0, size)
        def _(i):
            rows = pl.ds((first + i) * BLK, BLK)
            out[pl.ds(i * BLK, BLK), :] = total[rows, :].astype(jnp.bfloat16)

        at += size


def kept(value):
    return pltpu.with_memory_space_constraint(value, pltpu.HBM)


def tile_product(table, bounds, vals_a, vals_b, sources, offsets, group, cuts, transposed):
    unroll, depth = UNROLL, 3
    width = sources[0].shape[1]
    blocks = sum(cuts)
    vmem = pl.BlockSpec(memory_space=pltpu.VMEM)
    hbm = pl.BlockSpec(memory_space=pltpu.HBM)
    in_specs = [pl.BlockSpec(memory_space=pltpu.SMEM)] * 2 + [hbm] * 2
    out_shape = [jax.ShapeDtypeStruct((c * BLK, width), jnp.bfloat16) for c in cuts]
    scratch = [
        pltpu.VMEM(((blocks + 1) * BLK, width), jnp.float32),
        pltpu.VMEM((depth, unroll, BLK, BLK), jnp.bfloat16),
        pltpu.SemaphoreType.DMA((depth,)),
    ]
    if offsets:
        rows = max(o + p.shape[0] for o, p in zip(offsets, sources))
        in_specs += [pl.BlockSpec(memory_space=pl.ANY)] * len(sources)
        out_shape.append(jax.ShapeDtypeStruct((rows, width), jnp.bfloat16))
        scratch.append(pltpu.SemaphoreType.DMA((len(sources),)))
    else:
        in_specs += [vmem]
    return pl.pallas_call(
        functools.partial(
            tile_kernel, tuple(offsets), transposed, group, unroll, depth, tuple(cuts)
        ),
        out_shape=out_shape,
        in_specs=in_specs,
        out_specs=[vmem] * len(out_shape),
        scratch_shapes=scratch,
        compiler_params=pltpu.CompilerParams(vmem_limit_bytes=20 * 2**20),
        cost_estimate=pl.CostEstimate(
            flops=2 * BLK * BLK * width * 8 * blocks, bytes_accessed=2**20, transcendentals=0
        ),
        name="tile_product",
    )(table, bounds, *[kept(v) for v in (vals_a, vals_b)], *sources)


def chosen(index, values):
    return sum(jnp.where(index == i, v, 0) for i, v in enumerate(values) if v) + 0 * index


def slot_table(live, source, target, group, groups):
    slots = source.shape[1]
    slot = jnp.arange(slots, dtype=jnp.int32)[None]
    tile = jnp.arange(CORES, dtype=jnp.int32)[:, None]
    key = jnp.where(slot < live[:, None], group * CORES + tile, groups * CORES).reshape(-1)
    entry = (slot + source * 128 + target * 8192).reshape(-1)
    place = jnp.arange(CORES * slots, dtype=jnp.int32)
    before = key[None] < key[:, None]
    before |= (key[None] == key[:, None]) & (place[None] < place[:, None])
    rank = jnp.sum(before.astype(jnp.int32), axis=1)
    seat = jnp.arange(CORES * slots + UNROLL, dtype=jnp.int32)[:, None]
    table = jnp.sum(jnp.where(rank[None] == seat, entry[None], 0), axis=1)
    starts = jnp.arange(groups * CORES + 1, dtype=jnp.int32)[:, None]
    bounds = jnp.sum((key[None] < starts).astype(jnp.int32), axis=1)
    return table, bounds


def tied(*values):
    return lax.optimization_barrier(values)


def gather_plane(unit, first_ahead, first_behind, second_ahead, second_behind):
    half = unit.shape[0] // 2
    last, following = send(unit, first_ahead), send(unit, first_behind)
    last, following = tied(last, following)
    near = [unit, following, last]
    near = jnp.concatenate([v[:half] for v in near] + [v[half:] for v in near], 0)
    behind_near, ahead_near = send(near, second_behind), send(near, second_ahead)
    across = [send(following[:half], first_behind), send(last[half:], first_ahead)]
    across = jnp.concatenate(across, 0)
    behind_across, ahead_across = send(across, second_behind), send(across, second_ahead)
    middle = near.shape[0] // 2
    behind_near, ahead_near = tied(behind_near, ahead_near)
    far = [send(behind_near[:middle], second_behind), send(ahead_near[middle:], second_ahead)]
    far_across = [
        send(behind_across[:half], second_behind),
        send(ahead_across[half:], second_ahead),
    ]
    lines = [[near, across], [behind_near, behind_across], [*far, *far_across]]
    lines += [[ahead_near, ahead_across]]
    pieces, offsets = [], []
    at = 0
    for line in lines:
        for piece in line:
            pieces.append(piece)
            offsets.append(at)
            at += piece.shape[0]
    return pieces, offsets


def widened(*values):
    return functools.reduce(lambda a, b: a + b, [v.astype(jnp.float32) for v in values]).astype(
        jnp.bfloat16
    )


def sum_four(near, free, bound, far, ahead, behind):
    top, bottom = send(far[0], ahead), send(far[1], behind)
    low, high = free()
    low, high = send(low, ahead), send(high, behind)
    one, three = bound()
    top, bottom = tied(top, bottom)
    top, bottom = tied(widened(one, top), widened(three, bottom))
    low, high = tied(low, high)
    near, low, high = near(low, high)
    half = near.shape[0] // 2
    top, bottom = tied(send(top, ahead), send(bottom, behind))
    first = widened(near[:half], top, high)
    second = widened(near[half:], bottom, low)
    return jnp.concatenate([first, second], 0)


def sum_small(value, ahead, behind):
    rows = value.shape[0] // 4
    half = rows // 2
    part = [value[i * rows : (i + 1) * rows] for i in range(4)]
    top, bottom = tied(send(part[2][:half], ahead), send(part[2][half:], behind))
    to_ahead = jnp.concatenate([widened(part[1][:half], top), part[1][half:]], 0)
    to_behind = jnp.concatenate([part[3][:half], widened(part[3][half:], bottom)], 0)
    to_ahead, to_behind = tied(to_ahead, to_behind)
    from_behind, from_ahead = tied(send(to_ahead, ahead), send(to_behind, behind))
    return widened(part[0], from_behind, from_ahead)


def sum_z(part, far, ahead, behind):
    half = part[0].shape[0] // 2
    top, bottom = tied(send(far[0], ahead), send(far[1], behind))
    to_ahead = jnp.concatenate([widened(part[3][:half], top), part[3][half:]], 0)
    to_behind = jnp.concatenate([part[5][:half], widened(part[5][half:], bottom)], 0)
    for d in (2, 1, 0):
        to_ahead, to_behind = tied(to_ahead, to_behind)
        from_behind, from_ahead = tied(send(to_ahead, ahead), send(to_behind, behind))
        if d:
            to_ahead = widened(part[d], from_behind)
            to_behind = widened(part[NZ - d], from_ahead)
    return widened(part[0], from_behind, from_ahead)


def gather_z(value, grads):
    rows = value.shape[0]
    half = rows // 2
    ahead, behind = along_z(1), along_z(-1)
    pieces, offsets = [value], [0]
    following, last = value, value
    for d in range(1, NZ // 2):
        following, last = send(following, behind), send(last, ahead)
        if d == 2:
            following, last = tied(following, last)
        else:
            following, last, grads = tied(following, last, grads)
        if d == 1:
            grads = lax.all_to_all(grads, "col", 0, 0, tiled=True)
        pieces += [following, last]
        offsets += [d * rows, (NZ - d) * rows]
    grads = summed(grads)
    term = exchange_z(grads, 1)
    lead = [send(following[:half], behind), send(last[half:], ahead)]
    *lead, term = tied(*lead, term)
    pieces += lead
    offsets += [NZ // 2 * rows, NZ // 2 * rows + half]
    return pieces, offsets, widened(grads, term)


def own_rows(halves, core, node_rows, width):
    half = width // 2
    mine = lax.dynamic_slice_in_dim(halves, core * node_rows, node_rows, 0)
    other = swap(lax.dynamic_slice_in_dim(halves, (1 - core) * node_rows, node_rows, 0))
    first = jnp.where(core == 0, mine, other)
    second = jnp.where(core == 0, other, mine)
    return jnp.concatenate([first, second], 1)


def own_half(rows, core, width):
    half = width // 2
    mine = lax.dynamic_slice_in_dim(rows, core * half, half, 1)
    other = swap(lax.dynamic_slice_in_dim(rows, (1 - core) * half, half, 1))
    first = jnp.where(core == 0, mine, other)
    second = jnp.where(core == 0, other, mine)
    return jnp.concatenate([first, second], 0)


def summed(parts):
    return jnp.sum(parts.astype(jnp.float32), axis=0).astype(parts.dtype)


def plane_whole(value):
    spread = jnp.broadcast_to(value[None], (NX * NY, *value.shape))
    return lax.all_to_all(spread, "col", 0, 0, tiled=True)


def per_device(features, w_self, w_neigh, block_vals, block_coords, block_count, cotangent):
    bf16, f32 = jnp.bfloat16, jnp.float32
    node_rows, width = features.shape
    row, col = lax.axis_index("row"), lax.axis_index("col")
    z, core = row // CORES, row % CORES
    y, x = col // NX, col % NX
    near_first, near_second = along_first(1), along_second(1)
    far_first, far_second = along_first(-1), along_second(-1)

    vals = block_vals[0, 0]
    slots = vals.shape[0]
    facts = jnp.concatenate(
        [block_coords[0, 0], jnp.broadcast_to(block_count[0, 0], (1, slots))], 0
    )
    unit = own_half(features, core, width)
    later_facts, later_vals, unit = lax.optimization_barrier((facts, vals, unit))
    other_facts = swap(later_facts)
    other_vals = swap(later_vals)
    both = jnp.stack([facts, other_facts])
    live = both[:, 2, 0]
    tile_core = jnp.stack([core, 1 - core])[:, None]
    block_row, block_col = both[:, 0], both[:, 1]
    per_dev = node_rows // BLK
    per_chip = CORES * per_dev
    line = NX * per_chip
    z_away = (block_row // per_chip - z) % NZ
    row_in = block_row % per_chip
    owner = block_col // per_dev
    col_in = block_col % per_dev
    dx, dy = (owner % NX - x) % NX, (owner // NX - y) % NY
    first_away, second_away = jnp.where(core == 0, dx, dy), jnp.where(core == 0, dy, dx)
    in_line = jnp.where(
        first_away == 2,
        6 * per_dev + tile_core * per_dev,
        3 * per_dev * tile_core + per_dev * jnp.minimum(first_away, 2),
    )
    forward = slot_table(
        live,
        second_away * line + in_line + col_in,
        jnp.where(z_away > NZ // 2, per_chip, 0) + row_in,
        jnp.abs(NZ // 2 - z_away),
        5,
    )
    upper = first_away >= NX // 2
    backward = slot_table(
        live,
        z_away * per_chip + row_in,
        (first_away - jnp.where((second_away % 2 == 1) & upper, NX // 2, 0)) * per_chip
        + jnp.where(second_away == 3, line // 2, 0)
        + tile_core * per_dev
        + col_in,
        jnp.where(
            second_away % 2 == 1,
            jnp.where((second_away == 1) == upper, 1, 2),
            chosen(second_away, [3]),
        ),
        4,
    )

    pieces, offsets = gather_plane(unit, near_first, far_first, near_second, far_second)
    half_chip = per_chip // 2
    *far, held = tile_product(
        *forward, vals, other_vals, pieces, offsets, 0, [half_chip] * 2, False
    )
    part = [None] * NZ
    for group, away in enumerate([(3, 5), (2, 6), (1, 7), (0,)], 1):
        made = tile_product(
            *forward, vals, other_vals, [held], [], group, [per_chip] * len(away), False
        )
        for d, value in zip(away, made):
            part[d] = value
    neighbours = sum_z(part, far, along_z(1), along_z(-1))
    neighbours = own_rows(neighbours, core, node_rows, width)

    preact = jnp.dot(features, w_self, preferred_element_type=f32)
    preact = preact + jnp.dot(neighbours, w_neigh, preferred_element_type=f32)
    gate = jax.nn.sigmoid(preact)
    layer_out = (preact * gate).astype(bf16)
    slope_grad = (cotangent.astype(f32) * gate * (1.0 + preact * (1.0 - gate))).astype(bf16)
    contract_rows = (((0,), (0,)), ((), ()))
    contract_cols = (((1,), (1,)), ((), ()))
    neigh_grad = lax.dot_general(
        slope_grad, w_neigh, contract_cols, preferred_element_type=f32
    ).astype(bf16)
    grad_unit = own_half(neigh_grad, core, width)

    plane = NX * NY
    grads = [
        lax.dot_general(v, slope_grad, contract_rows, preferred_element_type=f32).astype(bf16)
        for v in (features, neighbours)
    ]
    mine = jnp.where(core == 0, grads[0], grads[1])
    other = swap(jnp.where(core == 0, grads[1], grads[0]))
    grads = widened(mine, other).reshape(plane, width // plane, width)
    pieces, offsets, total = gather_z(grad_unit, grads)
    term = exchange_z(total, 2)

    *far, held = tile_product(
        *backward,
        vals,
        other_vals,
        [kept(p) for p in pieces],
        offsets,
        0,
        [line // 2] * 2,
        True,
    )

    def group_of(index, held, cuts):
        return tile_product(*backward, vals, other_vals, [held], [], index, cuts, True)

    far[0], term = tied(far[0], term)
    total = widened(total, term)
    sums = [total, exchange_z(total, 4)]

    def bound():
        total, term = sums
        one, three, term = tied(*group_of(2, held, [line // 2] * 2), term)
        sums[:] = [plane_whole(widened(total, term))]
        return one, three

    def near(low, high):
        given, low, high = tied(held, low, high)
        return group_of(3, given, [line])[0], low, high

    back = sum_four(
        near,
        lambda: group_of(1, held, [line // 2] * 2),
        bound,
        far,
        near_second,
        far_second,
    )
    back, total = tied(back, sums[0])
    other_total = swap(total)
    back = sum_small(back, near_first, far_first)
    grad_self = jnp.where(core == 0, total, other_total).reshape(width, width).astype(f32)
    grad_neigh = jnp.where(core == 0, other_total, total).reshape(width, width).astype(f32)
    back, grad_self, grad_neigh = tied(back, grad_self, grad_neigh)
    back_rows = own_rows(back, core, node_rows, width)
    own_grad = lax.dot_general(slope_grad, w_self, contract_cols, preferred_element_type=f32)
    grad_features = (own_grad + back_rows.astype(f32)).astype(bf16)
    return layer_out, grad_features, grad_self, grad_neigh


def solution(mesh):
    in_specs = (
        P(("row", "col"), None),
        P(),
        P(),
        P("row", "col", None, None, None),
        P("row", "col", None, None),
        P("row", "col"),
        P(("row", "col"), None),
    )
    out_specs = (P(("row", "col"), None), P(("row", "col"), None), P(), P())
    return jax.shard_map(
        per_device, mesh=mesh, in_specs=in_specs, out_specs=out_specs, check_vma=False
    )
```

```python
import functools

import jax
import jax.numpy as jnp
from jax import lax
from jax.experimental import pallas as pl
from jax.experimental.pallas import tpu as pltpu
from jax.sharding import PartitionSpec as P

AXES = ("row", "col")
NX, NY, NZ, CORES = 4, 4, 8, 2
BLK = 128
UNROLL = 16


def place(x, y, z, core):
    return ((z % NZ) * CORES + core) * (NX * NY) + (y % NY) * NX + x % NX


def pairs(move):
    return [
        (place(x, y, z, c), place(*move(x, y, z, c)))
        for z in range(NZ)
        for c in range(CORES)
        for y in range(NY)
        for x in range(NX)
    ]


def along_first(step):
    return pairs(
        lambda x, y, z, c: (x + step, y, z, c) if c == 0 else (x, y + step, z, c)
    )


def along_second(step):
    return pairs(
        lambda x, y, z, c: (x, y + step, z, c) if c == 0 else (x + step, y, z, c)
    )


def along_z(step):
    return pairs(lambda x, y, z, c: (x, y, z + step, c))


def send(value, moved):
    return lax.ppermute(value, AXES, moved)


def exchange_z(value, bit):
    return send(value, pairs(lambda x, y, z, c: (x, y, z ^ bit, c)))


def swap(value):
    return send(value, pairs(lambda x, y, z, c: (x, y, z, 1 - c)))


def tile_kernel(offsets, transposed, group, unroll, depth, cuts, *refs):
    table, bounds, vals_a, vals_b = refs[:4]
    refs = refs[4:]
    pieces, refs = refs[: len(offsets)], refs[len(offsets) :]
    if offsets:
        outs, held = refs[: len(cuts)], refs[len(cuts)]
        total, ring, ring_sem, sem = refs[len(cuts) + 1 :]
    else:
        held, outs = refs[0], refs[1 : len(cuts) + 1]
        total, ring, ring_sem = refs[len(cuts) + 1 :]
    copies = [
        pltpu.make_async_copy(p, held.at[pl.ds(o, p.shape[0])], sem.at[i])
        for i, (p, o) in enumerate(zip(pieces, offsets))
    ]
    for copy in copies:
        copy.start()
    blocks = sum(cuts)
    low, middle, high = [bounds[CORES * group + k] for k in range(CORES + 1)]
    first_steps = (middle - low + unroll - 1) // unroll
    steps = first_steps + (high - middle + unroll - 1) // unroll

    def begin(i):
        return jnp.where(i < first_steps, low + i * unroll, middle + (i - first_steps) * unroll)

    def fetch(i, vals):
        base = begin(i)
        room = lax.rem(i, depth)
        for u in range(unroll):
            pltpu.make_async_copy(
                vals.at[table[base + u] & 127], ring.at[room, u], ring_sem.at[room]
            ).start()

    def ahead(i):
        @pl.when(i < first_steps)
        def _():
            fetch(i, vals_a)

        @pl.when((i >= first_steps) & (i < steps))
        def _():
            fetch(i, vals_b)

    for i in range(depth - 1):
        ahead(jnp.int32(i))

    @pl.loop(0, blocks)
    def _(i):
        total[pl.ds(i * BLK, BLK), :] = jnp.zeros((BLK, total.shape[1]), jnp.float32)

    for copy in copies:
        copy.wait()
    dims = (((0,), (0,)), ((), ())) if transposed else (((1,), (0,)), ((), ()))

    @pl.loop(0, steps)
    def _(i):
        ahead(i + depth - 1)
        room = lax.rem(i, depth)
        pltpu.make_async_copy(
            vals_a.at[pl.ds(0, unroll)], ring.at[room], ring_sem.at[room]
        ).wait()
        base = begin(i)
        limit = jnp.where(i < first_steps, middle, high)
        for u in range(unroll):
            entry = table[base + u]
            source = lax.shift_right_logical(entry, 7) & 63
            target = jnp.where(base + u < limit, lax.shift_right_logical(entry, 13), blocks)
            taken = held[pl.ds(pl.multiple_of(source * BLK, BLK), BLK), :]
            product = lax.dot_general(
                ring[room, u], taken, dims, preferred_element_type=jnp.float32
            )
            placed = pl.ds(pl.multiple_of(target * BLK, BLK), BLK)
            total[placed, :] = total[placed, :] + product

    at = 0
    for out, size in zip(outs, cuts):
        first = at

        @pl.loop(0, size)
        def _(i):
            rows = pl.ds((first + i) * BLK, BLK)
            out[pl.ds(i * BLK, BLK), :] = total[rows, :].astype(jnp.bfloat16)

        at += size


def kept(value):
    return pltpu.with_memory_space_constraint(value, pltpu.HBM)


def tile_product(table, bounds, vals_a, vals_b, sources, offsets, group, cuts, transposed):
    unroll, depth = UNROLL, 3
    width = sources[0].shape[1]
    blocks = sum(cuts)
    vmem = pl.BlockSpec(memory_space=pltpu.VMEM)
    hbm = pl.BlockSpec(memory_space=pltpu.HBM)
    in_specs = [pl.BlockSpec(memory_space=pltpu.SMEM)] * 2 + [hbm] * 2
    out_shape = [jax.ShapeDtypeStruct((c * BLK, width), jnp.bfloat16) for c in cuts]
    scratch = [
        pltpu.VMEM(((blocks + 1) * BLK, width), jnp.float32),
        pltpu.VMEM((depth, unroll, BLK, BLK), jnp.bfloat16),
        pltpu.SemaphoreType.DMA((depth,)),
    ]
    if offsets:
        rows = max(o + p.shape[0] for o, p in zip(offsets, sources))
        in_specs += [pl.BlockSpec(memory_space=pl.ANY)] * len(sources)
        out_shape.append(jax.ShapeDtypeStruct((rows, width), jnp.bfloat16))
        scratch.append(pltpu.SemaphoreType.DMA((len(sources),)))
    else:
        in_specs += [vmem]
    return pl.pallas_call(
        functools.partial(
            tile_kernel, tuple(offsets), transposed, group, unroll, depth, tuple(cuts)
        ),
        out_shape=out_shape,
        in_specs=in_specs,
        out_specs=[vmem] * len(out_shape),
        scratch_shapes=scratch,
        compiler_params=pltpu.CompilerParams(vmem_limit_bytes=20 * 2**20),
        cost_estimate=pl.CostEstimate(
            flops=2 * BLK * BLK * width * 8 * blocks, bytes_accessed=2**20, transcendentals=0
        ),
        name="tile_product",
    )(table, bounds, *[kept(v) for v in (vals_a, vals_b)], *sources)


def chosen(index, values):
    return sum(jnp.where(index == i, v, 0) for i, v in enumerate(values) if v) + 0 * index


def slot_table(live, source, target, group, groups):
    slots = source.shape[1]
    slot = jnp.arange(slots, dtype=jnp.int32)[None]
    tile = jnp.arange(CORES, dtype=jnp.int32)[:, None]
    key = jnp.where(slot < live[:, None], group * CORES + tile, groups * CORES).reshape(-1)
    entry = (slot + source * 128 + target * 8192).reshape(-1)
    place = jnp.arange(CORES * slots, dtype=jnp.int32)
    before = key[None] < key[:, None]
    before |= (key[None] == key[:, None]) & (place[None] < place[:, None])
    rank = jnp.sum(before.astype(jnp.int32), axis=1)
    seat = jnp.arange(CORES * slots + UNROLL, dtype=jnp.int32)[:, None]
    table = jnp.sum(jnp.where(rank[None] == seat, entry[None], 0), axis=1)
    starts = jnp.arange(groups * CORES + 1, dtype=jnp.int32)[:, None]
    bounds = jnp.sum((key[None] < starts).astype(jnp.int32), axis=1)
    return table, bounds


def tied(*values):
    return lax.optimization_barrier(values)


def gather_plane(unit, first_ahead, first_behind, second_ahead, second_behind):
    half = unit.shape[0] // 2
    last, following = send(unit, first_ahead), send(unit, first_behind)
    last, following = tied(last, following)
    near = [unit, following, last]
    near = jnp.concatenate([v[:half] for v in near] + [v[half:] for v in near], 0)
    behind_near, ahead_near = send(near, second_behind), send(near, second_ahead)
    across = [send(following[:half], first_behind), send(last[half:], first_ahead)]
    across = jnp.concatenate(across, 0)
    behind_across, ahead_across = send(across, second_behind), send(across, second_ahead)
    middle = near.shape[0] // 2
    behind_near, ahead_near = tied(behind_near, ahead_near)
    far = [send(behind_near[:middle], second_behind), send(ahead_near[middle:], second_ahead)]
    far_across = [
        send(behind_across[:half], second_behind),
        send(ahead_across[half:], second_ahead),
    ]
    lines = [[near, across], [behind_near, behind_across], [*far, *far_across]]
    lines += [[ahead_near, ahead_across]]
    pieces, offsets = [], []
    at = 0
    for line in lines:
        for piece in line:
            pieces.append(piece)
            offsets.append(at)
            at += piece.shape[0]
    return pieces, offsets


def widened(*values):
    return functools.reduce(lambda a, b: a + b, [v.astype(jnp.float32) for v in values]).astype(
        jnp.bfloat16
    )


def sum_four(near, free, bound, far, ahead, behind):
    top, bottom = send(far[0], ahead), send(far[1], behind)
    low, high = free()
    low, high = send(low, ahead), send(high, behind)
    one, three = bound()
    top, bottom = tied(top, bottom)
    top, bottom = tied(widened(one, top), widened(three, bottom))
    low, high = tied(low, high)
    near, low, high = near(low, high)
    half = near.shape[0] // 2
    top, bottom = tied(send(top, ahead), send(bottom, behind))
    first = widened(near[:half], top, high)
    second = widened(near[half:], bottom, low)
    return jnp.concatenate([first, second], 0)


def sum_small(value, ahead, behind, beside):
    rows = value.shape[0] // 4
    half = rows // 2
    part = [value[i * rows : (i + 1) * rows] for i in range(4)]
    top, bottom = tied(send(part[2][:half], ahead), send(part[2][half:], behind))
    to_ahead = jnp.concatenate([widened(part[1][:half], top), part[1][half:]], 0)
    to_behind = jnp.concatenate([part[3][:half], widened(part[3][half:], bottom)], 0)
    to_ahead, to_behind = tied(to_ahead, to_behind)
    from_behind, from_ahead = send(to_ahead, ahead), send(to_behind, behind)
    from_behind, from_ahead, *beside = tied(from_behind, from_ahead, *beside)
    return widened(part[0], from_behind, from_ahead), beside


def sum_z(part, far, ahead, behind):
    half = part[0].shape[0] // 2
    top, bottom = tied(send(far[0], ahead), send(far[1], behind))
    to_ahead = jnp.concatenate([widened(part[3][:half], top), part[3][half:]], 0)
    to_behind = jnp.concatenate([part[5][:half], widened(part[5][half:], bottom)], 0)
    for d in (2, 1, 0):
        to_ahead, to_behind = tied(to_ahead, to_behind)
        from_behind, from_ahead = tied(send(to_ahead, ahead), send(to_behind, behind))
        if d:
            to_ahead = widened(part[d], from_behind)
            to_behind = widened(part[NZ - d], from_ahead)
    return widened(part[0], from_behind, from_ahead)


def gather_z(value, grads):
    rows = value.shape[0]
    half = rows // 2
    ahead, behind = along_z(1), along_z(-1)
    pieces, offsets = [value], [0]
    following, last = value, value
    for d in range(1, NZ // 2):
        following, last = send(following, behind), send(last, ahead)
        if d == 2:
            following, last = tied(following, last)
        else:
            following, last, grads = tied(following, last, grads)
        if d == 1:
            grads = lax.all_to_all(grads, "col", 0, 0, tiled=True)
        pieces += [following, last]
        offsets += [d * rows, (NZ - d) * rows]
    grads = summed(grads)
    term = exchange_z(grads, 1)
    lead = [send(following[:half], behind), send(last[half:], ahead)]
    *lead, term = tied(*lead, term)
    pieces += lead
    offsets += [NZ // 2 * rows, NZ // 2 * rows + half]
    return pieces, offsets, widened(grads, term)


def own_rows(halves, core, node_rows, width):
    half = width // 2
    mine = lax.dynamic_slice_in_dim(halves, core * node_rows, node_rows, 0)
    other = swap(lax.dynamic_slice_in_dim(halves, (1 - core) * node_rows, node_rows, 0))
    first = jnp.where(core == 0, mine, other)
    second = jnp.where(core == 0, other, mine)
    return jnp.concatenate([first, second], 1)


def own_half(rows, core, width):
    half = width // 2
    mine = lax.dynamic_slice_in_dim(rows, core * half, half, 1)
    other = swap(lax.dynamic_slice_in_dim(rows, (1 - core) * half, half, 1))
    first = jnp.where(core == 0, mine, other)
    second = jnp.where(core == 0, other, mine)
    return jnp.concatenate([first, second], 0)


def summed(parts):
    return jnp.sum(parts.astype(jnp.float32), axis=0).astype(parts.dtype)


def plane_whole(value):
    spread = jnp.broadcast_to(value[None], (NX * NY, *value.shape))
    return lax.all_to_all(spread, "col", 0, 0, tiled=True)


def per_device(features, w_self, w_neigh, block_vals, block_coords, block_count, cotangent):
    bf16, f32 = jnp.bfloat16, jnp.float32
    node_rows, width = features.shape
    row, col = lax.axis_index("row"), lax.axis_index("col")
    z, core = row // CORES, row % CORES
    y, x = col // NX, col % NX
    near_first, near_second = along_first(1), along_second(1)
    far_first, far_second = along_first(-1), along_second(-1)

    vals = block_vals[0, 0]
    slots = vals.shape[0]
    facts = jnp.concatenate(
        [block_coords[0, 0], jnp.broadcast_to(block_count[0, 0], (1, slots))], 0
    )
    half = width // 2
    note = jnp.zeros((16, half), bf16).at[: facts.shape[0], :slots].set(facts.astype(bf16))
    mine = lax.dynamic_slice_in_dim(features, core * half, half, 1)
    other = lax.dynamic_slice_in_dim(features, (1 - core) * half, half, 1)
    other = swap(jnp.concatenate([other, note], 0))
    other_facts = other[node_rows : node_rows + facts.shape[0], :slots].astype(jnp.int32)
    other = other[:node_rows]
    unit = jnp.concatenate(
        [jnp.where(core == 0, mine, other), jnp.where(core == 0, other, mine)], 0
    )
    later_vals, unit = tied(vals, unit)
    other_vals = swap(later_vals)
    both = jnp.stack([facts, other_facts])
    live = both[:, 2, 0]
    tile_core = jnp.stack([core, 1 - core])[:, None]
    block_row, block_col = both[:, 0], both[:, 1]
    per_dev = node_rows // BLK
    per_chip = CORES * per_dev
    line = NX * per_chip
    z_away = (block_row // per_chip - z) % NZ
    row_in = block_row % per_chip
    owner = block_col // per_dev
    col_in = block_col % per_dev
    dx, dy = (owner % NX - x) % NX, (owner // NX - y) % NY
    first_away, second_away = jnp.where(core == 0, dx, dy), jnp.where(core == 0, dy, dx)
    in_line = jnp.where(
        first_away == 2,
        6 * per_dev + tile_core * per_dev,
        3 * per_dev * tile_core + per_dev * jnp.minimum(first_away, 2),
    )
    forward = slot_table(
        live,
        second_away * line + in_line + col_in,
        chosen(z_away, [2 * per_chip, 0, 0, 0, 0, per_chip, per_chip, per_chip]) + row_in,
        jnp.minimum(jnp.abs(NZ // 2 - z_away), 3),
        4,
    )
    upper = first_away >= NX // 2
    backward = slot_table(
        live,
        z_away * per_chip + row_in,
        (first_away - jnp.where((second_away % 2 == 1) & upper, NX // 2, 0)) * per_chip
        + jnp.where(second_away == 3, line // 2, 0)
        + tile_core * per_dev
        + col_in,
        jnp.where(
            second_away % 2 == 1,
            jnp.where((second_away == 1) == upper, 1, 2),
            chosen(second_away, [3]),
        ),
        4,
    )

    pieces, offsets = gather_plane(unit, near_first, far_first, near_second, far_second)
    half_chip = per_chip // 2
    *far, held = tile_product(
        *forward, vals, other_vals, pieces, offsets, 0, [half_chip] * 2, False
    )
    part = [None] * NZ
    for group, away in enumerate([(3, 5), (2, 6), (1, 7, 0)], 1):
        made = tile_product(
            *forward, vals, other_vals, [held], [], group, [per_chip] * len(away), False
        )
        for d, value in zip(away, made):
            part[d] = value
    neighbours = sum_z(part, far, along_z(1), along_z(-1))
    neighbours = own_rows(neighbours, core, node_rows, width)

    preact = jnp.dot(features, w_self, preferred_element_type=f32)
    preact = preact + jnp.dot(neighbours, w_neigh, preferred_element_type=f32)
    gate = jax.nn.sigmoid(preact)
    layer_out = (preact * gate).astype(bf16)
    slope_grad = (cotangent.astype(f32) * gate * (1.0 + preact * (1.0 - gate))).astype(bf16)
    contract_rows = (((0,), (0,)), ((), ()))
    contract_cols = (((1,), (1,)), ((), ()))
    neigh_grad = lax.dot_general(
        slope_grad, w_neigh, contract_cols, preferred_element_type=f32
    ).astype(bf16)
    grad_unit = own_half(neigh_grad, core, width)

    plane = NX * NY
    grads = [
        lax.dot_general(v, slope_grad, contract_rows, preferred_element_type=f32).astype(bf16)
        for v in (features, neighbours)
    ]
    mine = jnp.where(core == 0, grads[0], grads[1])
    other = swap(jnp.where(core == 0, grads[1], grads[0]))
    grads = widened(mine, other).reshape(plane, width // plane, width)
    pieces, offsets, total = gather_z(grad_unit, grads)
    term = exchange_z(total, 2)

    *far, held = tile_product(
        *backward,
        vals,
        other_vals,
        [kept(p) for p in pieces],
        offsets,
        0,
        [line // 2] * 2,
        True,
    )

    def group_of(index, held, cuts):
        return tile_product(*backward, vals, other_vals, [held], [], index, cuts, True)

    far[0], term = tied(far[0], term)
    total = widened(total, term)
    sums = [total, exchange_z(total, 4)]

    def bound():
        total, term = sums
        one, three, term = tied(*group_of(2, held, [line // 2] * 2), term)
        sums[:] = [plane_whole(widened(total, term))]
        return one, three

    def near(low, high):
        given, low, high = tied(held, low, high)
        return group_of(3, given, [line])[0], low, high

    back = sum_four(
        near,
        lambda: group_of(1, held, [line // 2] * 2),
        bound,
        far,
        near_second,
        far_second,
    )
    back, total = tied(back, sums[0])
    other_total = swap(total)
    sides = [jnp.where(core == 0, total, other_total), jnp.where(core == 0, other_total, total)]
    sides = [v.reshape(width, width).astype(f32) for v in sides]
    back, (grad_self, grad_neigh) = sum_small(back, near_first, far_first, sides)
    back_rows = own_rows(back, core, node_rows, width)
    own_grad = lax.dot_general(slope_grad, w_self, contract_cols, preferred_element_type=f32)
    grad_features = (own_grad + back_rows.astype(f32)).astype(bf16)
    return layer_out, grad_features, grad_self, grad_neigh


def solution(mesh):
    in_specs = (
        P(("row", "col"), None),
        P(),
        P(),
        P("row", "col", None, None, None),
        P("row", "col", None, None),
        P("row", "col"),
        P(("row", "col"), None),
    )
    out_specs = (P(("row", "col"), None), P(("row", "col"), None), P(), P())
    return jax.shard_map(
        per_device, mesh=mesh, in_specs=in_specs, out_specs=out_specs, check_vma=False
    )
```

```python
import functools

import jax
import jax.numpy as jnp
from jax import lax
from jax.experimental import pallas as pl
from jax.experimental.pallas import tpu as pltpu
from jax.sharding import PartitionSpec as P

AXES = ("row", "col")
NX, NY, NZ, CORES = 4, 4, 8, 2
BLK = 128
UNROLL = 16


def place(x, y, z, core):
    return ((z % NZ) * CORES + core) * (NX * NY) + (y % NY) * NX + x % NX


def pairs(move):
    return [
        (place(x, y, z, c), place(*move(x, y, z, c)))
        for z in range(NZ)
        for c in range(CORES)
        for y in range(NY)
        for x in range(NX)
    ]


def along_first(step):
    return pairs(
        lambda x, y, z, c: (x + step, y, z, c) if c == 0 else (x, y + step, z, c)
    )


def along_second(step):
    return pairs(
        lambda x, y, z, c: (x, y + step, z, c) if c == 0 else (x + step, y, z, c)
    )


def along_z(step):
    return pairs(lambda x, y, z, c: (x, y, z + step, c))


def send(value, moved):
    return lax.ppermute(value, AXES, moved)


def exchange_z(value, bit):
    return send(value, pairs(lambda x, y, z, c: (x, y, z ^ bit, c)))


def swap(value):
    return send(value, pairs(lambda x, y, z, c: (x, y, z, 1 - c)))


def tile_kernel(offsets, transposed, group, unroll, depth, cuts, *refs):
    table, bounds, vals_a, vals_b = refs[:4]
    refs = refs[4:]
    pieces, refs = refs[: len(offsets)], refs[len(offsets) :]
    if offsets:
        outs, held = refs[: len(cuts)], refs[len(cuts)]
        total, ring, ring_sem, sem = refs[len(cuts) + 1 :]
    else:
        held, outs = refs[0], refs[1 : len(cuts) + 1]
        total, ring, ring_sem = refs[len(cuts) + 1 :]
    copies = [
        pltpu.make_async_copy(p, held.at[pl.ds(o, p.shape[0])], sem.at[i])
        for i, (p, o) in enumerate(zip(pieces, offsets))
    ]
    for copy in copies:
        copy.start()
    blocks = sum(cuts)
    low, middle, high = [bounds[CORES * group + k] for k in range(CORES + 1)]
    first_steps = (middle - low + unroll - 1) // unroll
    steps = first_steps + (high - middle + unroll - 1) // unroll

    def begin(i):
        return jnp.where(i < first_steps, low + i * unroll, middle + (i - first_steps) * unroll)

    def fetch(i, vals):
        base = begin(i)
        room = lax.rem(i, depth)
        for u in range(unroll):
            pltpu.make_async_copy(
                vals.at[table[base + u] & 127], ring.at[room, u], ring_sem.at[room]
            ).start()

    def ahead(i):
        @pl.when(i < first_steps)
        def _():
            fetch(i, vals_a)

        @pl.when((i >= first_steps) & (i < steps))
        def _():
            fetch(i, vals_b)

    for i in range(depth - 1):
        ahead(jnp.int32(i))

    @pl.loop(0, blocks)
    def _(i):
        total[pl.ds(i * BLK, BLK), :] = jnp.zeros((BLK, total.shape[1]), jnp.float32)

    for copy in copies:
        copy.wait()
    dims = (((0,), (0,)), ((), ())) if transposed else (((1,), (0,)), ((), ()))

    @pl.loop(0, steps)
    def _(i):
        ahead(i + depth - 1)
        room = lax.rem(i, depth)
        pltpu.make_async_copy(
            vals_a.at[pl.ds(0, unroll)], ring.at[room], ring_sem.at[room]
        ).wait()
        base = begin(i)
        limit = jnp.where(i < first_steps, middle, high)
        for u in range(unroll):
            entry = table[base + u]
            source = lax.shift_right_logical(entry, 7) & 63
            target = jnp.where(base + u < limit, lax.shift_right_logical(entry, 13), blocks)
            taken = held[pl.ds(pl.multiple_of(source * BLK, BLK), BLK), :]
            product = lax.dot_general(
                ring[room, u], taken, dims, preferred_element_type=jnp.float32
            )
            placed = pl.ds(pl.multiple_of(target * BLK, BLK), BLK)
            total[placed, :] = total[placed, :] + product

    at = 0
    for out, size in zip(outs, cuts):
        first = at

        @pl.loop(0, size)
        def _(i):
            rows = pl.ds((first + i) * BLK, BLK)
            out[pl.ds(i * BLK, BLK), :] = total[rows, :].astype(jnp.bfloat16)

        at += size


def kept(value):
    return pltpu.with_memory_space_constraint(value, pltpu.HBM)


def tile_product(table, bounds, vals_a, vals_b, sources, offsets, group, cuts, transposed):
    unroll, depth = UNROLL, 3
    width = sources[0].shape[1]
    blocks = sum(cuts)
    vmem = pl.BlockSpec(memory_space=pltpu.VMEM)
    hbm = pl.BlockSpec(memory_space=pltpu.HBM)
    in_specs = [pl.BlockSpec(memory_space=pltpu.SMEM)] * 2 + [hbm] * 2
    out_shape = [jax.ShapeDtypeStruct((c * BLK, width), jnp.bfloat16) for c in cuts]
    scratch = [
        pltpu.VMEM(((blocks + 1) * BLK, width), jnp.float32),
        pltpu.VMEM((depth, unroll, BLK, BLK), jnp.bfloat16),
        pltpu.SemaphoreType.DMA((depth,)),
    ]
    if offsets:
        rows = max(o + p.shape[0] for o, p in zip(offsets, sources))
        in_specs += [pl.BlockSpec(memory_space=pl.ANY)] * len(sources)
        out_shape.append(jax.ShapeDtypeStruct((rows, width), jnp.bfloat16))
        scratch.append(pltpu.SemaphoreType.DMA((len(sources),)))
    else:
        in_specs += [vmem]
    return pl.pallas_call(
        functools.partial(
            tile_kernel, tuple(offsets), transposed, group, unroll, depth, tuple(cuts)
        ),
        out_shape=out_shape,
        in_specs=in_specs,
        out_specs=[vmem] * len(out_shape),
        scratch_shapes=scratch,
        compiler_params=pltpu.CompilerParams(vmem_limit_bytes=20 * 2**20),
        cost_estimate=pl.CostEstimate(
            flops=2 * BLK * BLK * width * 8 * blocks, bytes_accessed=2**20, transcendentals=0
        ),
        name="tile_product",
    )(table, bounds, *[kept(v) for v in (vals_a, vals_b)], *sources)


def chosen(index, values):
    return sum(jnp.where(index == i, v, 0) for i, v in enumerate(values) if v) + 0 * index


def slot_table(live, source, target, group, groups):
    slots = source.shape[1]
    slot = jnp.arange(slots, dtype=jnp.int32)[None]
    tile = jnp.arange(CORES, dtype=jnp.int32)[:, None]
    key = jnp.where(slot < live[:, None], group * CORES + tile, groups * CORES).reshape(-1)
    entry = (slot + source * 128 + target * 8192).reshape(-1)
    place = jnp.arange(CORES * slots, dtype=jnp.int32)
    before = key[None] < key[:, None]
    before |= (key[None] == key[:, None]) & (place[None] < place[:, None])
    rank = jnp.sum(before.astype(jnp.int32), axis=1)
    seat = jnp.arange(CORES * slots + UNROLL, dtype=jnp.int32)[:, None]
    table = jnp.sum(jnp.where(rank[None] == seat, entry[None], 0), axis=1)
    starts = jnp.arange(groups * CORES + 1, dtype=jnp.int32)[:, None]
    bounds = jnp.sum((key[None] < starts).astype(jnp.int32), axis=1)
    return table, bounds


def tied(*values):
    return lax.optimization_barrier(values)


def gather_plane(unit, first_ahead, first_behind, second_ahead, second_behind):
    half = unit.shape[0] // 2
    last, following = send(unit, first_ahead), send(unit, first_behind)
    last, following = tied(last, following)
    near = [unit, following, last]
    near = jnp.concatenate([v[:half] for v in near] + [v[half:] for v in near], 0)
    behind_near, ahead_near = send(near, second_behind), send(near, second_ahead)
    across = [send(following[:half], first_behind), send(last[half:], first_ahead)]
    across = jnp.concatenate(across, 0)
    behind_across, ahead_across = send(across, second_behind), send(across, second_ahead)
    middle = near.shape[0] // 2
    behind_near, ahead_near = tied(behind_near, ahead_near)
    far = [send(behind_near[:middle], second_behind), send(ahead_near[middle:], second_ahead)]
    far_across = [
        send(behind_across[:half], second_behind),
        send(ahead_across[half:], second_ahead),
    ]
    lines = [[near, across], [behind_near, behind_across], [*far, *far_across]]
    lines += [[ahead_near, ahead_across]]
    pieces, offsets = [], []
    at = 0
    for line in lines:
        for piece in line:
            pieces.append(piece)
            offsets.append(at)
            at += piece.shape[0]
    return pieces, offsets


def widened(*values):
    return functools.reduce(lambda a, b: a + b, [v.astype(jnp.float32) for v in values]).astype(
        jnp.bfloat16
    )


def sum_four(near, bound, given, ahead, behind):
    from_behind, from_ahead = send(given[0], ahead), send(given[1], behind)
    one, three = bound()
    from_behind, from_ahead = tied(from_behind, from_ahead)
    half = from_ahead.shape[0] // 2
    top, bottom = tied(
        widened(one, from_behind[:half]), widened(three, from_ahead[:half])
    )
    top, bottom = send(top, ahead), send(bottom, behind)
    near = near()
    first = widened(near[:half], top, from_ahead[half:])
    second = widened(near[half:], bottom, from_behind[half:])
    return jnp.concatenate([first, second], 0)


def sum_small(value, ahead, behind, beside):
    rows = value.shape[0] // 4
    half = rows // 2
    part = [value[i * rows : (i + 1) * rows] for i in range(4)]
    top, bottom = tied(send(part[2][:half], ahead), send(part[2][half:], behind))
    to_ahead = jnp.concatenate([widened(part[1][:half], top), part[1][half:]], 0)
    to_behind = jnp.concatenate([part[3][:half], widened(part[3][half:], bottom)], 0)
    to_ahead, to_behind = tied(to_ahead, to_behind)
    from_behind, from_ahead = send(to_ahead, ahead), send(to_behind, behind)
    from_behind, from_ahead, *beside = tied(from_behind, from_ahead, *beside)
    return widened(part[0], from_behind, from_ahead), beside


def sum_z(part, far, ahead, behind):
    half = part[0].shape[0] // 2
    top, bottom = tied(send(far[0], ahead), send(far[1], behind))
    to_ahead = jnp.concatenate([widened(part[3][:half], top), part[3][half:]], 0)
    to_behind = jnp.concatenate([part[5][:half], widened(part[5][half:], bottom)], 0)
    for d in (2, 1, 0):
        to_ahead, to_behind = tied(to_ahead, to_behind)
        from_behind, from_ahead = tied(send(to_ahead, ahead), send(to_behind, behind))
        if d:
            to_ahead = widened(part[d], from_behind)
            to_behind = widened(part[NZ - d], from_ahead)
    return widened(part[0], from_behind, from_ahead)


def gather_z(value, grads):
    rows = value.shape[0]
    half = rows // 2
    ahead, behind = along_z(1), along_z(-1)
    pieces, offsets = [value], [0]
    following, last = value, value
    for d in range(1, NZ // 2):
        following, last = send(following, behind), send(last, ahead)
        if d == 2:
            following, last = tied(following, last)
        else:
            following, last, grads = tied(following, last, grads)
        if d == 1:
            grads = lax.all_to_all(grads, "col", 0, 0, tiled=True)
        pieces += [following, last]
        offsets += [d * rows, (NZ - d) * rows]
    grads = summed(grads)
    term = exchange_z(grads, 1)
    lead = [send(following[:half], behind), send(last[half:], ahead)]
    *lead, term = tied(*lead, term)
    pieces += lead
    offsets += [NZ // 2 * rows, NZ // 2 * rows + half]
    return pieces, offsets, widened(grads, term)


def own_rows(halves, core, node_rows, width):
    half = width // 2
    mine = lax.dynamic_slice_in_dim(halves, core * node_rows, node_rows, 0)
    other = swap(lax.dynamic_slice_in_dim(halves, (1 - core) * node_rows, node_rows, 0))
    first = jnp.where(core == 0, mine, other)
    second = jnp.where(core == 0, other, mine)
    return jnp.concatenate([first, second], 1)


def own_half(rows, core, width):
    half = width // 2
    mine = lax.dynamic_slice_in_dim(rows, core * half, half, 1)
    other = swap(lax.dynamic_slice_in_dim(rows, (1 - core) * half, half, 1))
    first = jnp.where(core == 0, mine, other)
    second = jnp.where(core == 0, other, mine)
    return jnp.concatenate([first, second], 0)


def summed(parts):
    return jnp.sum(parts.astype(jnp.float32), axis=0).astype(parts.dtype)


def plane_whole(value):
    spread = jnp.broadcast_to(value[None], (NX * NY, *value.shape))
    return lax.all_to_all(spread, "col", 0, 0, tiled=True)


def per_device(features, w_self, w_neigh, block_vals, block_coords, block_count, cotangent):
    bf16, f32 = jnp.bfloat16, jnp.float32
    node_rows, width = features.shape
    row, col = lax.axis_index("row"), lax.axis_index("col")
    z, core = row // CORES, row % CORES
    y, x = col // NX, col % NX
    near_first, near_second = along_first(1), along_second(1)
    far_first, far_second = along_first(-1), along_second(-1)

    vals = block_vals[0, 0]
    slots = vals.shape[0]
    facts = jnp.concatenate(
        [block_coords[0, 0], jnp.broadcast_to(block_count[0, 0], (1, slots))], 0
    )
    half = width // 2
    note = jnp.zeros((16, half), bf16).at[: facts.shape[0], :slots].set(facts.astype(bf16))
    mine = lax.dynamic_slice_in_dim(features, core * half, half, 1)
    other = lax.dynamic_slice_in_dim(features, (1 - core) * half, half, 1)
    other = swap(jnp.concatenate([other, note], 0))
    other_facts = other[node_rows : node_rows + facts.shape[0], :slots].astype(jnp.int32)
    other = other[:node_rows]
    unit = jnp.concatenate(
        [jnp.where(core == 0, mine, other), jnp.where(core == 0, other, mine)], 0
    )
    later_vals, unit = tied(vals, unit)
    other_vals = swap(later_vals)
    both = jnp.stack([facts, other_facts])
    live = both[:, 2, 0]
    tile_core = jnp.stack([core, 1 - core])[:, None]
    block_row, block_col = both[:, 0], both[:, 1]
    per_dev = node_rows // BLK
    per_chip = CORES * per_dev
    line = NX * per_chip
    z_away = (block_row // per_chip - z) % NZ
    row_in = block_row % per_chip
    owner = block_col // per_dev
    col_in = block_col % per_dev
    dx, dy = (owner % NX - x) % NX, (owner // NX - y) % NY
    first_away, second_away = jnp.where(core == 0, dx, dy), jnp.where(core == 0, dy, dx)
    in_line = jnp.where(
        first_away == 2,
        6 * per_dev + tile_core * per_dev,
        3 * per_dev * tile_core + per_dev * jnp.minimum(first_away, 2),
    )
    forward = slot_table(
        live,
        second_away * line + in_line + col_in,
        chosen(z_away, [2 * per_chip, 0, 0, 0, 0, per_chip, per_chip, per_chip]) + row_in,
        jnp.minimum(jnp.abs(NZ // 2 - z_away), 3),
        4,
    )
    upper = first_away >= NX // 2
    backward = slot_table(
        live,
        z_away * per_chip + row_in,
        first_away * per_chip
        + jnp.where((second_away == 2) & upper, line // 2, 0)
        + jnp.where((second_away == 3) & ~upper, line // 2 + line, 0)
        + tile_core * per_dev
        + col_in,
        jnp.where(
            second_away % 2 == 1,
            jnp.where((second_away == 1) == upper, 0, 1),
            chosen(second_away, [2]),
        ),
        3,
    )

    pieces, offsets = gather_plane(unit, near_first, far_first, near_second, far_second)
    half_chip = per_chip // 2
    *far, held = tile_product(
        *forward, vals, other_vals, pieces, offsets, 0, [half_chip] * 2, False
    )
    part = [None] * NZ
    for group, away in enumerate([(3, 5), (2, 6), (1, 7, 0)], 1):
        made = tile_product(
            *forward, vals, other_vals, [held], [], group, [per_chip] * len(away), False
        )
        for d, value in zip(away, made):
            part[d] = value
    neighbours = sum_z(part, far, along_z(1), along_z(-1))
    neighbours = own_rows(neighbours, core, node_rows, width)

    preact = jnp.dot(features, w_self, preferred_element_type=f32)
    preact = preact + jnp.dot(neighbours, w_neigh, preferred_element_type=f32)
    gate = jax.nn.sigmoid(preact)
    layer_out = (preact * gate).astype(bf16)
    slope_grad = (cotangent.astype(f32) * gate * (1.0 + preact * (1.0 - gate))).astype(bf16)
    contract_rows = (((0,), (0,)), ((), ()))
    contract_cols = (((1,), (1,)), ((), ()))
    neigh_grad = lax.dot_general(
        slope_grad, w_neigh, contract_cols, preferred_element_type=f32
    ).astype(bf16)
    grad_unit = own_half(neigh_grad, core, width)

    plane = NX * NY
    grads = [
        lax.dot_general(v, slope_grad, contract_rows, preferred_element_type=f32).astype(bf16)
        for v in (features, neighbours)
    ]
    mine = jnp.where(core == 0, grads[0], grads[1])
    other = swap(jnp.where(core == 0, grads[1], grads[0]))
    grads = widened(mine, other).reshape(plane, width // plane, width)
    pieces, offsets, total = gather_z(grad_unit, grads)
    term = exchange_z(total, 2)

    *given, held = tile_product(
        *backward,
        vals,
        other_vals,
        [kept(p) for p in pieces],
        offsets,
        0,
        [line] * 2,
        True,
    )

    def group_of(index, held, cuts):
        return tile_product(*backward, vals, other_vals, [held], [], index, cuts, True)

    given[0], term = tied(given[0], term)
    total = widened(total, term)
    sums = [total, exchange_z(total, 4)]

    def bound():
        total, term = sums
        one, three, term = tied(*group_of(1, held, [line // 2] * 2), term)
        sums[:] = [plane_whole(widened(total, term))]
        return one, three

    def near():
        last, sums[0] = tied(held, sums[0])
        return group_of(2, last, [line])[0]

    back = sum_four(near, bound, given, near_second, far_second)
    back, total = tied(back, sums[0])
    other_total = swap(total)
    sides = [jnp.where(core == 0, total, other_total), jnp.where(core == 0, other_total, total)]
    sides = [v.reshape(width, width).astype(f32) for v in sides]
    back, (grad_self, grad_neigh) = sum_small(back, near_first, far_first, sides)
    back_rows = own_rows(back, core, node_rows, width)
    own_grad = lax.dot_general(slope_grad, w_self, contract_cols, preferred_element_type=f32)
    grad_features = (own_grad + back_rows.astype(f32)).astype(bf16)
    return layer_out, grad_features, grad_self, grad_neigh


def solution(mesh):
    in_specs = (
        P(("row", "col"), None),
        P(),
        P(),
        P("row", "col", None, None, None),
        P("row", "col", None, None),
        P("row", "col"),
        P(("row", "col"), None),
    )
    out_specs = (P(("row", "col"), None), P(("row", "col"), None), P(), P())
    return jax.shard_map(
        per_device, mesh=mesh, in_specs=in_specs, out_specs=out_specs, check_vma=False
    )
```

```python
import functools

import jax
import jax.numpy as jnp
from jax import lax
from jax.experimental import pallas as pl
from jax.experimental.pallas import tpu as pltpu
from jax.sharding import PartitionSpec as P

AXES = ("row", "col")
NX, NY, NZ, CORES = 4, 4, 8, 2
BLK = 128
UNROLL = 16


def place(x, y, z, core):
    return ((z % NZ) * CORES + core) * (NX * NY) + (y % NY) * NX + x % NX


def pairs(move):
    return [
        (place(x, y, z, c), place(*move(x, y, z, c)))
        for z in range(NZ)
        for c in range(CORES)
        for y in range(NY)
        for x in range(NX)
    ]


def along_first(step):
    return pairs(
        lambda x, y, z, c: (x + step, y, z, c) if c == 0 else (x, y + step, z, c)
    )


def along_second(step):
    return pairs(
        lambda x, y, z, c: (x, y + step, z, c) if c == 0 else (x + step, y, z, c)
    )


def along_z(step):
    return pairs(lambda x, y, z, c: (x, y, z + step, c))


def send(value, moved):
    return lax.ppermute(value, AXES, moved)


def exchange_z(value, bit):
    return send(value, pairs(lambda x, y, z, c: (x, y, z ^ bit, c)))


def swap(value):
    return send(value, pairs(lambda x, y, z, c: (x, y, z, 1 - c)))


def tile_kernel(offsets, transposed, group, unroll, depth, cuts, *refs):
    table, bounds, vals_a, vals_b = refs[:4]
    refs = refs[4:]
    pieces, refs = refs[: len(offsets)], refs[len(offsets) :]
    if offsets:
        outs, held = refs[: len(cuts)], refs[len(cuts)]
        total, ring, ring_sem, sem = refs[len(cuts) + 1 :]
    else:
        held, outs = refs[0], refs[1 : len(cuts) + 1]
        total, ring, ring_sem = refs[len(cuts) + 1 :]
    copies = [
        pltpu.make_async_copy(p, held.at[pl.ds(o, p.shape[0])], sem.at[i])
        for i, (p, o) in enumerate(zip(pieces, offsets))
    ]
    for copy in copies:
        copy.start()
    blocks = sum(cuts)
    low, middle, high = [bounds[CORES * group + k] for k in range(CORES + 1)]
    first_steps = (middle - low + unroll - 1) // unroll
    steps = first_steps + (high - middle + unroll - 1) // unroll

    def begin(i):
        return jnp.where(i < first_steps, low + i * unroll, middle + (i - first_steps) * unroll)

    def fetch(i, vals):
        base = begin(i)
        room = lax.rem(i, depth)
        for u in range(unroll):
            pltpu.make_async_copy(
                vals.at[table[base + u] & 127], ring.at[room, u], ring_sem.at[room]
            ).start()

    def ahead(i):
        @pl.when(i < first_steps)
        def _():
            fetch(i, vals_a)

        @pl.when((i >= first_steps) & (i < steps))
        def _():
            fetch(i, vals_b)

    for i in range(depth - 1):
        ahead(jnp.int32(i))

    @pl.loop(0, blocks)
    def _(i):
        total[pl.ds(i * BLK, BLK), :] = jnp.zeros((BLK, total.shape[1]), jnp.float32)

    for copy in copies:
        copy.wait()
    dims = (((0,), (0,)), ((), ())) if transposed else (((1,), (0,)), ((), ()))

    @pl.loop(0, steps)
    def _(i):
        ahead(i + depth - 1)
        room = lax.rem(i, depth)
        pltpu.make_async_copy(
            vals_a.at[pl.ds(0, unroll)], ring.at[room], ring_sem.at[room]
        ).wait()
        base = begin(i)
        limit = jnp.where(i < first_steps, middle, high)
        for u in range(unroll):
            entry = table[base + u]
            source = lax.shift_right_logical(entry, 7) & 63
            target = jnp.where(base + u < limit, lax.shift_right_logical(entry, 13), blocks)
            taken = held[pl.ds(pl.multiple_of(source * BLK, BLK), BLK), :]
            product = lax.dot_general(
                ring[room, u], taken, dims, preferred_element_type=jnp.float32
            )
            placed = pl.ds(pl.multiple_of(target * BLK, BLK), BLK)
            total[placed, :] = total[placed, :] + product

    at = 0
    for out, size in zip(outs, cuts):
        first = at

        @pl.loop(0, size)
        def _(i):
            rows = pl.ds((first + i) * BLK, BLK)
            out[pl.ds(i * BLK, BLK), :] = total[rows, :].astype(jnp.bfloat16)

        at += size


def kept(value):
    return pltpu.with_memory_space_constraint(value, pltpu.HBM)


def tile_product(table, bounds, vals_a, vals_b, sources, offsets, group, cuts, transposed):
    unroll, depth = UNROLL, 3
    width = sources[0].shape[1]
    blocks = sum(cuts)
    vmem = pl.BlockSpec(memory_space=pltpu.VMEM)
    hbm = pl.BlockSpec(memory_space=pltpu.HBM)
    in_specs = [pl.BlockSpec(memory_space=pltpu.SMEM)] * 2 + [hbm] * 2
    out_shape = [jax.ShapeDtypeStruct((c * BLK, width), jnp.bfloat16) for c in cuts]
    scratch = [
        pltpu.VMEM(((blocks + 1) * BLK, width), jnp.float32),
        pltpu.VMEM((depth, unroll, BLK, BLK), jnp.bfloat16),
        pltpu.SemaphoreType.DMA((depth,)),
    ]
    if offsets:
        rows = max(o + p.shape[0] for o, p in zip(offsets, sources))
        in_specs += [pl.BlockSpec(memory_space=pl.ANY)] * len(sources)
        out_shape.append(jax.ShapeDtypeStruct((rows, width), jnp.bfloat16))
        scratch.append(pltpu.SemaphoreType.DMA((len(sources),)))
    else:
        in_specs += [vmem]
    return pl.pallas_call(
        functools.partial(
            tile_kernel, tuple(offsets), transposed, group, unroll, depth, tuple(cuts)
        ),
        out_shape=out_shape,
        in_specs=in_specs,
        out_specs=[vmem] * len(out_shape),
        scratch_shapes=scratch,
        compiler_params=pltpu.CompilerParams(vmem_limit_bytes=20 * 2**20),
        cost_estimate=pl.CostEstimate(
            flops=2 * BLK * BLK * width * 8 * blocks, bytes_accessed=2**20, transcendentals=0
        ),
        name="tile_product",
    )(table, bounds, *[kept(v) for v in (vals_a, vals_b)], *sources)


def chosen(index, values):
    return sum(jnp.where(index == i, v, 0) for i, v in enumerate(values) if v) + 0 * index


def slot_table(live, source, target, group, groups):
    slots = source.shape[1]
    slot = jnp.arange(slots, dtype=jnp.int32)[None]
    tile = jnp.arange(CORES, dtype=jnp.int32)[:, None]
    key = jnp.where(slot < live[:, None], group * CORES + tile, groups * CORES).reshape(-1)
    entry = (slot + source * 128 + target * 8192).reshape(-1)
    place = jnp.arange(CORES * slots, dtype=jnp.int32)
    before = key[None] < key[:, None]
    before |= (key[None] == key[:, None]) & (place[None] < place[:, None])
    rank = jnp.sum(before.astype(jnp.int32), axis=1)
    seat = jnp.arange(CORES * slots + UNROLL, dtype=jnp.int32)[:, None]
    table = jnp.sum(jnp.where(rank[None] == seat, entry[None], 0), axis=1)
    starts = jnp.arange(groups * CORES + 1, dtype=jnp.int32)[:, None]
    bounds = jnp.sum((key[None] < starts).astype(jnp.int32), axis=1)
    return table, bounds


def tied(*values):
    return lax.optimization_barrier(values)


def gather_plane(unit, first_ahead, first_behind, second_ahead, second_behind):
    half = unit.shape[0] // 2
    last, following = send(unit, first_ahead), send(unit, first_behind)
    last, following = tied(last, following)
    near = [unit, following, last]
    near = jnp.concatenate([v[:half] for v in near] + [v[half:] for v in near], 0)
    behind_near, ahead_near = send(near, second_behind), send(near, second_ahead)
    across = [send(following[:half], first_behind), send(last[half:], first_ahead)]
    across = jnp.concatenate(across, 0)
    behind_across, ahead_across = send(across, second_behind), send(across, second_ahead)
    middle = near.shape[0] // 2
    behind_near, ahead_near = tied(behind_near, ahead_near)
    far = [send(behind_near[:middle], second_behind), send(ahead_near[middle:], second_ahead)]
    far_across = [
        send(behind_across[:half], second_behind),
        send(ahead_across[half:], second_ahead),
    ]
    lines = [[near, across], [behind_near, behind_across], [*far, *far_across]]
    lines += [[ahead_near, ahead_across]]
    pieces, offsets = [], []
    at = 0
    for line in lines:
        for piece in line:
            pieces.append(piece)
            offsets.append(at)
            at += piece.shape[0]
    return pieces, offsets


def widened(*values):
    return functools.reduce(lambda a, b: a + b, [v.astype(jnp.float32) for v in values]).astype(
        jnp.bfloat16
    )


def sum_four(near, free, bound, far, ahead, behind):
    top, bottom = send(far[0], ahead), send(far[1], behind)
    low, high = free()
    low, high = send(low, ahead), send(high, behind)
    one, three = bound()
    top, bottom = tied(top, bottom)
    top, bottom = tied(widened(one, top), widened(three, bottom))
    low, high = tied(low, high)
    near, low, high = near(low, high)
    half = near.shape[0] // 2
    top, bottom = tied(send(top, ahead), send(bottom, behind))
    first = widened(near[:half], top, high)
    second = widened(near[half:], bottom, low)
    return jnp.concatenate([first, second], 0)


def sum_small(value, ahead, behind, beside):
    rows = value.shape[0] // 4
    half = rows // 2
    part = [value[i * rows : (i + 1) * rows] for i in range(4)]
    top, bottom = tied(send(part[2][:half], ahead), send(part[2][half:], behind))
    to_ahead = jnp.concatenate([widened(part[1][:half], top), part[1][half:]], 0)
    to_behind = jnp.concatenate([part[3][:half], widened(part[3][half:], bottom)], 0)
    to_ahead, to_behind = tied(to_ahead, to_behind)
    from_behind, from_ahead = send(to_ahead, ahead), send(to_behind, behind)
    from_behind, from_ahead, *beside = tied(from_behind, from_ahead, *beside)
    return widened(part[0], from_behind, from_ahead), beside


def sum_z(part, far, ahead, behind):
    half = part[0].shape[0] // 2
    top, bottom = tied(send(far[0], ahead), send(far[1], behind))
    to_ahead = jnp.concatenate([widened(part[3][:half], top), part[3][half:]], 0)
    to_behind = jnp.concatenate([part[5][:half], widened(part[5][half:], bottom)], 0)
    for d in (2, 1, 0):
        to_ahead, to_behind = tied(to_ahead, to_behind)
        from_behind, from_ahead = tied(send(to_ahead, ahead), send(to_behind, behind))
        if d:
            to_ahead = widened(part[d], from_behind)
            to_behind = widened(part[NZ - d], from_ahead)
    return widened(part[0], from_behind, from_ahead)


def gather_z(value, grads):
    rows = value.shape[0]
    half = rows // 2
    ahead, behind = along_z(1), along_z(-1)
    pieces, offsets = [value], [0]
    following, last = value, value
    for d in range(1, NZ // 2):
        following, last = send(following, behind), send(last, ahead)
        if d == 2:
            following, last = tied(following, last)
        else:
            following, last, grads = tied(following, last, grads)
        if d == 1:
            grads = lax.all_to_all(grads, "col", 0, 0, tiled=True)
        pieces += [following, last]
        offsets += [d * rows, (NZ - d) * rows]
    grads = summed(grads)
    term = exchange_z(grads, 1)
    lead = [send(following[:half], behind), send(last[half:], ahead)]
    *lead, term = tied(*lead, term)
    pieces += lead
    offsets += [NZ // 2 * rows, NZ // 2 * rows + half]
    return pieces, offsets, widened(grads, term)


def own_rows(halves, core, node_rows, width):
    half = width // 2
    mine = lax.dynamic_slice_in_dim(halves, core * node_rows, node_rows, 0)
    other = swap(lax.dynamic_slice_in_dim(halves, (1 - core) * node_rows, node_rows, 0))
    first = jnp.where(core == 0, mine, other)
    second = jnp.where(core == 0, other, mine)
    return jnp.concatenate([first, second], 1)


def own_half(rows, core, width):
    half = width // 2
    mine = lax.dynamic_slice_in_dim(rows, core * half, half, 1)
    other = swap(lax.dynamic_slice_in_dim(rows, (1 - core) * half, half, 1))
    first = jnp.where(core == 0, mine, other)
    second = jnp.where(core == 0, other, mine)
    return jnp.concatenate([first, second], 0)


def summed(parts):
    return jnp.sum(parts.astype(jnp.float32), axis=0).astype(parts.dtype)


def plane_whole(value):
    spread = jnp.broadcast_to(value[None], (NX * NY, *value.shape))
    return lax.all_to_all(spread, "col", 0, 0, tiled=True)


def per_device(features, w_self, w_neigh, block_vals, block_coords, block_count, cotangent):
    bf16, f32 = jnp.bfloat16, jnp.float32
    node_rows, width = features.shape
    row, col = lax.axis_index("row"), lax.axis_index("col")
    z, core = row // CORES, row % CORES
    y, x = col // NX, col % NX
    near_first, near_second = along_first(1), along_second(1)
    far_first, far_second = along_first(-1), along_second(-1)

    vals = block_vals[0, 0]
    slots = vals.shape[0]
    facts = jnp.concatenate(
        [block_coords[0, 0], jnp.broadcast_to(block_count[0, 0], (1, slots))], 0
    )
    half = width // 2
    note = jnp.zeros((16, half), bf16).at[: facts.shape[0], :slots].set(facts.astype(bf16))
    mine = lax.dynamic_slice_in_dim(features, core * half, half, 1)
    other = lax.dynamic_slice_in_dim(features, (1 - core) * half, half, 1)
    other = swap(jnp.concatenate([other, note], 0))
    other_facts = other[node_rows : node_rows + facts.shape[0], :slots].astype(jnp.int32)
    other = other[:node_rows]
    unit = jnp.concatenate(
        [jnp.where(core == 0, mine, other), jnp.where(core == 0, other, mine)], 0
    )
    later_vals, unit = tied(vals, unit)
    other_vals = swap(later_vals)
    both = jnp.stack([facts, other_facts])
    live = both[:, 2, 0]
    tile_core = jnp.stack([core, 1 - core])[:, None]
    block_row, block_col = both[:, 0], both[:, 1]
    per_dev = node_rows // BLK
    per_chip = CORES * per_dev
    line = NX * per_chip
    z_away = (block_row // per_chip - z) % NZ
    row_in = block_row % per_chip
    owner = block_col // per_dev
    col_in = block_col % per_dev
    dx, dy = (owner % NX - x) % NX, (owner // NX - y) % NY
    first_away, second_away = jnp.where(core == 0, dx, dy), jnp.where(core == 0, dy, dx)
    in_line = jnp.where(
        first_away == 2,
        6 * per_dev + tile_core * per_dev,
        3 * per_dev * tile_core + per_dev * jnp.minimum(first_away, 2),
    )
    forward = slot_table(
        live,
        second_away * line + in_line + col_in,
        chosen(z_away, [2 * per_chip, 0, 0, 0, 0, per_chip, per_chip, per_chip]) + row_in,
        jnp.minimum(jnp.abs(NZ // 2 - z_away), 3),
        4,
    )
    upper = first_away >= NX // 2
    backward = slot_table(
        live,
        z_away * per_chip + row_in,
        (first_away - jnp.where((second_away % 2 == 1) & upper, NX // 2, 0)) * per_chip
        + jnp.where(second_away == 3, line // 2, 0)
        + tile_core * per_dev
        + col_in,
        jnp.where(
            second_away % 2 == 1,
            jnp.where((second_away == 1) == upper, 1, 2),
            chosen(second_away, [3]),
        ),
        4,
    )

    pieces, offsets = gather_plane(unit, near_first, far_first, near_second, far_second)
    half_chip = per_chip // 2
    *far, held = tile_product(
        *forward, vals, other_vals, pieces, offsets, 0, [half_chip] * 2, False
    )
    part = [None] * NZ
    for group, away in enumerate([(3, 5), (2, 6), (1, 7, 0)], 1):
        made = tile_product(
            *forward, vals, other_vals, [held], [], group, [per_chip] * len(away), False
        )
        for d, value in zip(away, made):
            part[d] = value
    neighbours = sum_z(part, far, along_z(1), along_z(-1))
    neighbours = own_rows(neighbours, core, node_rows, width)

    preact = jnp.dot(features, w_self, preferred_element_type=f32)
    preact = preact + jnp.dot(neighbours, w_neigh, preferred_element_type=f32)
    gate = jax.nn.sigmoid(preact)
    layer_out = (preact * gate).astype(bf16)
    slope_grad = (cotangent.astype(f32) * gate * (1.0 + preact * (1.0 - gate))).astype(bf16)
    contract_rows = (((0,), (0,)), ((), ()))
    contract_cols = (((1,), (1,)), ((), ()))
    neigh_grad = lax.dot_general(
        slope_grad, w_neigh, contract_cols, preferred_element_type=f32
    ).astype(bf16)
    grad_unit = own_half(neigh_grad, core, width)

    plane = NX * NY
    grads = [
        lax.dot_general(v, slope_grad, contract_rows, preferred_element_type=f32).astype(bf16)
        for v in (features, neighbours)
    ]
    mine = jnp.where(core == 0, grads[0], grads[1])
    other = swap(jnp.where(core == 0, grads[1], grads[0]))
    grads = widened(mine, other).reshape(plane, width // plane, width)
    pieces, offsets, total = gather_z(grad_unit, grads)
    term = exchange_z(total, 2)

    *far, held = tile_product(
        *backward,
        vals,
        other_vals,
        [kept(p) for p in pieces],
        offsets,
        0,
        [line // 2] * 2,
        True,
    )

    def group_of(index, held, cuts):
        return tile_product(*backward, vals, other_vals, [held], [], index, cuts, True)

    far[0], term = tied(far[0], term)
    total = widened(total, term)
    term = exchange_z(total, 4)

    def near(low, high):
        given, low, high = tied(held, low, high)
        return group_of(3, given, [line])[0], low, high

    back = sum_four(
        near,
        lambda: group_of(1, held, [line // 2] * 2),
        lambda: group_of(2, held, [line // 2] * 2),
        far,
        near_second,
        far_second,
    )
    back, term = tied(back, term)
    total = plane_whole(widened(total, term))
    back, (total,) = sum_small(back, near_first, far_first, [total])
    other_total = swap(total)
    total, other_total = [v.reshape(width, width).astype(f32) for v in (total, other_total)]
    grad_self = jnp.where(core == 0, total, other_total)
    grad_neigh = jnp.where(core == 0, other_total, total)
    back_rows = own_rows(back, core, node_rows, width)
    own_grad = lax.dot_general(slope_grad, w_self, contract_cols, preferred_element_type=f32)
    grad_features = (own_grad + back_rows.astype(f32)).astype(bf16)
    return layer_out, grad_features, grad_self, grad_neigh


def solution(mesh):
    in_specs = (
        P(("row", "col"), None),
        P(),
        P(),
        P("row", "col", None, None, None),
        P("row", "col", None, None),
        P("row", "col"),
        P(("row", "col"), None),
    )
    out_specs = (P(("row", "col"), None), P(("row", "col"), None), P(), P())
    return jax.shard_map(
        per_device, mesh=mesh, in_specs=in_specs, out_specs=out_specs, check_vma=False
    )
```

```python
import functools

import jax
import jax.numpy as jnp
from jax import lax
from jax.experimental import pallas as pl
from jax.experimental.pallas import tpu as pltpu
from jax.sharding import PartitionSpec as P

AXES = ("row", "col")
NX, NY, NZ, CORES = 4, 4, 8, 2
BLK = 128
UNROLL = 16


def place(x, y, z, core):
    return ((z % NZ) * CORES + core) * (NX * NY) + (y % NY) * NX + x % NX


def pairs(move):
    return [
        (place(x, y, z, c), place(*move(x, y, z, c)))
        for z in range(NZ)
        for c in range(CORES)
        for y in range(NY)
        for x in range(NX)
    ]


def along_first(step):
    return pairs(
        lambda x, y, z, c: (x + step, y, z, c) if c == 0 else (x, y + step, z, c)
    )


def along_second(step):
    return pairs(
        lambda x, y, z, c: (x, y + step, z, c) if c == 0 else (x + step, y, z, c)
    )


def along_z(step):
    return pairs(lambda x, y, z, c: (x, y, z + step, c))


def send(value, moved):
    return lax.ppermute(value, AXES, moved)


def exchange_z(value, bit):
    return send(value, pairs(lambda x, y, z, c: (x, y, z ^ bit, c)))


def swap(value):
    return send(value, pairs(lambda x, y, z, c: (x, y, z, 1 - c)))


def tile_kernel(offsets, transposed, group, unroll, depth, cuts, *refs):
    table, bounds, vals_a, vals_b = refs[:4]
    refs = refs[4:]
    pieces, refs = refs[: len(offsets)], refs[len(offsets) :]
    if offsets:
        outs, held = refs[: len(cuts)], refs[len(cuts)]
        total, ring, ring_sem, sem = refs[len(cuts) + 1 :]
    else:
        held, outs = refs[0], refs[1 : len(cuts) + 1]
        total, ring, ring_sem = refs[len(cuts) + 1 :]
    moves = [(p, move) for p, o in zip(pieces, offsets) for move in o]
    copies = [
        pltpu.make_async_copy(p.at[pl.ds(a, n)], held.at[pl.ds(b, n)], sem.at[i])
        for i, (p, (a, b, n)) in enumerate(moves)
    ]
    for copy in copies:
        copy.start()
    blocks = sum(cuts)
    low, middle, high = [bounds[CORES * group + k] for k in range(CORES + 1)]
    first_steps = (middle - low + unroll - 1) // unroll
    steps = first_steps + (high - middle + unroll - 1) // unroll

    def begin(i):
        return jnp.where(i < first_steps, low + i * unroll, middle + (i - first_steps) * unroll)

    def fetch(i, vals):
        base = begin(i)
        room = lax.rem(i, depth)
        for u in range(unroll):
            pltpu.make_async_copy(
                vals.at[table[base + u] & 127], ring.at[room, u], ring_sem.at[room]
            ).start()

    def ahead(i):
        @pl.when(i < first_steps)
        def _():
            fetch(i, vals_a)

        @pl.when((i >= first_steps) & (i < steps))
        def _():
            fetch(i, vals_b)

    for i in range(depth - 1):
        ahead(jnp.int32(i))

    @pl.loop(0, blocks)
    def _(i):
        total[pl.ds(i * BLK, BLK), :] = jnp.zeros((BLK, total.shape[1]), jnp.float32)

    for copy in copies:
        copy.wait()
    dims = (((0,), (0,)), ((), ())) if transposed else (((1,), (0,)), ((), ()))

    @pl.loop(0, steps)
    def _(i):
        ahead(i + depth - 1)
        room = lax.rem(i, depth)
        pltpu.make_async_copy(
            vals_a.at[pl.ds(0, unroll)], ring.at[room], ring_sem.at[room]
        ).wait()
        base = begin(i)
        limit = jnp.where(i < first_steps, middle, high)
        for u in range(unroll):
            entry = table[base + u]
            source = lax.shift_right_logical(entry, 7) & 63
            target = jnp.where(base + u < limit, lax.shift_right_logical(entry, 13), blocks)
            taken = held[pl.ds(pl.multiple_of(source * BLK, BLK), BLK), :]
            product = lax.dot_general(
                ring[room, u], taken, dims, preferred_element_type=jnp.float32
            )
            placed = pl.ds(pl.multiple_of(target * BLK, BLK), BLK)
            total[placed, :] = total[placed, :] + product

    at = 0
    for out, size in zip(outs, cuts):
        first = at

        @pl.loop(0, size)
        def _(i):
            rows = pl.ds((first + i) * BLK, BLK)
            out[pl.ds(i * BLK, BLK), :] = total[rows, :].astype(jnp.bfloat16)

        at += size


def kept(value):
    return pltpu.with_memory_space_constraint(value, pltpu.HBM)


def tile_product(table, bounds, vals_a, vals_b, sources, offsets, group, cuts, transposed):
    unroll, depth = UNROLL, 3
    width = sources[0].shape[1]
    blocks = sum(cuts)
    vmem = pl.BlockSpec(memory_space=pltpu.VMEM)
    hbm = pl.BlockSpec(memory_space=pltpu.HBM)
    in_specs = [pl.BlockSpec(memory_space=pltpu.SMEM)] * 2 + [hbm] * 2
    out_shape = [jax.ShapeDtypeStruct((c * BLK, width), jnp.bfloat16) for c in cuts]
    scratch = [
        pltpu.VMEM(((blocks + 1) * BLK, width), jnp.float32),
        pltpu.VMEM((depth, unroll, BLK, BLK), jnp.bfloat16),
        pltpu.SemaphoreType.DMA((depth,)),
    ]
    if offsets:
        rows = max(b + n for o in offsets for _, b, n in o)
        in_specs += [pl.BlockSpec(memory_space=pl.ANY)] * len(sources)
        out_shape.append(jax.ShapeDtypeStruct((rows, width), jnp.bfloat16))
        scratch.append(pltpu.SemaphoreType.DMA((sum(map(len, offsets)),)))
    else:
        in_specs += [vmem]
    return pl.pallas_call(
        functools.partial(
            tile_kernel, tuple(offsets), transposed, group, unroll, depth, tuple(cuts)
        ),
        out_shape=out_shape,
        in_specs=in_specs,
        out_specs=[vmem] * len(out_shape),
        scratch_shapes=scratch,
        compiler_params=pltpu.CompilerParams(vmem_limit_bytes=20 * 2**20),
        cost_estimate=pl.CostEstimate(
            flops=2 * BLK * BLK * width * 8 * blocks, bytes_accessed=2**20, transcendentals=0
        ),
        name="tile_product",
    )(table, bounds, *[kept(v) for v in (vals_a, vals_b)], *sources)


def chosen(index, values):
    return sum(jnp.where(index == i, v, 0) for i, v in enumerate(values) if v) + 0 * index


def slot_table(live, source, target, group, groups):
    slots = source.shape[1]
    slot = jnp.arange(slots, dtype=jnp.int32)[None]
    tile = jnp.arange(CORES, dtype=jnp.int32)[:, None]
    key = jnp.where(slot < live[:, None], group * CORES + tile, groups * CORES).reshape(-1)
    entry = (slot + source * 128 + target * 8192).reshape(-1)
    place = jnp.arange(CORES * slots, dtype=jnp.int32)
    before = key[None] < key[:, None]
    before |= (key[None] == key[:, None]) & (place[None] < place[:, None])
    rank = jnp.sum(before.astype(jnp.int32), axis=1)
    seat = jnp.arange(CORES * slots + UNROLL, dtype=jnp.int32)[:, None]
    table = jnp.sum(jnp.where(rank[None] == seat, entry[None], 0), axis=1)
    starts = jnp.arange(groups * CORES + 1, dtype=jnp.int32)[:, None]
    bounds = jnp.sum((key[None] < starts).astype(jnp.int32), axis=1)
    return table, bounds


def tied(*values):
    return lax.optimization_barrier(values)


def gather_plane(unit, first_ahead, first_behind, second_ahead, second_behind):
    half = unit.shape[0] // 2
    last, following = send(unit, first_ahead), send(unit, first_behind)
    last, following = tied(last, following)
    near = [unit, following, last]
    near = jnp.concatenate([v[:half] for v in near] + [v[half:] for v in near], 0)
    behind_near, ahead_near = send(near, second_behind), send(near, second_ahead)
    across = [send(following[:half], first_behind), send(last[half:], first_ahead)]
    across = jnp.concatenate(across, 0)
    behind_across, ahead_across = send(across, second_behind), send(across, second_ahead)
    behind_near, ahead_near, behind_across, ahead_across = tied(
        behind_near, ahead_near, behind_across, ahead_across
    )
    middle, line = near.shape[0] // 2, near.shape[0] + across.shape[0]
    far = [
        send(jnp.concatenate([behind_near[:middle], behind_across[:half]], 0), second_behind),
        send(jnp.concatenate([ahead_near[middle:], ahead_across[half:]], 0), second_ahead),
    ]
    pieces, offsets = [], []
    for d, pair in ((0, (near, across)), (1, (behind_near, behind_across)), (3, (ahead_near, ahead_across))):
        pieces += pair
        offsets += [((0, d * line, 2 * middle),), ((0, d * line + 2 * middle, 2 * half),)]
    for k in range(CORES):
        pieces.append(far[k])
        at = 2 * line
        offsets.append(
            ((0, at + k * middle, middle), (middle, at + 2 * middle + k * half, half))
        )
    return pieces, offsets


def widened(*values):
    return functools.reduce(lambda a, b: a + b, [v.astype(jnp.float32) for v in values]).astype(
        jnp.bfloat16
    )


def sum_four(near, free, bound, far, ahead, behind):
    top, bottom = send(far[0], ahead), send(far[1], behind)
    low, high = free()
    low, high = send(low, ahead), send(high, behind)
    one, three = bound()
    top, bottom = tied(top, bottom)
    top, bottom = tied(widened(one, top), widened(three, bottom))
    low, high = tied(low, high)
    near, low, high = near(low, high)
    half = near.shape[0] // 2
    top, bottom = tied(send(top, ahead), send(bottom, behind))
    first = widened(near[:half], top, high)
    second = widened(near[half:], bottom, low)
    return jnp.concatenate([first, second], 0)


def sum_small(value, ahead, behind, beside):
    rows = value.shape[0] // 4
    half = rows // 2
    part = [value[i * rows : (i + 1) * rows] for i in range(4)]
    top, bottom = tied(send(part[2][:half], ahead), send(part[2][half:], behind))
    to_ahead = jnp.concatenate([widened(part[1][:half], top), part[1][half:]], 0)
    to_behind = jnp.concatenate([part[3][:half], widened(part[3][half:], bottom)], 0)
    to_ahead, to_behind = tied(to_ahead, to_behind)
    from_behind, from_ahead = send(to_ahead, ahead), send(to_behind, behind)
    from_behind, from_ahead, *beside = tied(from_behind, from_ahead, *beside)
    return widened(part[0], from_behind, from_ahead), beside


def sum_z(part, far, ahead, behind):
    half = part[0].shape[0] // 2
    top, bottom = tied(send(far[0], ahead), send(far[1], behind))
    to_ahead = jnp.concatenate([widened(part[3][:half], top), part[3][half:]], 0)
    to_behind = jnp.concatenate([part[5][:half], widened(part[5][half:], bottom)], 0)
    for d in (2, 1, 0):
        to_ahead, to_behind = tied(to_ahead, to_behind)
        from_behind, from_ahead = tied(send(to_ahead, ahead), send(to_behind, behind))
        if d:
            to_ahead = widened(part[d], from_behind)
            to_behind = widened(part[NZ - d], from_ahead)
    return widened(part[0], from_behind, from_ahead)


def gather_z(value, grads):
    rows = value.shape[0]
    half = rows // 2
    ahead, behind = along_z(1), along_z(-1)
    pieces, offsets = [value], [0]
    following, last = value, value
    for d in range(1, NZ // 2):
        following, last = send(following, behind), send(last, ahead)
        if d == 2:
            following, last = tied(following, last)
        else:
            following, last, grads = tied(following, last, grads)
        if d == 1:
            grads = lax.all_to_all(grads, "col", 0, 0, tiled=True)
        pieces += [following, last]
        offsets += [d * rows, (NZ - d) * rows]
    grads = summed(grads)
    term = exchange_z(grads, 1)
    lead = [send(following[:half], behind), send(last[half:], ahead)]
    *lead, term = tied(*lead, term)
    pieces += lead
    offsets += [NZ // 2 * rows, NZ // 2 * rows + half]
    offsets = [((0, o, p.shape[0]),) for o, p in zip(offsets, pieces)]
    return pieces, offsets, widened(grads, term)


def own_rows(halves, core, node_rows, width):
    half = width // 2
    mine = lax.dynamic_slice_in_dim(halves, core * node_rows, node_rows, 0)
    other = swap(lax.dynamic_slice_in_dim(halves, (1 - core) * node_rows, node_rows, 0))
    first = jnp.where(core == 0, mine, other)
    second = jnp.where(core == 0, other, mine)
    return jnp.concatenate([first, second], 1)


def own_half(rows, core, width):
    half = width // 2
    mine = lax.dynamic_slice_in_dim(rows, core * half, half, 1)
    other = swap(lax.dynamic_slice_in_dim(rows, (1 - core) * half, half, 1))
    first = jnp.where(core == 0, mine, other)
    second = jnp.where(core == 0, other, mine)
    return jnp.concatenate([first, second], 0)


def summed(parts):
    return jnp.sum(parts.astype(jnp.float32), axis=0).astype(parts.dtype)


def plane_whole(value):
    spread = jnp.broadcast_to(value[None], (NX * NY, *value.shape))
    return lax.all_to_all(spread, "col", 0, 0, tiled=True)


def per_device(features, w_self, w_neigh, block_vals, block_coords, block_count, cotangent):
    bf16, f32 = jnp.bfloat16, jnp.float32
    node_rows, width = features.shape
    row, col = lax.axis_index("row"), lax.axis_index("col")
    z, core = row // CORES, row % CORES
    y, x = col // NX, col % NX
    near_first, near_second = along_first(1), along_second(1)
    far_first, far_second = along_first(-1), along_second(-1)

    vals = block_vals[0, 0]
    slots = vals.shape[0]
    facts = jnp.concatenate(
        [block_coords[0, 0], jnp.broadcast_to(block_count[0, 0], (1, slots))], 0
    )
    half = width // 2
    note = jnp.zeros((16, half), bf16).at[: facts.shape[0], :slots].set(facts.astype(bf16))
    mine = lax.dynamic_slice_in_dim(features, core * half, half, 1)
    other = lax.dynamic_slice_in_dim(features, (1 - core) * half, half, 1)
    other = swap(jnp.concatenate([other, note], 0))
    other_facts = other[node_rows : node_rows + facts.shape[0], :slots].astype(jnp.int32)
    other = other[:node_rows]
    unit = jnp.concatenate(
        [jnp.where(core == 0, mine, other), jnp.where(core == 0, other, mine)], 0
    )
    later_vals, unit = tied(vals, unit)
    other_vals = swap(later_vals)
    both = jnp.stack([facts, other_facts])
    live = both[:, 2, 0]
    tile_core = jnp.stack([core, 1 - core])[:, None]
    block_row, block_col = both[:, 0], both[:, 1]
    per_dev = node_rows // BLK
    per_chip = CORES * per_dev
    line = NX * per_chip
    z_away = (block_row // per_chip - z) % NZ
    row_in = block_row % per_chip
    owner = block_col // per_dev
    col_in = block_col % per_dev
    dx, dy = (owner % NX - x) % NX, (owner // NX - y) % NY
    first_away, second_away = jnp.where(core == 0, dx, dy), jnp.where(core == 0, dy, dx)
    in_line = jnp.where(
        first_away == 2,
        6 * per_dev + tile_core * per_dev,
        3 * per_dev * tile_core + per_dev * jnp.minimum(first_away, 2),
    )
    forward = slot_table(
        live,
        second_away * line + in_line + col_in,
        chosen(z_away, [2 * per_chip, 0, 0, 0, 0, per_chip, per_chip, per_chip]) + row_in,
        jnp.minimum(jnp.abs(NZ // 2 - z_away), 3),
        4,
    )
    upper = first_away >= NX // 2
    backward = slot_table(
        live,
        z_away * per_chip + row_in,
        (first_away - jnp.where((second_away % 2 == 1) & upper, NX // 2, 0)) * per_chip
        + jnp.where(second_away == 3, line // 2, 0)
        + tile_core * per_dev
        + col_in,
        jnp.where(
            second_away % 2 == 1,
            jnp.where((second_away == 1) == upper, 1, 2),
            chosen(second_away, [3]),
        ),
        4,
    )

    pieces, offsets = gather_plane(unit, near_first, far_first, near_second, far_second)
    half_chip = per_chip // 2
    *far, held = tile_product(
        *forward, vals, other_vals, pieces, offsets, 0, [half_chip] * 2, False
    )
    part = [None] * NZ
    for group, away in enumerate([(3, 5), (2, 6), (1, 7, 0)], 1):
        made = tile_product(
            *forward, vals, other_vals, [held], [], group, [per_chip] * len(away), False
        )
        for d, value in zip(away, made):
            part[d] = value
    neighbours = sum_z(part, far, along_z(1), along_z(-1))
    neighbours = own_rows(neighbours, core, node_rows, width)

    preact = jnp.dot(features, w_self, preferred_element_type=f32)
    preact = preact + jnp.dot(neighbours, w_neigh, preferred_element_type=f32)
    gate = jax.nn.sigmoid(preact)
    layer_out = (preact * gate).astype(bf16)
    slope_grad = (cotangent.astype(f32) * gate * (1.0 + preact * (1.0 - gate))).astype(bf16)
    contract_rows = (((0,), (0,)), ((), ()))
    contract_cols = (((1,), (1,)), ((), ()))
    neigh_grad = lax.dot_general(
        slope_grad, w_neigh, contract_cols, preferred_element_type=f32
    ).astype(bf16)
    grad_unit = own_half(neigh_grad, core, width)

    plane = NX * NY
    slope_later, grad_unit = tied(slope_grad, grad_unit)
    grads = [
        lax.dot_general(v, slope_later, contract_rows, preferred_element_type=f32).astype(bf16)
        for v in (features, neighbours)
    ]
    mine = jnp.where(core == 0, grads[0], grads[1])
    other = swap(jnp.where(core == 0, grads[1], grads[0]))
    grads = widened(mine, other).reshape(plane, width // plane, width)
    pieces, offsets, total = gather_z(grad_unit, grads)
    term = exchange_z(total, 2)

    *far, held = tile_product(
        *backward,
        vals,
        other_vals,
        [kept(p) for p in pieces],
        offsets,
        0,
        [line // 2] * 2,
        True,
    )

    def group_of(index, held, cuts):
        return tile_product(*backward, vals, other_vals, [held], [], index, cuts, True)

    far[0], term = tied(far[0], term)
    total = widened(total, term)
    term = exchange_z(total, 4)

    def near(low, high):
        given, low, high = tied(held, low, high)
        return group_of(3, given, [line])[0], low, high

    back = sum_four(
        near,
        lambda: group_of(1, held, [line // 2] * 2),
        lambda: group_of(2, held, [line // 2] * 2),
        far,
        near_second,
        far_second,
    )
    back, term = tied(back, term)
    total = plane_whole(widened(total, term))
    back, (total,) = sum_small(back, near_first, far_first, [total])
    other_total = swap(total)
    total, other_total = [v.reshape(width, width).astype(f32) for v in (total, other_total)]
    grad_self = jnp.where(core == 0, total, other_total)
    grad_neigh = jnp.where(core == 0, other_total, total)
    back_rows = own_rows(back, core, node_rows, width)
    own_grad = lax.dot_general(slope_grad, w_self, contract_cols, preferred_element_type=f32)
    grad_features = (own_grad + back_rows.astype(f32)).astype(bf16)
    return layer_out, grad_features, grad_self, grad_neigh


def solution(mesh):
    in_specs = (
        P(("row", "col"), None),
        P(),
        P(),
        P("row", "col", None, None, None),
        P("row", "col", None, None),
        P("row", "col"),
        P(("row", "col"), None),
    )
    out_specs = (P(("row", "col"), None), P(("row", "col"), None), P(), P())
    return jax.shard_map(
        per_device, mesh=mesh, in_specs=in_specs, out_specs=out_specs, check_vma=False
    )
```

```python
import functools

import jax
import jax.numpy as jnp
from jax import lax
from jax.experimental import pallas as pl
from jax.experimental.pallas import tpu as pltpu
from jax.sharding import PartitionSpec as P

AXES = ("row", "col")
NX, NY, NZ, CORES = 4, 4, 8, 2
BLK = 128
UNROLL = 16


def place(x, y, z, core):
    return ((z % NZ) * CORES + core) * (NX * NY) + (y % NY) * NX + x % NX


def pairs(move):
    return [
        (place(x, y, z, c), place(*move(x, y, z, c)))
        for z in range(NZ)
        for c in range(CORES)
        for y in range(NY)
        for x in range(NX)
    ]


def along_first(step):
    return pairs(
        lambda x, y, z, c: (x + step, y, z, c) if c == 0 else (x, y + step, z, c)
    )


def along_second(step):
    return pairs(
        lambda x, y, z, c: (x, y + step, z, c) if c == 0 else (x + step, y, z, c)
    )


def along_z(step):
    return pairs(lambda x, y, z, c: (x, y, z + step, c))


def send(value, moved):
    return lax.ppermute(value, AXES, moved)


def exchange_z(value, bit):
    return send(value, pairs(lambda x, y, z, c: (x, y, z ^ bit, c)))


def swap(value):
    return send(value, pairs(lambda x, y, z, c: (x, y, z, 1 - c)))


def tile_kernel(offsets, transposed, group, unroll, depth, cuts, *refs):
    table, bounds, vals_a, vals_b = refs[:4]
    refs = refs[4:]
    pieces, refs = refs[: len(offsets)], refs[len(offsets) :]
    if offsets:
        outs, held = refs[: len(cuts)], refs[len(cuts)]
        total, ring, ring_sem, sem = refs[len(cuts) + 1 :]
    else:
        held, outs = refs[0], refs[1 : len(cuts) + 1]
        total, ring, ring_sem = refs[len(cuts) + 1 :]
    copies = [
        pltpu.make_async_copy(p, held.at[pl.ds(o, p.shape[0])], sem.at[i])
        for i, (p, o) in enumerate(zip(pieces, offsets))
    ]
    for copy in copies:
        copy.start()
    blocks = sum(cuts)
    low, middle, high = [bounds[CORES * group + k] for k in range(CORES + 1)]
    first_steps = (middle - low + unroll - 1) // unroll
    steps = first_steps + (high - middle + unroll - 1) // unroll

    def begin(i):
        return jnp.where(i < first_steps, low + i * unroll, middle + (i - first_steps) * unroll)

    def fetch(i, vals):
        base = begin(i)
        room = lax.rem(i, depth)
        for u in range(unroll):
            pltpu.make_async_copy(
                vals.at[table[base + u] & 127], ring.at[room, u], ring_sem.at[room]
            ).start()

    def ahead(i):
        @pl.when(i < first_steps)
        def _():
            fetch(i, vals_a)

        @pl.when((i >= first_steps) & (i < steps))
        def _():
            fetch(i, vals_b)

    for i in range(depth - 1):
        ahead(jnp.int32(i))

    @pl.loop(0, blocks)
    def _(i):
        total[pl.ds(i * BLK, BLK), :] = jnp.zeros((BLK, total.shape[1]), jnp.float32)

    for copy in copies:
        copy.wait()
    dims = (((0,), (0,)), ((), ())) if transposed else (((1,), (0,)), ((), ()))

    @pl.loop(0, steps)
    def _(i):
        ahead(i + depth - 1)
        room = lax.rem(i, depth)
        pltpu.make_async_copy(
            vals_a.at[pl.ds(0, unroll)], ring.at[room], ring_sem.at[room]
        ).wait()
        base = begin(i)
        limit = jnp.where(i < first_steps, middle, high)
        for u in range(unroll):
            entry = table[base + u]
            source = lax.shift_right_logical(entry, 7) & 63
            target = jnp.where(base + u < limit, lax.shift_right_logical(entry, 13), blocks)
            taken = held[pl.ds(pl.multiple_of(source * BLK, BLK), BLK), :]
            product = lax.dot_general(
                ring[room, u], taken, dims, preferred_element_type=jnp.float32
            )
            placed = pl.ds(pl.multiple_of(target * BLK, BLK), BLK)
            total[placed, :] = total[placed, :] + product

    at = 0
    for out, size in zip(outs, cuts):
        first = at

        @pl.loop(0, size)
        def _(i):
            rows = pl.ds((first + i) * BLK, BLK)
            out[pl.ds(i * BLK, BLK), :] = total[rows, :].astype(jnp.bfloat16)

        at += size


def kept(value):
    return pltpu.with_memory_space_constraint(value, pltpu.HBM)


def tile_product(table, bounds, vals_a, vals_b, sources, offsets, group, cuts, transposed):
    unroll, depth = UNROLL, 3
    width = sources[0].shape[1]
    blocks = sum(cuts)
    vmem = pl.BlockSpec(memory_space=pltpu.VMEM)
    hbm = pl.BlockSpec(memory_space=pltpu.HBM)
    in_specs = [pl.BlockSpec(memory_space=pltpu.SMEM)] * 2 + [hbm] * 2
    out_shape = [jax.ShapeDtypeStruct((c * BLK, width), jnp.bfloat16) for c in cuts]
    scratch = [
        pltpu.VMEM(((blocks + 1) * BLK, width), jnp.float32),
        pltpu.VMEM((depth, unroll, BLK, BLK), jnp.bfloat16),
        pltpu.SemaphoreType.DMA((depth,)),
    ]
    if offsets:
        rows = max(o + p.shape[0] for o, p in zip(offsets, sources))
        in_specs += [pl.BlockSpec(memory_space=pl.ANY)] * len(sources)
        out_shape.append(jax.ShapeDtypeStruct((rows, width), jnp.bfloat16))
        scratch.append(pltpu.SemaphoreType.DMA((len(sources),)))
    else:
        in_specs += [vmem]
    return pl.pallas_call(
        functools.partial(
            tile_kernel, tuple(offsets), transposed, group, unroll, depth, tuple(cuts)
        ),
        out_shape=out_shape,
        in_specs=in_specs,
        out_specs=[vmem] * len(out_shape),
        scratch_shapes=scratch,
        compiler_params=pltpu.CompilerParams(vmem_limit_bytes=20 * 2**20),
        cost_estimate=pl.CostEstimate(
            flops=2 * BLK * BLK * width * 8 * blocks, bytes_accessed=2**20, transcendentals=0
        ),
        name="tile_product",
    )(table, bounds, *[kept(v) for v in (vals_a, vals_b)], *sources)


def chosen(index, values):
    return sum(jnp.where(index == i, v, 0) for i, v in enumerate(values) if v) + 0 * index


def slot_table(live, source, target, group, groups):
    slots = source.shape[1]
    slot = jnp.arange(slots, dtype=jnp.int32)[None]
    tile = jnp.arange(CORES, dtype=jnp.int32)[:, None]
    key = jnp.where(slot < live[:, None], group * CORES + tile, groups * CORES).reshape(-1)
    entry = (slot + source * 128 + target * 8192).reshape(-1)
    place = jnp.arange(CORES * slots, dtype=jnp.int32)
    before = key[None] < key[:, None]
    before |= (key[None] == key[:, None]) & (place[None] < place[:, None])
    rank = jnp.sum(before.astype(jnp.int32), axis=1)
    seat = jnp.arange(CORES * slots + UNROLL, dtype=jnp.int32)[:, None]
    table = jnp.sum(jnp.where(rank[None] == seat, entry[None], 0), axis=1)
    starts = jnp.arange(groups * CORES + 1, dtype=jnp.int32)[:, None]
    bounds = jnp.sum((key[None] < starts).astype(jnp.int32), axis=1)
    return table, bounds


def tied(*values):
    return lax.optimization_barrier(values)


def gather_plane(unit, first_ahead, first_behind, first_across, second_ahead, second_behind):
    half = unit.shape[0] // 2
    last, following = send(unit, first_ahead), send(unit, first_behind)
    across = send(unit, first_across)
    last, following = tied(last, following)
    near = [unit, following, last]
    near = jnp.concatenate([v[:half] for v in near] + [v[half:] for v in near], 0)
    behind_near, ahead_near = send(near, second_behind), send(near, second_ahead)
    behind_across, ahead_across = send(across, second_behind), send(across, second_ahead)
    middle = near.shape[0] // 2
    behind_near, ahead_near = tied(behind_near, ahead_near)
    far = [send(behind_near[:middle], second_behind), send(ahead_near[middle:], second_ahead)]
    far_across = [
        send(behind_across[:half], second_behind),
        send(ahead_across[half:], second_ahead),
    ]
    lines = [[near, across], [behind_near, behind_across], [*far, *far_across]]
    lines += [[ahead_near, ahead_across]]
    pieces, offsets = [], []
    at = 0
    for line in lines:
        for piece in line:
            pieces.append(piece)
            offsets.append(at)
            at += piece.shape[0]
    return pieces, offsets


def widened(*values):
    return functools.reduce(lambda a, b: a + b, [v.astype(jnp.float32) for v in values]).astype(
        jnp.bfloat16
    )


def sum_four(near, free, bound, far, ahead, behind):
    top, bottom = send(far[0], ahead), send(far[1], behind)
    low, high = free()
    low, high = send(low, ahead), send(high, behind)
    one, three = bound()
    top, bottom = tied(top, bottom)
    top, bottom = tied(widened(one, top), widened(three, bottom))
    low, high = tied(low, high)
    near, low, high = near(low, high)
    half = near.shape[0] // 2
    top, bottom = tied(send(top, ahead), send(bottom, behind))
    first = widened(near[:half], top, high)
    second = widened(near[half:], bottom, low)
    return jnp.concatenate([first, second], 0)


def sum_small(value, ahead, behind, beside):
    rows = value.shape[0] // 4
    half = rows // 2
    part = [value[i * rows : (i + 1) * rows] for i in range(4)]
    top, bottom = tied(send(part[2][:half], ahead), send(part[2][half:], behind))
    to_ahead = jnp.concatenate([widened(part[1][:half], top), part[1][half:]], 0)
    to_behind = jnp.concatenate([part[3][:half], widened(part[3][half:], bottom)], 0)
    to_ahead, to_behind = tied(to_ahead, to_behind)
    from_behind, from_ahead = send(to_ahead, ahead), send(to_behind, behind)
    from_behind, from_ahead, *beside = tied(from_behind, from_ahead, *beside)
    return widened(part[0], from_behind, from_ahead), beside


def sum_z(part, far, ahead, behind):
    half = part[0].shape[0] // 2
    top, bottom = tied(send(far[0], ahead), send(far[1], behind))
    to_ahead = jnp.concatenate([widened(part[3][:half], top), part[3][half:]], 0)
    to_behind = jnp.concatenate([part[5][:half], widened(part[5][half:], bottom)], 0)
    for d in (2, 1, 0):
        to_ahead, to_behind = tied(to_ahead, to_behind)
        from_behind, from_ahead = tied(send(to_ahead, ahead), send(to_behind, behind))
        if d:
            to_ahead = widened(part[d], from_behind)
            to_behind = widened(part[NZ - d], from_ahead)
    return widened(part[0], from_behind, from_ahead)


def gather_z(value, grads):
    rows = value.shape[0]
    half = rows // 2
    ahead, behind = along_z(1), along_z(-1)
    pieces, offsets = [value], [0]
    following, last = value, value
    for d in range(1, NZ // 2):
        following, last = send(following, behind), send(last, ahead)
        if d == 2:
            following, last = tied(following, last)
        else:
            following, last, grads = tied(following, last, grads)
        if d == 1:
            grads = lax.all_to_all(grads, "col", 0, 0, tiled=True)
        pieces += [following, last]
        offsets += [d * rows, (NZ - d) * rows]
    grads = summed(grads)
    term = exchange_z(grads, 1)
    lead = [send(following[:half], behind), send(last[half:], ahead)]
    *lead, term = tied(*lead, term)
    pieces += lead
    offsets += [NZ // 2 * rows, NZ // 2 * rows + half]
    return pieces, offsets, widened(grads, term)


def own_rows(halves, core, node_rows, width):
    half = width // 2
    mine = lax.dynamic_slice_in_dim(halves, core * node_rows, node_rows, 0)
    other = swap(lax.dynamic_slice_in_dim(halves, (1 - core) * node_rows, node_rows, 0))
    first = jnp.where(core == 0, mine, other)
    second = jnp.where(core == 0, other, mine)
    return jnp.concatenate([first, second], 1)


def own_half(rows, core, width):
    half = width // 2
    mine = lax.dynamic_slice_in_dim(rows, core * half, half, 1)
    other = swap(lax.dynamic_slice_in_dim(rows, (1 - core) * half, half, 1))
    first = jnp.where(core == 0, mine, other)
    second = jnp.where(core == 0, other, mine)
    return jnp.concatenate([first, second], 0)


def summed(parts):
    return jnp.sum(parts.astype(jnp.float32), axis=0).astype(parts.dtype)


def plane_whole(value):
    spread = jnp.broadcast_to(value[None], (NX * NY, *value.shape))
    return lax.all_to_all(spread, "col", 0, 0, tiled=True)


def per_device(features, w_self, w_neigh, block_vals, block_coords, block_count, cotangent):
    bf16, f32 = jnp.bfloat16, jnp.float32
    node_rows, width = features.shape
    row, col = lax.axis_index("row"), lax.axis_index("col")
    z, core = row // CORES, row % CORES
    y, x = col // NX, col % NX
    near_first, near_second = along_first(1), along_second(1)
    far_first, far_second = along_first(-1), along_second(-1)

    vals = block_vals[0, 0]
    slots = vals.shape[0]
    facts = jnp.concatenate(
        [block_coords[0, 0], jnp.broadcast_to(block_count[0, 0], (1, slots))], 0
    )
    half = width // 2
    note = jnp.zeros((16, half), bf16).at[: facts.shape[0], :slots].set(facts.astype(bf16))
    mine = lax.dynamic_slice_in_dim(features, core * half, half, 1)
    other = lax.dynamic_slice_in_dim(features, (1 - core) * half, half, 1)
    other = swap(jnp.concatenate([other, note], 0))
    other_facts = other[node_rows : node_rows + facts.shape[0], :slots].astype(jnp.int32)
    other = other[:node_rows]
    unit = jnp.concatenate(
        [jnp.where(core == 0, mine, other), jnp.where(core == 0, other, mine)], 0
    )
    later_vals, unit = tied(vals, unit)
    other_vals = swap(later_vals)
    both = jnp.stack([facts, other_facts])
    live = both[:, 2, 0]
    tile_core = jnp.stack([core, 1 - core])[:, None]
    block_row, block_col = both[:, 0], both[:, 1]
    per_dev = node_rows // BLK
    per_chip = CORES * per_dev
    line = NX * per_chip
    z_away = (block_row // per_chip - z) % NZ
    row_in = block_row % per_chip
    owner = block_col // per_dev
    col_in = block_col % per_dev
    dx, dy = (owner % NX - x) % NX, (owner // NX - y) % NY
    first_away, second_away = jnp.where(core == 0, dx, dy), jnp.where(core == 0, dy, dx)
    in_line = jnp.where(
        first_away == 2,
        6 * per_dev + tile_core * per_dev,
        3 * per_dev * tile_core + per_dev * jnp.minimum(first_away, 2),
    )
    forward = slot_table(
        live,
        second_away * line + in_line + col_in,
        jnp.where(z_away > NZ // 2, per_chip, 0) + row_in,
        jnp.abs(NZ // 2 - z_away),
        5,
    )
    upper = first_away >= NX // 2
    backward = slot_table(
        live,
        z_away * per_chip + row_in,
        (first_away - jnp.where((second_away % 2 == 1) & upper, NX // 2, 0)) * per_chip
        + jnp.where(second_away == 3, line // 2, 0)
        + tile_core * per_dev
        + col_in,
        jnp.where(
            second_away % 2 == 1,
            jnp.where((second_away == 1) == upper, 1, 2),
            chosen(second_away, [3]),
        ),
        4,
    )

    pieces, offsets = gather_plane(
        unit, near_first, far_first, along_first(2), near_second, far_second
    )
    half_chip = per_chip // 2
    *far, held = tile_product(
        *forward, vals, other_vals, pieces, offsets, 0, [half_chip] * 2, False
    )
    part = [None] * NZ
    for group, away in enumerate([(3, 5), (2, 6), (1, 7), (0,)], 1):
        made = tile_product(
            *forward, vals, other_vals, [held], [], group, [per_chip] * len(away), False
        )
        for d, value in zip(away, made):
            part[d] = value
    neighbours = sum_z(part, far, along_z(1), along_z(-1))
    neighbours = own_rows(neighbours, core, node_rows, width)

    preact = jnp.dot(features, w_self, preferred_element_type=f32)
    preact = preact + jnp.dot(neighbours, w_neigh, preferred_element_type=f32)
    gate = jax.nn.sigmoid(preact)
    layer_out = (preact * gate).astype(bf16)
    slope_grad = (cotangent.astype(f32) * gate * (1.0 + preact * (1.0 - gate))).astype(bf16)
    contract_rows = (((0,), (0,)), ((), ()))
    contract_cols = (((1,), (1,)), ((), ()))
    neigh_grad = lax.dot_general(
        slope_grad, w_neigh, contract_cols, preferred_element_type=f32
    ).astype(bf16)
    grad_unit = own_half(neigh_grad, core, width)

    plane = NX * NY
    slope_later, grad_unit = tied(slope_grad, grad_unit)
    grads = [
        lax.dot_general(v, slope_later, contract_rows, preferred_element_type=f32).astype(bf16)
        for v in (features, neighbours)
    ]
    mine = jnp.where(core == 0, grads[0], grads[1])
    other = swap(jnp.where(core == 0, grads[1], grads[0]))
    grads = widened(mine, other).reshape(plane, width // plane, width)
    pieces, offsets, total = gather_z(grad_unit, grads)
    term = exchange_z(total, 2)

    *far, held = tile_product(
        *backward,
        vals,
        other_vals,
        [kept(p) for p in pieces],
        offsets,
        0,
        [line // 2] * 2,
        True,
    )

    def group_of(index, held, cuts):
        return tile_product(*backward, vals, other_vals, [held], [], index, cuts, True)

    far[0], term = tied(far[0], term)
    total = widened(total, term)
    term = exchange_z(total, 4)

    def near(low, high):
        given, low, high = tied(held, low, high)
        return group_of(3, given, [line])[0], low, high

    back = sum_four(
        near,
        lambda: group_of(1, held, [line // 2] * 2),
        lambda: group_of(2, held, [line // 2] * 2),
        far,
        near_second,
        far_second,
    )
    back, term = tied(back, term)
    total = plane_whole(widened(total, term))
    back, (total,) = sum_small(back, near_first, far_first, [total])
    other_total = swap(total)
    total, other_total = [v.reshape(width, width).astype(f32) for v in (total, other_total)]
    grad_self = jnp.where(core == 0, total, other_total)
    grad_neigh = jnp.where(core == 0, other_total, total)
    back_rows = own_rows(back, core, node_rows, width)
    own_grad = lax.dot_general(slope_grad, w_self, contract_cols, preferred_element_type=f32)
    grad_features = (own_grad + back_rows.astype(f32)).astype(bf16)
    return layer_out, grad_features, grad_self, grad_neigh


def solution(mesh):
    in_specs = (
        P(("row", "col"), None),
        P(),
        P(),
        P("row", "col", None, None, None),
        P("row", "col", None, None),
        P("row", "col"),
        P(("row", "col"), None),
    )
    out_specs = (P(("row", "col"), None), P(("row", "col"), None), P(), P())
    return jax.shard_map(
        per_device, mesh=mesh, in_specs=in_specs, out_specs=out_specs, check_vma=False
    )
```

```python
import functools

import jax
import jax.numpy as jnp
from jax import lax
from jax.experimental import pallas as pl
from jax.experimental.pallas import tpu as pltpu
from jax.sharding import PartitionSpec as P

AXES = ("row", "col")
NX, NY, NZ, CORES = 4, 4, 8, 2
BLK = 128
UNROLL = 16


def place(x, y, z, core):
    return ((z % NZ) * CORES + core) * (NX * NY) + (y % NY) * NX + x % NX


def pairs(move):
    return [
        (place(x, y, z, c), place(*move(x, y, z, c)))
        for z in range(NZ)
        for c in range(CORES)
        for y in range(NY)
        for x in range(NX)
    ]


def along_first(step):
    return pairs(
        lambda x, y, z, c: (x + step, y, z, c) if c == 0 else (x, y + step, z, c)
    )


def along_second(step):
    return pairs(
        lambda x, y, z, c: (x, y + step, z, c) if c == 0 else (x + step, y, z, c)
    )


def along_z(step):
    return pairs(lambda x, y, z, c: (x, y, z + step, c))


def send(value, moved):
    return lax.ppermute(value, AXES, moved)


def exchange_z(value, bit):
    return send(value, pairs(lambda x, y, z, c: (x, y, z ^ bit, c)))


def swap(value):
    return send(value, pairs(lambda x, y, z, c: (x, y, z, 1 - c)))


def tile_kernel(offsets, transposed, group, unroll, depth, cuts, *refs):
    table, bounds, vals_a, vals_b = refs[:4]
    refs = refs[4:]
    pieces, refs = refs[: len(offsets)], refs[len(offsets) :]
    if offsets:
        outs, held = refs[: len(cuts)], refs[len(cuts)]
        total, ring, ring_sem, sem = refs[len(cuts) + 1 :]
    else:
        held, outs = refs[0], refs[1 : len(cuts) + 1]
        total, ring, ring_sem = refs[len(cuts) + 1 :]
    moves = [(p, move) for p, o in zip(pieces, offsets) for move in o]
    copies = [
        pltpu.make_async_copy(p.at[pl.ds(a, n)], held.at[pl.ds(b, n)], sem.at[i])
        for i, (p, (a, b, n)) in enumerate(moves)
    ]
    for copy in copies:
        copy.start()
    blocks = sum(cuts)
    low, middle, high = [bounds[CORES * group + k] for k in range(CORES + 1)]
    first_steps = (middle - low + unroll - 1) // unroll
    steps = first_steps + (high - middle + unroll - 1) // unroll

    def begin(i):
        return jnp.where(i < first_steps, low + i * unroll, middle + (i - first_steps) * unroll)

    def fetch(i, vals):
        base = begin(i)
        room = lax.rem(i, depth)
        for u in range(unroll):
            pltpu.make_async_copy(
                vals.at[table[base + u] & 127], ring.at[room, u], ring_sem.at[room]
            ).start()

    def ahead(i):
        @pl.when(i < first_steps)
        def _():
            fetch(i, vals_a)

        @pl.when((i >= first_steps) & (i < steps))
        def _():
            fetch(i, vals_b)

    for i in range(depth - 1):
        ahead(jnp.int32(i))

    @pl.loop(0, blocks)
    def _(i):
        total[pl.ds(i * BLK, BLK), :] = jnp.zeros((BLK, total.shape[1]), jnp.float32)

    for copy in copies:
        copy.wait()
    dims = (((0,), (0,)), ((), ())) if transposed else (((1,), (0,)), ((), ()))

    @pl.loop(0, steps)
    def _(i):
        ahead(i + depth - 1)
        room = lax.rem(i, depth)
        pltpu.make_async_copy(
            vals_a.at[pl.ds(0, unroll)], ring.at[room], ring_sem.at[room]
        ).wait()
        base = begin(i)
        limit = jnp.where(i < first_steps, middle, high)
        for u in range(unroll):
            entry = table[base + u]
            source = lax.shift_right_logical(entry, 7) & 63
            target = jnp.where(base + u < limit, lax.shift_right_logical(entry, 13), blocks)
            taken = held[pl.ds(pl.multiple_of(source * BLK, BLK), BLK), :]
            product = lax.dot_general(
                ring[room, u], taken, dims, preferred_element_type=jnp.float32
            )
            placed = pl.ds(pl.multiple_of(target * BLK, BLK), BLK)
            total[placed, :] = total[placed, :] + product

    at = 0
    for out, size in zip(outs, cuts):
        first = at

        @pl.loop(0, size)
        def _(i):
            rows = pl.ds((first + i) * BLK, BLK)
            out[pl.ds(i * BLK, BLK), :] = total[rows, :].astype(jnp.bfloat16)

        at += size


def kept(value):
    return pltpu.with_memory_space_constraint(value, pltpu.HBM)


def tile_product(table, bounds, vals_a, vals_b, sources, offsets, group, cuts, transposed):
    unroll, depth = UNROLL, 3
    width = sources[0].shape[1]
    blocks = sum(cuts)
    vmem = pl.BlockSpec(memory_space=pltpu.VMEM)
    hbm = pl.BlockSpec(memory_space=pltpu.HBM)
    in_specs = [pl.BlockSpec(memory_space=pltpu.SMEM)] * 2 + [hbm] * 2
    out_shape = [jax.ShapeDtypeStruct((c * BLK, width), jnp.bfloat16) for c in cuts]
    scratch = [
        pltpu.VMEM(((blocks + 1) * BLK, width), jnp.float32),
        pltpu.VMEM((depth, unroll, BLK, BLK), jnp.bfloat16),
        pltpu.SemaphoreType.DMA((depth,)),
    ]
    if offsets:
        rows = max(b + n for o in offsets for _, b, n in o)
        in_specs += [pl.BlockSpec(memory_space=pl.ANY)] * len(sources)
        out_shape.append(jax.ShapeDtypeStruct((rows, width), jnp.bfloat16))
        scratch.append(pltpu.SemaphoreType.DMA((sum(map(len, offsets)),)))
    else:
        in_specs += [vmem]
    return pl.pallas_call(
        functools.partial(
            tile_kernel, tuple(offsets), transposed, group, unroll, depth, tuple(cuts)
        ),
        out_shape=out_shape,
        in_specs=in_specs,
        out_specs=[vmem] * len(out_shape),
        scratch_shapes=scratch,
        compiler_params=pltpu.CompilerParams(vmem_limit_bytes=20 * 2**20),
        cost_estimate=pl.CostEstimate(
            flops=2 * BLK * BLK * width * 8 * blocks, bytes_accessed=2**20, transcendentals=0
        ),
        name="tile_product",
    )(table, bounds, *[kept(v) for v in (vals_a, vals_b)], *sources)


def chosen(index, values):
    return sum(jnp.where(index == i, v, 0) for i, v in enumerate(values) if v) + 0 * index


def slot_table(live, source, target, group, groups):
    slots = source.shape[1]
    slot = jnp.arange(slots, dtype=jnp.int32)[None]
    tile = jnp.arange(CORES, dtype=jnp.int32)[:, None]
    key = jnp.where(slot < live[:, None], group * CORES + tile, groups * CORES).reshape(-1)
    entry = (slot + source * 128 + target * 8192).reshape(-1)
    place = jnp.arange(CORES * slots, dtype=jnp.int32)
    before = key[None] < key[:, None]
    before |= (key[None] == key[:, None]) & (place[None] < place[:, None])
    rank = jnp.sum(before.astype(jnp.int32), axis=1)
    seat = jnp.arange(CORES * slots + UNROLL, dtype=jnp.int32)[:, None]
    table = jnp.sum(jnp.where(rank[None] == seat, entry[None], 0), axis=1)
    starts = jnp.arange(groups * CORES + 1, dtype=jnp.int32)[:, None]
    bounds = jnp.sum((key[None] < starts).astype(jnp.int32), axis=1)
    return table, bounds


def tied(*values):
    return lax.optimization_barrier(values)


def gather_plane(unit, first_ahead, first_behind, first_across, second_ahead, second_behind):
    rows = unit.shape[0]
    last, following = send(unit, first_ahead), send(unit, first_behind)
    across = send(unit, first_across)
    last, following = tied(last, following)
    near = jnp.concatenate([unit, following, last], 0)
    behind_near, ahead_near = send(near, second_behind), send(near, second_ahead)
    behind_across, ahead_across = send(across, second_behind), send(across, second_ahead)
    behind_near, ahead_near, behind_across, ahead_across = tied(
        behind_near, ahead_near, behind_across, ahead_across
    )
    middle, half, line = 3 * rows // 2, rows // 2, 4 * rows
    far = [
        send(jnp.concatenate([behind_near[:middle], behind_across[:half]], 0), second_behind),
        send(jnp.concatenate([ahead_near[middle:], ahead_across[half:]], 0), second_ahead),
    ]
    pieces, offsets = [], []
    whole = [(0, near, across), (1, behind_near, behind_across), (3, ahead_near, ahead_across)]
    for d, most, rest in whole:
        pieces += [most, rest]
        offsets += [((0, d * line, 2 * middle),), ((0, d * line + 2 * middle, rows),)]
    for k in range(2):
        at = 2 * line
        pieces.append(far[k])
        offsets.append(
            ((0, at + k * middle, middle), (middle, at + 2 * middle + k * half, half))
        )
    return pieces, offsets


def widened(*values):
    return functools.reduce(lambda a, b: a + b, [v.astype(jnp.float32) for v in values]).astype(
        jnp.bfloat16
    )


def sum_four(near, free, bound, far, ahead, behind):
    top, bottom = send(far[0], ahead), send(far[1], behind)
    low, high = free()
    low, high = send(low, ahead), send(high, behind)
    one, three = bound()
    top, bottom = tied(top, bottom)
    top, bottom = tied(widened(one, top), widened(three, bottom))
    low, high = tied(low, high)
    near, low, high = near(low, high)
    half = near.shape[0] // 2
    top, bottom = tied(send(top, ahead), send(bottom, behind))
    first = widened(near[:half], top, high)
    second = widened(near[half:], bottom, low)
    return jnp.concatenate([first, second], 0)


def sum_small(value, ahead, behind, beside):
    rows = value.shape[0] // 4
    half = rows // 2
    part = [value[i * rows : (i + 1) * rows] for i in range(4)]
    top, bottom = tied(send(part[2][:half], ahead), send(part[2][half:], behind))
    to_ahead = jnp.concatenate([widened(part[1][:half], top), part[1][half:]], 0)
    to_behind = jnp.concatenate([part[3][:half], widened(part[3][half:], bottom)], 0)
    to_ahead, to_behind = tied(to_ahead, to_behind)
    from_behind, from_ahead = send(to_ahead, ahead), send(to_behind, behind)
    from_behind, from_ahead, *beside = tied(from_behind, from_ahead, *beside)
    return widened(part[0], from_behind, from_ahead), beside


def sum_z(part, far, ahead, behind):
    half = part[0].shape[0] // 2
    top, bottom = tied(send(far[0], ahead), send(far[1], behind))
    to_ahead = jnp.concatenate([widened(part[3][:half], top), part[3][half:]], 0)
    to_behind = jnp.concatenate([part[5][:half], widened(part[5][half:], bottom)], 0)
    for d in (2, 1, 0):
        to_ahead, to_behind = tied(to_ahead, to_behind)
        from_behind, from_ahead = tied(send(to_ahead, ahead), send(to_behind, behind))
        if d:
            to_ahead = widened(part[d], from_behind)
            to_behind = widened(part[NZ - d], from_ahead)
    return widened(part[0], from_behind, from_ahead)


def gather_z(value, grads):
    rows = value.shape[0]
    half = rows // 2
    ahead, behind = along_z(1), along_z(-1)
    pieces, offsets = [value], [0]
    following, last = value, value
    for d in range(1, NZ // 2):
        following, last = send(following, behind), send(last, ahead)
        if d == 2:
            following, last = tied(following, last)
        else:
            following, last, grads = tied(following, last, grads)
        if d == 1:
            grads = lax.all_to_all(grads, "col", 0, 0, tiled=True)
        pieces += [following, last]
        offsets += [d * rows, (NZ - d) * rows]
    grads = summed(grads)
    term = exchange_z(grads, 1)
    lead = [send(following[:half], behind), send(last[half:], ahead)]
    *lead, term = tied(*lead, term)
    pieces += lead
    offsets += [NZ // 2 * rows, NZ // 2 * rows + half]
    offsets = [((0, o, p.shape[0]),) for o, p in zip(offsets, pieces)]
    return pieces, offsets, widened(grads, term)


def own_rows(halves, core, node_rows, width):
    half = width // 2
    mine = lax.dynamic_slice_in_dim(halves, core * node_rows, node_rows, 0)
    other = swap(lax.dynamic_slice_in_dim(halves, (1 - core) * node_rows, node_rows, 0))
    first = jnp.where(core == 0, mine, other)
    second = jnp.where(core == 0, other, mine)
    return jnp.concatenate([first, second], 1)


def own_half(rows, core, width):
    half = width // 2
    mine = lax.dynamic_slice_in_dim(rows, core * half, half, 1)
    other = swap(lax.dynamic_slice_in_dim(rows, (1 - core) * half, half, 1))
    first = jnp.where(core == 0, mine, other)
    second = jnp.where(core == 0, other, mine)
    return jnp.concatenate([first, second], 0)


def summed(parts):
    return jnp.sum(parts.astype(jnp.float32), axis=0).astype(parts.dtype)


def plane_whole(value):
    spread = jnp.broadcast_to(value[None], (NX * NY, *value.shape))
    return lax.all_to_all(spread, "col", 0, 0, tiled=True)


def per_device(features, w_self, w_neigh, block_vals, block_coords, block_count, cotangent):
    bf16, f32 = jnp.bfloat16, jnp.float32
    node_rows, width = features.shape
    row, col = lax.axis_index("row"), lax.axis_index("col")
    z, core = row // CORES, row % CORES
    y, x = col // NX, col % NX
    near_first, near_second = along_first(1), along_second(1)
    far_first, far_second = along_first(-1), along_second(-1)

    vals = block_vals[0, 0]
    slots = vals.shape[0]
    facts = jnp.concatenate(
        [block_coords[0, 0], jnp.broadcast_to(block_count[0, 0], (1, slots))], 0
    )
    half = width // 2
    note = jnp.zeros((16, half), bf16).at[: facts.shape[0], :slots].set(facts.astype(bf16))
    mine = lax.dynamic_slice_in_dim(features, core * half, half, 1)
    other = lax.dynamic_slice_in_dim(features, (1 - core) * half, half, 1)
    other = swap(jnp.concatenate([other, note], 0))
    other_facts = other[node_rows : node_rows + facts.shape[0], :slots].astype(jnp.int32)
    other = other[:node_rows]
    unit = jnp.concatenate(
        [jnp.where(core == 0, mine, other), jnp.where(core == 0, other, mine)], 0
    )
    later_vals, unit = tied(vals, unit)
    other_vals = swap(later_vals)
    both = jnp.stack([facts, other_facts])
    live = both[:, 2, 0]
    tile_core = jnp.stack([core, 1 - core])[:, None]
    block_row, block_col = both[:, 0], both[:, 1]
    per_dev = node_rows // BLK
    per_chip = CORES * per_dev
    line = NX * per_chip
    z_away = (block_row // per_chip - z) % NZ
    row_in = block_row % per_chip
    owner = block_col // per_dev
    col_in = block_col % per_dev
    dx, dy = (owner % NX - x) % NX, (owner // NX - y) % NY
    first_away, second_away = jnp.where(core == 0, dx, dy), jnp.where(core == 0, dy, dx)
    in_line = chosen(first_away, [0, per_chip, 3 * per_chip, 2 * per_chip]) + tile_core * per_dev
    forward = slot_table(
        live,
        second_away * line + in_line + col_in,
        jnp.where(z_away > NZ // 2, per_chip, 0) + row_in,
        jnp.abs(NZ // 2 - z_away),
        5,
    )
    upper = first_away >= NX // 2
    backward = slot_table(
        live,
        z_away * per_chip + row_in,
        (first_away - jnp.where((second_away % 2 == 1) & upper, NX // 2, 0)) * per_chip
        + jnp.where(second_away == 3, line // 2, 0)
        + tile_core * per_dev
        + col_in,
        jnp.where(
            second_away % 2 == 1,
            jnp.where((second_away == 1) == upper, 1, 2),
            chosen(second_away, [3]),
        ),
        4,
    )

    pieces, offsets = gather_plane(
        unit, near_first, far_first, along_first(2), near_second, far_second
    )
    half_chip = per_chip // 2
    *far, held = tile_product(
        *forward, vals, other_vals, pieces, offsets, 0, [half_chip] * 2, False
    )
    part = [None] * NZ
    for group, away in enumerate([(3, 5), (2, 6), (1, 7), (0,)], 1):
        made = tile_product(
            *forward, vals, other_vals, [held], [], group, [per_chip] * len(away), False
        )
        for d, value in zip(away, made):
            part[d] = value
    neighbours = sum_z(part, far, along_z(1), along_z(-1))
    neighbours = own_rows(neighbours, core, node_rows, width)

    preact = jnp.dot(features, w_self, preferred_element_type=f32)
    preact = preact + jnp.dot(neighbours, w_neigh, preferred_element_type=f32)
    gate = jax.nn.sigmoid(preact)
    layer_out = (preact * gate).astype(bf16)
    slope_grad = (cotangent.astype(f32) * gate * (1.0 + preact * (1.0 - gate))).astype(bf16)
    contract_rows = (((0,), (0,)), ((), ()))
    contract_cols = (((1,), (1,)), ((), ()))
    neigh_grad = lax.dot_general(
        slope_grad, w_neigh, contract_cols, preferred_element_type=f32
    ).astype(bf16)
    grad_unit = own_half(neigh_grad, core, width)

    plane = NX * NY
    slope_later, grad_unit = tied(slope_grad, grad_unit)
    grads = [
        lax.dot_general(v, slope_later, contract_rows, preferred_element_type=f32).astype(bf16)
        for v in (features, neighbours)
    ]
    mine = jnp.where(core == 0, grads[0], grads[1])
    other = swap(jnp.where(core == 0, grads[1], grads[0]))
    grads = widened(mine, other).reshape(plane, width // plane, width)
    pieces, offsets, total = gather_z(grad_unit, grads)
    term = exchange_z(total, 2)

    *far, held = tile_product(
        *backward,
        vals,
        other_vals,
        [kept(p) for p in pieces],
        offsets,
        0,
        [line // 2] * 2,
        True,
    )

    def group_of(index, held, cuts):
        return tile_product(*backward, vals, other_vals, [held], [], index, cuts, True)

    far[0], term = tied(far[0], term)
    total = widened(total, term)
    term = exchange_z(total, 4)

    def near(low, high):
        given, low, high = tied(held, low, high)
        return group_of(3, given, [line])[0], low, high

    back = sum_four(
        near,
        lambda: group_of(1, held, [line // 2] * 2),
        lambda: group_of(2, held, [line // 2] * 2),
        far,
        near_second,
        far_second,
    )
    back, term = tied(back, term)
    total = plane_whole(widened(total, term))
    back, (total,) = sum_small(back, near_first, far_first, [total])
    other_total = swap(total)
    total, other_total = [v.reshape(width, width).astype(f32) for v in (total, other_total)]
    grad_self = jnp.where(core == 0, total, other_total)
    grad_neigh = jnp.where(core == 0, other_total, total)
    back_rows = own_rows(back, core, node_rows, width)
    own_grad = lax.dot_general(slope_grad, w_self, contract_cols, preferred_element_type=f32)
    grad_features = (own_grad + back_rows.astype(f32)).astype(bf16)
    return layer_out, grad_features, grad_self, grad_neigh


def solution(mesh):
    in_specs = (
        P(("row", "col"), None),
        P(),
        P(),
        P("row", "col", None, None, None),
        P("row", "col", None, None),
        P("row", "col"),
        P(("row", "col"), None),
    )
    out_specs = (P(("row", "col"), None), P(("row", "col"), None), P(), P())
    return jax.shard_map(
        per_device, mesh=mesh, in_specs=in_specs, out_specs=out_specs, check_vma=False
    )
```

```python
import functools

import jax
import jax.numpy as jnp
from jax import lax
from jax.experimental import pallas as pl
from jax.experimental.pallas import tpu as pltpu
from jax.sharding import PartitionSpec as P

AXES = ("row", "col")
NX, NY, NZ, CORES = 4, 4, 8, 2
BLK = 128
UNROLL = 16


def place(x, y, z, core):
    return ((z % NZ) * CORES + core) * (NX * NY) + (y % NY) * NX + x % NX


def pairs(move):
    return [
        (place(x, y, z, c), place(*move(x, y, z, c)))
        for z in range(NZ)
        for c in range(CORES)
        for y in range(NY)
        for x in range(NX)
    ]


def along_first(step):
    return pairs(
        lambda x, y, z, c: (x + step, y, z, c) if c == 0 else (x, y + step, z, c)
    )


def along_second(step):
    return pairs(
        lambda x, y, z, c: (x, y + step, z, c) if c == 0 else (x + step, y, z, c)
    )


def along_z(step):
    return pairs(lambda x, y, z, c: (x, y, z + step, c))


def send(value, moved):
    return lax.ppermute(value, AXES, moved)


def exchange_z(value, bit):
    return send(value, pairs(lambda x, y, z, c: (x, y, z ^ bit, c)))


def swap(value):
    return send(value, pairs(lambda x, y, z, c: (x, y, z, 1 - c)))


def tile_kernel(offsets, transposed, group, unroll, depth, cuts, *refs):
    table, bounds, vals_a, vals_b = refs[:4]
    refs = refs[4:]
    pieces, refs = refs[: len(offsets)], refs[len(offsets) :]
    if offsets:
        outs, held = refs[: len(cuts)], refs[len(cuts)]
        total, ring, ring_sem, sem = refs[len(cuts) + 1 :]
    else:
        held, outs = refs[0], refs[1 : len(cuts) + 1]
        total, ring, ring_sem = refs[len(cuts) + 1 :]
    copies = [
        pltpu.make_async_copy(p, held.at[pl.ds(o, p.shape[0])], sem.at[i])
        for i, (p, o) in enumerate(zip(pieces, offsets))
    ]
    for copy in copies:
        copy.start()
    blocks = sum(cuts)
    low, middle, high = [bounds[CORES * group + k] for k in range(CORES + 1)]
    first_steps = (middle - low + unroll - 1) // unroll
    steps = first_steps + (high - middle + unroll - 1) // unroll

    def begin(i):
        return jnp.where(i < first_steps, low + i * unroll, middle + (i - first_steps) * unroll)

    def fetch(i, vals):
        base = begin(i)
        room = lax.rem(i, depth)
        for u in range(unroll):
            pltpu.make_async_copy(
                vals.at[table[base + u] & 127], ring.at[room, u], ring_sem.at[room]
            ).start()

    def ahead(i):
        @pl.when(i < first_steps)
        def _():
            fetch(i, vals_a)

        @pl.when((i >= first_steps) & (i < steps))
        def _():
            fetch(i, vals_b)

    for i in range(depth - 1):
        ahead(jnp.int32(i))

    @pl.loop(0, blocks)
    def _(i):
        total[pl.ds(i * BLK, BLK), :] = jnp.zeros((BLK, total.shape[1]), jnp.float32)

    for copy in copies:
        copy.wait()
    dims = (((0,), (0,)), ((), ())) if transposed else (((1,), (0,)), ((), ()))

    @pl.loop(0, steps)
    def _(i):
        ahead(i + depth - 1)
        room = lax.rem(i, depth)
        pltpu.make_async_copy(
            vals_a.at[pl.ds(0, unroll)], ring.at[room], ring_sem.at[room]
        ).wait()
        base = begin(i)
        limit = jnp.where(i < first_steps, middle, high)
        for u in range(unroll):
            entry = table[base + u]
            source = lax.shift_right_logical(entry, 7) & 63
            target = jnp.where(base + u < limit, lax.shift_right_logical(entry, 13), blocks)
            taken = held[pl.ds(pl.multiple_of(source * BLK, BLK), BLK), :]
            product = lax.dot_general(
                ring[room, u], taken, dims, preferred_element_type=jnp.float32
            )
            placed = pl.ds(pl.multiple_of(target * BLK, BLK), BLK)
            total[placed, :] = total[placed, :] + product

    at = 0
    for out, size in zip(outs, cuts):
        first = at

        @pl.loop(0, size)
        def _(i):
            rows = pl.ds((first + i) * BLK, BLK)
            out[pl.ds(i * BLK, BLK), :] = total[rows, :].astype(jnp.bfloat16)

        at += size


def kept(value):
    return pltpu.with_memory_space_constraint(value, pltpu.HBM)


def tile_product(table, bounds, vals_a, vals_b, sources, offsets, group, cuts, transposed):
    unroll, depth = UNROLL, 3
    width = sources[0].shape[1]
    blocks = sum(cuts)
    vmem = pl.BlockSpec(memory_space=pltpu.VMEM)
    hbm = pl.BlockSpec(memory_space=pltpu.HBM)
    in_specs = [pl.BlockSpec(memory_space=pltpu.SMEM)] * 2 + [hbm] * 2
    out_shape = [jax.ShapeDtypeStruct((c * BLK, width), jnp.bfloat16) for c in cuts]
    scratch = [
        pltpu.VMEM(((blocks + 1) * BLK, width), jnp.float32),
        pltpu.VMEM((depth, unroll, BLK, BLK), jnp.bfloat16),
        pltpu.SemaphoreType.DMA((depth,)),
    ]
    if offsets:
        rows = max(o + p.shape[0] for o, p in zip(offsets, sources))
        in_specs += [pl.BlockSpec(memory_space=pl.ANY)] * len(sources)
        out_shape.append(jax.ShapeDtypeStruct((rows, width), jnp.bfloat16))
        scratch.append(pltpu.SemaphoreType.DMA((len(sources),)))
    else:
        in_specs += [vmem]
    return pl.pallas_call(
        functools.partial(
            tile_kernel, tuple(offsets), transposed, group, unroll, depth, tuple(cuts)
        ),
        out_shape=out_shape,
        in_specs=in_specs,
        out_specs=[vmem] * len(out_shape),
        scratch_shapes=scratch,
        compiler_params=pltpu.CompilerParams(vmem_limit_bytes=20 * 2**20),
        cost_estimate=pl.CostEstimate(
            flops=2 * BLK * BLK * width * 8 * blocks, bytes_accessed=2**20, transcendentals=0
        ),
        name="tile_product",
    )(table, bounds, *[kept(v) for v in (vals_a, vals_b)], *sources)


def chosen(index, values):
    return sum(jnp.where(index == i, v, 0) for i, v in enumerate(values) if v) + 0 * index


def slot_table(live, source, target, group, groups):
    slots = source.shape[1]
    slot = jnp.arange(slots, dtype=jnp.int32)[None]
    tile = jnp.arange(CORES, dtype=jnp.int32)[:, None]
    key = jnp.where(slot < live[:, None], group * CORES + tile, groups * CORES).reshape(-1)
    entry = (slot + source * 128 + target * 8192).reshape(-1)
    place = jnp.arange(CORES * slots, dtype=jnp.int32)
    before = key[None] < key[:, None]
    before |= (key[None] == key[:, None]) & (place[None] < place[:, None])
    rank = jnp.sum(before.astype(jnp.int32), axis=1)
    seat = jnp.arange(CORES * slots + UNROLL, dtype=jnp.int32)[:, None]
    table = jnp.sum(jnp.where(rank[None] == seat, entry[None], 0), axis=1)
    starts = jnp.arange(groups * CORES + 1, dtype=jnp.int32)[:, None]
    bounds = jnp.sum((key[None] < starts).astype(jnp.int32), axis=1)
    return table, bounds


def tied(*values):
    return lax.optimization_barrier(values)


def gather_plane(unit, first_ahead, first_behind, first_across, second_ahead, second_behind):
    half = unit.shape[0] // 2
    last, following = send(unit, first_ahead), send(unit, first_behind)
    across = send(unit, first_across)
    last, following = tied(last, following)
    near = jnp.concatenate([unit, following, last], 0)
    behind_near, ahead_near = send(near, second_behind), send(near, second_ahead)
    behind_across, ahead_across = send(across, second_behind), send(across, second_ahead)
    middle = near.shape[0] // 2
    behind_near, ahead_near = tied(behind_near, ahead_near)
    far = [send(behind_near[:middle], second_behind), send(ahead_near[middle:], second_ahead)]
    far_across = [
        send(behind_across[:half], second_behind),
        send(ahead_across[half:], second_ahead),
    ]
    lines = [[near, across], [behind_near, behind_across], [*far, *far_across]]
    lines += [[ahead_near, ahead_across]]
    pieces, offsets = [], []
    at = 0
    for line in lines:
        for piece in line:
            pieces.append(piece)
            offsets.append(at)
            at += piece.shape[0]
    return pieces, offsets


def widened(*values):
    return functools.reduce(lambda a, b: a + b, [v.astype(jnp.float32) for v in values]).astype(
        jnp.bfloat16
    )


def sum_four(near, free, bound, far, ahead, behind):
    top, bottom = send(far[0], ahead), send(far[1], behind)
    low, high = free()
    low, high = send(low, ahead), send(high, behind)
    one, three = bound()
    top, bottom = tied(top, bottom)
    top, bottom = tied(widened(one, top), widened(three, bottom))
    low, high = tied(low, high)
    near, low, high = near(low, high)
    half = near.shape[0] // 2
    top, bottom = tied(send(top, ahead), send(bottom, behind))
    first = widened(near[:half], top, high)
    second = widened(near[half:], bottom, low)
    return jnp.concatenate([first, second], 0)


def sum_small(value, ahead, behind, beside):
    rows = value.shape[0] // 4
    half = rows // 2
    part = [value[i * rows : (i + 1) * rows] for i in range(4)]
    top, bottom = tied(send(part[2][:half], ahead), send(part[2][half:], behind))
    to_ahead = jnp.concatenate([widened(part[1][:half], top), part[1][half:]], 0)
    to_behind = jnp.concatenate([part[3][:half], widened(part[3][half:], bottom)], 0)
    to_ahead, to_behind = tied(to_ahead, to_behind)
    from_behind, from_ahead = send(to_ahead, ahead), send(to_behind, behind)
    from_behind, from_ahead, *beside = tied(from_behind, from_ahead, *beside)
    return widened(part[0], from_behind, from_ahead), beside


def sum_z(part, far, ahead, behind):
    half = part[0].shape[0] // 2
    top, bottom = tied(send(far[0], ahead), send(far[1], behind))
    to_ahead = jnp.concatenate([widened(part[3][:half], top), part[3][half:]], 0)
    to_behind = jnp.concatenate([part[5][:half], widened(part[5][half:], bottom)], 0)
    for d in (2, 1, 0):
        to_ahead, to_behind = tied(to_ahead, to_behind)
        from_behind, from_ahead = tied(send(to_ahead, ahead), send(to_behind, behind))
        if d:
            to_ahead = widened(part[d], from_behind)
            to_behind = widened(part[NZ - d], from_ahead)
    return widened(part[0], from_behind, from_ahead)


def gather_z(value, grads):
    rows = value.shape[0]
    half = rows // 2
    ahead, behind = along_z(1), along_z(-1)
    pieces, offsets = [value], [0]
    following, last = value, value
    for d in range(1, NZ // 2):
        following, last = send(following, behind), send(last, ahead)
        if d == 2:
            following, last = tied(following, last)
        else:
            following, last, grads = tied(following, last, grads)
        if d == 1:
            grads = lax.all_to_all(grads, "col", 0, 0, tiled=True)
        pieces += [following, last]
        offsets += [d * rows, (NZ - d) * rows]
    grads = summed(grads)
    term = exchange_z(grads, 1)
    lead = [send(following[:half], behind), send(last[half:], ahead)]
    *lead, term = tied(*lead, term)
    pieces += lead
    offsets += [NZ // 2 * rows, NZ // 2 * rows + half]
    return pieces, offsets, widened(grads, term)


def own_rows(halves, core, node_rows, width):
    half = width // 2
    mine = lax.dynamic_slice_in_dim(halves, core * node_rows, node_rows, 0)
    other = swap(lax.dynamic_slice_in_dim(halves, (1 - core) * node_rows, node_rows, 0))
    first = jnp.where(core == 0, mine, other)
    second = jnp.where(core == 0, other, mine)
    return jnp.concatenate([first, second], 1)


def own_half(rows, core, width):
    half = width // 2
    mine = lax.dynamic_slice_in_dim(rows, core * half, half, 1)
    other = swap(lax.dynamic_slice_in_dim(rows, (1 - core) * half, half, 1))
    first = jnp.where(core == 0, mine, other)
    second = jnp.where(core == 0, other, mine)
    return jnp.concatenate([first, second], 0)


def summed(parts):
    return jnp.sum(parts.astype(jnp.float32), axis=0).astype(parts.dtype)


def plane_whole(value):
    spread = jnp.broadcast_to(value[None], (NX * NY, *value.shape))
    return lax.all_to_all(spread, "col", 0, 0, tiled=True)


def per_device(features, w_self, w_neigh, block_vals, block_coords, block_count, cotangent):
    bf16, f32 = jnp.bfloat16, jnp.float32
    node_rows, width = features.shape
    row, col = lax.axis_index("row"), lax.axis_index("col")
    z, core = row // CORES, row % CORES
    y, x = col // NX, col % NX
    near_first, near_second = along_first(1), along_second(1)
    far_first, far_second = along_first(-1), along_second(-1)

    vals = block_vals[0, 0]
    slots = vals.shape[0]
    facts = jnp.concatenate(
        [block_coords[0, 0], jnp.broadcast_to(block_count[0, 0], (1, slots))], 0
    )
    half = width // 2
    note = jnp.zeros((16, half), bf16).at[: facts.shape[0], :slots].set(facts.astype(bf16))
    mine = lax.dynamic_slice_in_dim(features, core * half, half, 1)
    other = lax.dynamic_slice_in_dim(features, (1 - core) * half, half, 1)
    other = swap(jnp.concatenate([other, note], 0))
    other_facts = other[node_rows : node_rows + facts.shape[0], :slots].astype(jnp.int32)
    other = other[:node_rows]
    unit = jnp.concatenate(
        [jnp.where(core == 0, mine, other), jnp.where(core == 0, other, mine)], 0
    )
    later_vals, unit = tied(vals, unit)
    other_vals = swap(later_vals)
    both = jnp.stack([facts, other_facts])
    live = both[:, 2, 0]
    tile_core = jnp.stack([core, 1 - core])[:, None]
    block_row, block_col = both[:, 0], both[:, 1]
    per_dev = node_rows // BLK
    per_chip = CORES * per_dev
    line = NX * per_chip
    z_away = (block_row // per_chip - z) % NZ
    row_in = block_row % per_chip
    owner = block_col // per_dev
    col_in = block_col % per_dev
    dx, dy = (owner % NX - x) % NX, (owner // NX - y) % NY
    first_away, second_away = jnp.where(core == 0, dx, dy), jnp.where(core == 0, dy, dx)
    in_line = chosen(first_away, [0, per_chip, 3 * per_chip, 2 * per_chip]) + tile_core * per_dev
    forward = slot_table(
        live,
        second_away * line + in_line + col_in,
        jnp.where(z_away > NZ // 2, per_chip, 0) + row_in,
        jnp.abs(NZ // 2 - z_away),
        5,
    )
    upper = first_away >= NX // 2
    backward = slot_table(
        live,
        z_away * per_chip + row_in,
        (first_away - jnp.where((second_away % 2 == 1) & upper, NX // 2, 0)) * per_chip
        + jnp.where(second_away == 3, line // 2, 0)
        + tile_core * per_dev
        + col_in,
        jnp.where(
            second_away % 2 == 1,
            jnp.where((second_away == 1) == upper, 1, 2),
            chosen(second_away, [3]),
        ),
        4,
    )

    pieces, offsets = gather_plane(
        unit, near_first, far_first, along_first(2), near_second, far_second
    )
    half_chip = per_chip // 2
    *far, held = tile_product(
        *forward, vals, other_vals, pieces, offsets, 0, [half_chip] * 2, False
    )
    part = [None] * NZ
    for group, away in enumerate([(3, 5), (2, 6), (1, 7), (0,)], 1):
        made = tile_product(
            *forward, vals, other_vals, [held], [], group, [per_chip] * len(away), False
        )
        for d, value in zip(away, made):
            part[d] = value
    neighbours = sum_z(part, far, along_z(1), along_z(-1))
    neighbours = own_rows(neighbours, core, node_rows, width)

    preact = jnp.dot(features, w_self, preferred_element_type=f32)
    preact = preact + jnp.dot(neighbours, w_neigh, preferred_element_type=f32)
    gate = jax.nn.sigmoid(preact)
    layer_out = (preact * gate).astype(bf16)
    slope_grad = (cotangent.astype(f32) * gate * (1.0 + preact * (1.0 - gate))).astype(bf16)
    contract_rows = (((0,), (0,)), ((), ()))
    contract_cols = (((1,), (1,)), ((), ()))
    neigh_grad = lax.dot_general(
        slope_grad, w_neigh, contract_cols, preferred_element_type=f32
    ).astype(bf16)
    grad_unit = own_half(neigh_grad, core, width)

    plane = NX * NY
    slope_later, grad_unit = tied(slope_grad, grad_unit)
    grads = [
        lax.dot_general(v, slope_later, contract_rows, preferred_element_type=f32).astype(bf16)
        for v in (features, neighbours)
    ]
    mine = jnp.where(core == 0, grads[0], grads[1])
    other = swap(jnp.where(core == 0, grads[1], grads[0]))
    grads = widened(mine, other).reshape(plane, width // plane, width)
    pieces, offsets, total = gather_z(grad_unit, grads)
    term = exchange_z(total, 2)

    *far, held = tile_product(
        *backward,
        vals,
        other_vals,
        [kept(p) for p in pieces],
        offsets,
        0,
        [line // 2] * 2,
        True,
    )

    def group_of(index, held, cuts):
        return tile_product(*backward, vals, other_vals, [held], [], index, cuts, True)

    far[0], term = tied(far[0], term)
    total = widened(total, term)
    term = exchange_z(total, 4)

    def near(low, high):
        given, low, high = tied(held, low, high)
        return group_of(3, given, [line])[0], low, high

    back = sum_four(
        near,
        lambda: group_of(1, held, [line // 2] * 2),
        lambda: group_of(2, held, [line // 2] * 2),
        far,
        near_second,
        far_second,
    )
    back, term = tied(back, term)
    total = plane_whole(widened(total, term))
    back, (total,) = sum_small(back, near_first, far_first, [total])
    other_total = swap(total)
    total, other_total = [v.reshape(width, width).astype(f32) for v in (total, other_total)]
    grad_self = jnp.where(core == 0, total, other_total)
    grad_neigh = jnp.where(core == 0, other_total, total)
    back_rows = own_rows(back, core, node_rows, width)
    own_grad = lax.dot_general(slope_grad, w_self, contract_cols, preferred_element_type=f32)
    grad_features = (own_grad + back_rows.astype(f32)).astype(bf16)
    return layer_out, grad_features, grad_self, grad_neigh


def solution(mesh):
    in_specs = (
        P(("row", "col"), None),
        P(),
        P(),
        P("row", "col", None, None, None),
        P("row", "col", None, None),
        P("row", "col"),
        P(("row", "col"), None),
    )
    out_specs = (P(("row", "col"), None), P(("row", "col"), None), P(), P())
    return jax.shard_map(
        per_device, mesh=mesh, in_specs=in_specs, out_specs=out_specs, check_vma=False
    )
```
